128 devices in a mesh: pipe: 2 (over z_hi), dp: 64 (over y, z_lo, x, core).
Axes of the slice: x: 4, y: 4, z: 4 (z_hi: 2, z_lo: 2; z = z_hi * 2 + z_lo), core: 2. Of those that a mesh axis runs over, the one named last changes fastest.
Arguments:
- video: bfloat16 [2, 64, 1088, 512], P(None, 'dp'), may hold values from -6 to 6
- cot_h: bfloat16 [2, 64, 1088, 512], P(None, 'dp'), may hold values from -6 to 6
- cot_q: bfloat16 [2, 64, 8, 1088], P(None, 'dp'), may hold values from -6 to 6
- frames: int32 [2, 64], P(None, 'dp'), may hold values from 5 to 17, as said below
- codes: int32 [2, 64, 1088], P(None, 'dp'), may hold values from 0 to 8191
- w_attn: bfloat16 [2, 512, 2048], P('pipe')
- w_up: bfloat16 [2, 512, 2048], P('pipe'), may hold values from -0.25 to 0.25
- w_down: bfloat16 [2, 2048, 512], P('pipe'), may hold values from -0.125 to 0.125
- gains: float32 [2, 2, 512], P('pipe'), may hold values from 0.5 to 1.5
- proj: bfloat16 [512, 8], P(('pipe', 'dp')), may hold values from -0.25 to 0.25
- codebook: bfloat16 [8, 8192], P(None, ('pipe', 'dp')), may hold values from -5 to 5
- ema_attn: float32 [2, 512, 2048], P('pipe', 'dp'), may hold values from -0.25 to 0.25
- ema_up: float32 [2, 512, 2048], P('pipe', 'dp'), may hold values from -0.25 to 0.25
- ema_down: float32 [2, 2048, 512], P('pipe', 'dp'), may hold values from -0.125 to 0.125
- ema_gains: float32 [2, 2, 512], P('pipe', None, 'dp'), may hold values from 0.5 to 1.5
- ema_proj: float32 [512, 8], P(('pipe', 'dp')), may hold values from -0.25 to 0.25
- ema_code: float32 [8, 8192], P(None, ('pipe', 'dp')), may hold values from -5 to 5
- decay: float32 [3], replicated, may hold values from 0.5 to 0.95
Outputs:
- acts: bfloat16 [2, 2, 64, 1088, 512], P('pipe', None, 'dp')
- grad_in: bfloat16 [2, 2, 64, 1088, 512], P('pipe', None, 'dp')
- g_attn: float32 [2, 512, 2048], P('pipe', 'dp')
- g_up: float32 [2, 512, 2048], P('pipe', 'dp')
- g_down: float32 [2, 2048, 512], P('pipe', 'dp')
- g_gains: float32 [2, 2, 512], P('pipe', None, 'dp')
- g_proj: float32 [512, 8], P(('pipe', 'dp'))
- g_code: float32 [8, 8192], P(None, ('pipe', 'dp'))
- new_attn: float32 [2, 512, 2048], P('pipe', 'dp')
- new_up: float32 [2, 512, 2048], P('pipe', 'dp')
- new_down: float32 [2, 2048, 512], P('pipe', 'dp')
- new_gains: float32 [2, 2, 512], P('pipe', None, 'dp')
- new_proj: float32 [512, 8], P(('pipe', 'dp'))
- new_code: float32 [8, 8192], P(None, ('pipe', 'dp'))
The draws below stay inside these ranges and needn't reach their ends.
Inputs may be any that keep to these rules, and one draw needn't show every extreme that they name: `frames`: each count is 5, 9 or 17, and 17 occurs in every draw.
All inputs are finite; a program needn't handle non-finite values.
Results may differ from the reference program's by a relative error of at most 0.02.
Values may be sent and summed in bfloat16 or wider, within the bound.
A program may use at most 512 MiB of HBM per device.

```python
import jax
import jax.numpy as jnp
from jax import lax

D = 512
HEADS = 8
HEAD_DIM = 64
FF = 2048
CODES = 8192
CODE_DIM = 8
PATCHES = 64
FRAMES = 17
MICRO = 2
VIDS = 64
SEQ = 1088


def draw_frames(key, part):
    key = jax.random.fold_in(key, 11)
    level_key, place_key = jax.random.split(key)
    level = jax.random.randint(level_key, (MICRO * VIDS,), 0, 3)
    factor = jnp.where(level == 0, 1, jnp.where(level == 1, 2, 4))
    counts = (FRAMES - 1) // 4 * factor + 1
    place = jax.random.randint(place_key, (), 0, MICRO * VIDS)
    counts = counts.at[place].set(FRAMES)
    return counts.reshape(MICRO, VIDS).astype(jnp.int32)


def draw_w_attn(key, part):
    key = jax.random.fold_in(key, 5)
    base = jnp.clip(jax.random.normal(key, (2, D, 4 * D), jnp.float32), -6.0, 6.0) * D ** (-0.5)
    column = jnp.arange(4 * D)
    boost = jnp.array([PATCHES ** 0.5, 3.0], jnp.float32)[:, None, None]
    scaled = jnp.where(column[None, None, :] >= 3 * D, base * boost, base)
    return scaled.astype(jnp.bfloat16)


def with_ends(values, own_key, low, largest):
    spot = [jax.random.randint(jax.random.fold_in(own_key, axis), (), 0, length) for axis, length in enumerate(values.shape)]
    widest = values.shape.index(max(values.shape))
    neighbour = spot[:widest] + [(spot[widest] + 1) % values.shape[widest]] + spot[widest + 1:]
    return values.at[tuple(spot)].set(low).at[tuple(neighbour)].set(largest)


def level_of(own_key, dims, cuts, smallest, high):
    factor_of = 1.0
    for dim, parts in cuts:
        heights = jax.random.uniform(jax.random.fold_in(jax.random.fold_in(own_key, 6), dim), (parts,), jnp.float32, smallest / len(cuts), high / len(cuts))
        factor_of = factor_of * jnp.repeat(jnp.exp(heights), dims[dim] // parts).reshape((-1,) + (1,) * (len(dims) - 1 - dim))
    return factor_of


def bell_draw(stream_key, shape, deviation, limit, shards=(), dtype=jnp.bfloat16):
    level = level_of(stream_key, shape, shards, -0.22, 0.18) if shards else 1.0
    values = jax.random.normal(stream_key, shape, jnp.float32) * deviation * level
    return jnp.minimum(jnp.maximum(values, -limit), limit).astype(dtype)


def setup_inputs(seed: int = 0) -> dict:
    seeds = jax.random.split(jax.random.key(seed), 19)
    video = bell_draw(seeds[0], (MICRO, VIDS, SEQ, D), 1.0, 6.0, ((1, 64),))
    cot_h = bell_draw(seeds[1], (MICRO, VIDS, SEQ, D), 1.0, 6.0, ((1, 64),))
    cot_q = bell_draw(seeds[2], (MICRO, VIDS, CODE_DIM, SEQ), 1.0, 6.0, ((1, 64),))
    frames = draw_frames(jax.random.fold_in(seeds[18], 71), 0)
    codes = with_ends(jax.random.randint(seeds[4], (MICRO, VIDS, SEQ), 0, CODES), jax.random.fold_in(seeds[4], 1), 0, CODES - 1).astype(jnp.int32)
    w_attn = draw_w_attn(jax.random.fold_in(seeds[18], 71), 0)
    w_up = bell_draw(seeds[6], (2, D, FF), D ** -0.5, 0.25, ((0, 2),))
    w_down = bell_draw(seeds[7], (2, FF, D), FF ** -0.5, 0.125, ((0, 2),))
    gains = jnp.clip(1.0 + 0.1 * jax.random.normal(seeds[8], (2, 2, D), jnp.float32), 0.5, 1.5)
    proj = bell_draw(seeds[9], (D, CODE_DIM), D ** -0.5, 0.25, ((0, 128),))
    codebook = bell_draw(seeds[10], (CODE_DIM, CODES), 1.0, 5.0, ((1, 128),))
    ema_attn = bell_draw(seeds[11], (2, D, 4 * D), D ** -0.5, 0.25, ((0, 2), (1, 64)), jnp.float32)
    ema_up = bell_draw(seeds[12], (2, D, FF), D ** -0.5, 0.25, ((0, 2), (1, 64)), jnp.float32)
    ema_down = bell_draw(seeds[13], (2, FF, D), FF ** -0.5, 0.125, ((0, 2), (1, 64)), jnp.float32)
    ema_gains = jnp.clip(1.0 + 0.1 * jax.random.normal(seeds[14], (2, 2, D), jnp.float32), 0.5, 1.5)
    ema_proj = bell_draw(seeds[15], (D, CODE_DIM), D ** -0.5, 0.25, ((0, 128),), jnp.float32)
    ema_code = bell_draw(seeds[16], (CODE_DIM, CODES), 1.0, 5.0, ((1, 128),), jnp.float32)
    decay = jnp.clip(jax.random.uniform(seeds[17], (3,), jnp.float32, 0.5, 0.95), 0.5, 0.95)
    return dict(video=video, cot_h=cot_h, cot_q=cot_q, frames=frames, codes=codes, w_attn=w_attn, w_up=w_up, w_down=w_down, gains=gains, proj=proj, codebook=codebook, ema_attn=ema_attn, ema_up=ema_up, ema_down=ema_down, ema_gains=ema_gains, ema_proj=ema_proj, ema_code=ema_code, decay=decay)


@jax.custom_vjp
def low(v):
    return lax.optimization_barrier(v.astype(jnp.bfloat16)).astype(jnp.float32)

@jax.custom_vjp
def low_back(v):
    return v

def low_keep(v):
    return (low(v), None)

def low_pass(kept, grad):
    return (grad,)

def back_keep(v):
    return (v, None)

def back_low(kept, grad):
    return (low(grad),)
low.defvjp(low_keep, low_pass)
low_back.defvjp(back_keep, back_low)
HIGH = lax.Precision.HIGHEST
EPSILON = 1e-05
BETA = 0.25
LEARN_RATE = 0.0001
MASKED = -1e+30

def layer_norm(value, gain):
    center = lax.optimization_barrier(jnp.mean(value, axis=-1, keepdims=True))
    centred = value - center
    spread = lax.optimization_barrier(jnp.mean(centred * centred, axis=-1, keepdims=True))
    return centred * lax.rsqrt(spread + EPSILON) * gain

def attend(query, keys, values, allowed):
    scores = jnp.einsum('glhe,gmhe->ghlm', query, keys, precision=HIGH) * HEAD_DIM ** (-0.5)
    scores = low_back(scores)
    scores = jnp.where(allowed, scores, MASKED)
    probs = low(jax.nn.softmax(scores, axis=-1))
    return jnp.einsum('ghlm,gmhe->glhe', probs, values, precision=HIGH)

def block(params, value, frame_count, temporal):
    weight_attn, weight_up, weight_down, gain_pair = params
    normed = low(layer_norm(value, gain_pair[0]))
    mixed = low(low_back(jnp.dot(normed, weight_attn[:, :3 * D], precision=HIGH)))
    shaped = mixed.reshape(FRAMES, PATCHES, 3, HEADS, HEAD_DIM)
    if temporal:
        shaped = jnp.swapaxes(shaped, 0, 1)
        frame_ids = jnp.arange(FRAMES)
        allowed = (frame_ids[None, :] <= frame_ids[:, None]) & (frame_ids[None, :] < frame_count)
        allowed = allowed[None, None]
    else:
        allowed = jnp.ones((1, 1, PATCHES, PATCHES), jnp.bool_)
    heads_out = attend(shaped[:, :, 0], shaped[:, :, 1], shaped[:, :, 2], allowed)
    if temporal:
        heads_out = jnp.swapaxes(heads_out, 0, 1)
    context = low(low_back(heads_out.reshape(SEQ, D)))
    branch = low_back(jnp.dot(context, weight_attn[:, 3 * D:], precision=HIGH))
    middle = value + branch
    normed_two = low(layer_norm(middle, gain_pair[1]))
    hidden_pre = low_back(jnp.dot(normed_two, weight_up, precision=HIGH))
    activated = low(jax.nn.gelu(hidden_pre))
    return middle + low_back(jnp.dot(activated, weight_down, precision=HIGH))

def average(ema, weight, grad, rate):
    return rate * ema + (1.0 - rate) * (weight - LEARN_RATE * grad)

def reference(video, cot_h, cot_q, frames, codes, w_attn, w_up, w_down, gains, proj, codebook, ema_attn, ema_up, ema_down, ema_gains, ema_proj, ema_code, decay):
    wide = [w.astype(jnp.float32) for w in (w_attn, w_up, w_down, gains)]
    params_first = tuple((w[0] for w in wide))
    params_second = tuple((w[1] for w in wide))
    quant = (proj.astype(jnp.float32), codebook.astype(jnp.float32))
    number = MICRO * VIDS
    items = (video.reshape(number, SEQ, D), cot_h.reshape(number, SEQ, D), cot_q.reshape(number, CODE_DIM, SEQ), frames.reshape(number), codes.reshape(number, SEQ))
    zeros = jax.tree.map(lambda a: jnp.zeros(a.shape, jnp.float32), (params_first, params_second, quant))

    def step(carry, item):
        video_one, cot_h_one, cot_q_one, count_one, code_one = item
        valid = (jnp.arange(SEQ) // PATCHES < count_one).astype(jnp.float32)[:, None]
        onehot = (code_one[:, None] == jnp.arange(CODES)[None, :]).astype(jnp.float32)

        def first_section(params, value):
            return low(block(params, value, count_one, False))
        sent, first_back = jax.vjp(first_section, params_first, video_one.astype(jnp.float32))

        def second_section(params, weights, value):
            out = block(params, low_back(value), count_one, True)
            latent = low_back(jnp.dot(low(out), weights[0], precision=HIGH))
            looked = low_back(jnp.dot(onehot, weights[1].T, precision=HIGH))
            return (out, latent, looked)
        (out, latent, looked), second_back = jax.vjp(second_section, params_second, quant, sent)
        cot_latent = valid * (cot_q_one.astype(jnp.float32).T + 2.0 * BETA * (latent - looked))
        cot_looked = 2.0 * valid * (looked - latent)
        cotangents = (cot_h_one.astype(jnp.float32) * valid, cot_latent, cot_looked)
        grads_second, grads_quant, sent_grad = second_back(cotangents)
        grads_first, video_grad = first_back(sent_grad)
        carry = jax.tree.map(lambda a, b: a + b, carry, (grads_first, grads_second, grads_quant))
        return (carry, (sent * valid, out * valid, video_grad, sent_grad))
    totals, (acts_first, acts_second, back_first, back_second) = lax.scan(step, zeros, items)
    shape = (2, MICRO, VIDS, SEQ, D)
    acts = jnp.stack([acts_first, acts_second]).reshape(shape).astype(jnp.bfloat16)
    grad_in = jnp.stack([back_first, back_second]).reshape(shape).astype(jnp.bfloat16)
    stacked = [jnp.stack([totals[0][i], totals[1][i]]) for i in range(4)]
    g_proj, g_code = totals[2]
    rates = decay[:2].reshape(2, 1, 1)
    new_attn = average(ema_attn, wide[0], stacked[0], rates)
    new_up = average(ema_up, wide[1], stacked[1], rates)
    new_down = average(ema_down, wide[2], stacked[2], rates)
    new_gains = average(ema_gains, wide[3], stacked[3], rates)
    new_proj = average(ema_proj, quant[0], g_proj, decay[2])
    new_code = average(ema_code, quant[1], g_code, decay[2])
    return (acts, grad_in, stacked[0], stacked[1], stacked[2], stacked[3], g_proj, g_code, new_attn, new_up, new_down, new_gains, new_proj, new_code)
```

```python
import jax
import jax.numpy as jnp
from jax import lax
from jax.experimental import pallas as pl
from jax.experimental.pallas import tpu as pltpu
from jax.sharding import PartitionSpec as P

D = 512
HEADS = 8
HEAD_DIM = 64
FF = 2048
CODES = 8192
CODE_DIM = 8
ROWS_OF_CODES = 128
LOW_CODES = 64
PATCHES = 64
FRAMES = 17
SEQ = 1088


EPSILON = 1e-05
BETA = 0.25
LEARN_RATE = 0.0001
MASKED = -1e30
MESH = pl.DeviceIdType.MESH
WIDE = 3200


def gather_kernel(block_ref, out_ref, landed, send_sems, recv_sems):
    pipe = lax.axis_index("pipe")
    dp = lax.axis_index("dp")
    own = pipe * 64 + dp

    def copy_to(step):
        target = lax.rem(dp + step, 64)
        return pltpu.make_async_remote_copy(
            src_ref=block_ref,
            dst_ref=landed.at[own],
            send_sem=send_sems.at[step],
            recv_sem=recv_sems.at[own],
            device_id=(1, target),
            device_id_type=MESH,
        )

    def start(step, carry):
        copy_to(step).start()
        return carry

    def finish(step, carry):
        copy_to(step).wait_send()
        return carry

    @pl.when(pipe == 0)
    def _():
        copy_to(0).start()

    lax.fori_loop(1, 64, start, 0)

    @pl.when(pipe == 0)
    def _():
        copy_to(0).wait_send()
        out_ref[...] = jnp.zeros_like(out_ref)

    lax.fori_loop(1, 64, finish, 0)

    @pl.when(pipe == 1)
    def _():
        landed[own] = block_ref[...]

        def arrive(step, carry):
            source = lax.rem(own + step, 128)
            pltpu.make_async_remote_copy(
                src_ref=block_ref,
                dst_ref=landed.at[source],
                send_sem=send_sems.at[0],
                recv_sem=recv_sems.at[source],
                device_id=(1, lax.rem(dp + 1, 64)),
                device_id_type=MESH,
            ).wait_recv()
            return carry

        lax.fori_loop(1, 128, arrive, 0)
        out_ref[...] = landed[...]


def gather_blocks(block):
    return pl.pallas_call(
        gather_kernel,
        out_shape=jax.ShapeDtypeStruct((128, 8, 128), jnp.float32),
        in_specs=[pl.BlockSpec(memory_space=pltpu.VMEM)],
        out_specs=pl.BlockSpec(memory_space=pltpu.VMEM),
        scratch_shapes=[
            pltpu.VMEM((128, 8, 128), jnp.float32),
            pltpu.SemaphoreType.DMA((64,)),
            pltpu.SemaphoreType.DMA((128,)),
        ],
        compiler_params=pltpu.CompilerParams(has_side_effects=True),
    )(block)


def chip_after(chip, step):
    x = lax.rem(lax.rem(chip, 4) + lax.rem(step, 4), 4)
    z = lax.rem(lax.rem(chip // 4, 2) + lax.rem(step // 4, 2), 2)
    y = lax.rem(chip // 8 + step // 8, 4)
    return (y * 2 + z) * 4 + x


def scatter_kernel(blocks, out_ref, mine, other, landed, local_sems, near_send, near_recv, far_send, far_recv):
    pipe = lax.axis_index("pipe")
    dp = lax.axis_index("dp")
    core = lax.rem(dp, 2)
    chip = dp // 2
    partner = dp + 1 - 2 * core

    def near(step):
        target = chip_after(chip, step)
        return pltpu.make_async_remote_copy(
            src_ref=blocks.at[1 - core, target],
            dst_ref=other.at[target],
            send_sem=near_send.at[step],
            recv_sem=near_recv.at[step],
            device_id=(pipe, partner),
            device_id_type=MESH,
        )

    def local(step):
        target = chip_after(chip, step)
        return pltpu.make_async_copy(blocks.at[core, target], mine.at[target], local_sems.at[step])

    def far(step):
        target = chip_after(chip, step)
        return pltpu.make_async_remote_copy(
            src_ref=mine.at[target],
            dst_ref=landed.at[step],
            send_sem=far_send.at[step],
            recv_sem=far_recv.at[step],
            device_id=(pipe, target * 2 + core),
            device_id_type=MESH,
        )

    def begin(step, carry):
        at = lax.rem(step + 1, 32)
        near(at).start()
        local(at).start()
        return carry

    lax.fori_loop(0, 32, begin, 0)

    def pair(step, carry):
        target = chip_after(chip, step)
        local(step).wait()
        near(step).wait_recv()
        mine[target] = (mine[target].astype(jnp.float32) + other[target].astype(jnp.float32)).astype(jnp.bfloat16)
        far(step).start()
        return carry

    lax.fori_loop(1, 32, pair, 0)
    local(0).wait()
    near(0).wait_recv()
    out_ref[...] = mine[chip].astype(jnp.float32) + other[chip].astype(jnp.float32)

    def total(step, carry):
        far(step).wait_recv()
        out_ref[...] += landed[step].astype(jnp.float32)
        return carry

    lax.fori_loop(1, 32, total, 0)

    def finish(step, carry):
        near(step).wait_send()
        return carry

    lax.fori_loop(0, 32, finish, 0)

    def finish_far(step, carry):
        far(step).wait_send()
        return carry

    lax.fori_loop(1, 32, finish_far, 0)


def scatter_blocks(blocks):
    shape = (32, 16, WIDE)
    return pl.pallas_call(
        scatter_kernel,
        out_shape=jax.ShapeDtypeStruct((16, WIDE), jnp.float32),
        in_specs=[pl.BlockSpec(memory_space=pl.ANY)],
        out_specs=pl.BlockSpec(memory_space=pltpu.VMEM),
        scratch_shapes=[
            pltpu.VMEM(shape, jnp.bfloat16),
            pltpu.VMEM(shape, jnp.bfloat16),
            pltpu.VMEM(shape, jnp.bfloat16),
            pltpu.SemaphoreType.DMA((32,)),
            pltpu.SemaphoreType.DMA((32,)),
            pltpu.SemaphoreType.DMA((32,)),
            pltpu.SemaphoreType.DMA((32,)),
            pltpu.SemaphoreType.DMA((32,)),
        ],
        compiler_params=pltpu.CompilerParams(has_side_effects=True, vmem_limit_bytes=40 << 20),
    )(blocks)


def from_behind(block, axis, distance):
    devices = range(lax.axis_size(axis))
    route = [(i - distance, i) for i in devices if i - distance in devices]
    return lax.ppermute(block, axis, route)


def layer_norm(value, gain):
    center = jnp.mean(value, axis=-1, keepdims=True)
    centred = value - center
    spread = jnp.mean(centred * centred, axis=-1, keepdims=True)
    return centred * lax.rsqrt(spread + EPSILON) * gain


def spatial_groups(tokens):
    return tokens.reshape((tokens.shape[0] * FRAMES, PATCHES) + tokens.shape[2:])


def spatial_tokens(grouped, videos):
    return grouped.reshape((videos, FRAMES * PATCHES) + grouped.shape[2:])


def spatial_allowed():
    return jnp.ones((1, 1, PATCHES, PATCHES), jnp.bool_)


def attend_forward(grouped, allowed):
    query, keys, values = (grouped[:, :, 0], grouped[:, :, 1], grouped[:, :, 2])
    scores = jnp.einsum(
        "glhe,gmhe->ghlm", query, keys, preferred_element_type=jnp.float32
    ) * HEAD_DIM ** (-0.5)
    scores = jnp.where(allowed, scores, MASKED)
    highest = jnp.max(scores, axis=-1, keepdims=True)
    logsum = highest + jnp.log(jnp.sum(jnp.exp(scores - highest), axis=-1, keepdims=True))
    probs = jnp.exp(scores - logsum).astype(jnp.bfloat16)
    context = jnp.einsum("ghlm,gmhe->glhe", probs, values, preferred_element_type=jnp.float32)
    return (context.astype(jnp.bfloat16), jnp.swapaxes(logsum[..., 0], 1, 2))


def attend_backward(grouped, allowed, logsum, d_context):
    query, keys, values = (grouped[:, :, 0], grouped[:, :, 1], grouped[:, :, 2])
    scores = jnp.einsum(
        "glhe,gmhe->ghlm", query, keys, preferred_element_type=jnp.float32
    ) * HEAD_DIM ** (-0.5)
    scores = jnp.where(allowed, scores, MASKED)
    probs = jnp.exp(scores - jnp.swapaxes(logsum, 1, 2)[..., None])
    d_values = jnp.einsum(
        "ghlm,glhe->gmhe", probs.astype(jnp.bfloat16), d_context, preferred_element_type=jnp.float32
    )
    d_probs = jnp.einsum("glhe,gmhe->ghlm", d_context, values, preferred_element_type=jnp.float32)
    d_scores = probs * (d_probs - jnp.sum(d_probs * probs, axis=-1, keepdims=True))
    d_low = d_scores.astype(jnp.bfloat16)
    d_query = jnp.einsum(
        "ghlm,gmhe->glhe", d_low, keys, preferred_element_type=jnp.float32
    ) * HEAD_DIM ** (-0.5)
    d_keys = jnp.einsum(
        "ghlm,glhe->gmhe", d_low, query, preferred_element_type=jnp.float32
    ) * HEAD_DIM ** (-0.5)
    return jnp.stack([d_query, d_keys, d_values], axis=2)


def spatial_forward(mixed, frame_count):
    videos = mixed.shape[0]
    grouped = spatial_groups(mixed.reshape(videos, SEQ, 3, HEADS, HEAD_DIM))
    context, logsum = attend_forward(grouped, spatial_allowed())
    return (spatial_tokens(context, videos).reshape(videos, SEQ, D), spatial_tokens(logsum, videos))


def spatial_backward(mixed, logsum, d_context, frame_count):
    videos = mixed.shape[0]
    grouped = spatial_groups(mixed.reshape(videos, SEQ, 3, HEADS, HEAD_DIM))
    d_heads = spatial_groups(d_context.reshape(videos, SEQ, HEADS, HEAD_DIM))
    d_grouped = attend_backward(grouped, spatial_allowed(), spatial_groups(logsum), d_heads)
    return spatial_tokens(d_grouped, videos).reshape(videos, SEQ, 3 * D)


def to_lanes(tokens, parts):
    videos = tokens.shape[0]
    shaped = tokens.reshape(videos, FRAMES, PATCHES, parts, HEADS, HEAD_DIM)
    shaped = jnp.transpose(shaped, (0, 3, 1, 5, 4, 2))
    return shaped.reshape(videos, parts, FRAMES, HEAD_DIM, HEADS * PATCHES)


def from_lanes(lanes):
    videos, parts = (lanes.shape[0], lanes.shape[1])
    shaped = lanes.reshape(videos, parts, FRAMES, HEAD_DIM, HEADS, PATCHES)
    shaped = jnp.transpose(shaped, (0, 2, 5, 1, 4, 3))
    return shaped.reshape(videos, SEQ, parts * HEADS * HEAD_DIM)


def lane_scores(queries, key_lanes, frame_count):
    scores = jnp.sum(
        queries.astype(jnp.float32)[:, :, None] * key_lanes.astype(jnp.float32)[:, None], axis=3
    ) * HEAD_DIM ** (-0.5)
    frame_ids = jnp.arange(FRAMES)
    allowed = (frame_ids[None, None, :] <= frame_ids[None, :, None]) & (
        frame_ids[None, None, :] < frame_count[:, None, None]
    )
    return jnp.where(allowed[..., None], scores, MASKED)


def temporal_forward(mixed, frame_count):
    videos = mixed.shape[0]
    lanes = to_lanes(mixed, 3)
    queries, key_lanes, value_lanes = (lanes[:, 0], lanes[:, 1], lanes[:, 2])
    scores = lane_scores(queries, key_lanes, frame_count)
    highest = jnp.max(scores, axis=2, keepdims=True)
    logsum = highest + jnp.log(jnp.sum(jnp.exp(scores - highest), axis=2, keepdims=True))
    probs = jnp.exp(scores - logsum).astype(jnp.bfloat16)
    context = jnp.sum(
        probs.astype(jnp.float32)[:, :, :, None] * value_lanes.astype(jnp.float32)[:, None], axis=2
    )
    context_tokens = from_lanes(context.astype(jnp.bfloat16)[:, None])
    shaped = jnp.transpose(logsum.reshape(videos, FRAMES, HEADS, PATCHES), (0, 1, 3, 2))
    return (context_tokens, shaped.reshape(videos, SEQ, HEADS))


def temporal_backward(mixed, logsum, d_context, frame_count):
    videos = mixed.shape[0]
    lanes = to_lanes(mixed, 3)
    queries, key_lanes, value_lanes = (lanes[:, 0], lanes[:, 1], lanes[:, 2])
    lane_logsum = jnp.transpose(
        logsum.reshape(videos, FRAMES, PATCHES, HEADS), (0, 1, 3, 2)
    ).reshape(videos, FRAMES, 1, HEADS * PATCHES)
    d_lanes = to_lanes(d_context, 1)[:, 0].astype(jnp.float32)
    scores = lane_scores(queries, key_lanes, frame_count)
    probs = jnp.exp(scores - lane_logsum)
    probs_low = probs.astype(jnp.bfloat16).astype(jnp.float32)
    d_values = jnp.sum(probs_low[:, :, :, None] * d_lanes[:, :, None], axis=1)
    d_probs = jnp.sum(d_lanes[:, :, None] * value_lanes.astype(jnp.float32)[:, None], axis=3)
    d_scores = probs * (d_probs - jnp.sum(d_probs * probs, axis=2, keepdims=True))
    d_low = d_scores.astype(jnp.bfloat16).astype(jnp.float32)
    d_query = jnp.sum(
        d_low[:, :, :, None] * key_lanes.astype(jnp.float32)[:, None], axis=2
    ) * HEAD_DIM ** (-0.5)
    d_keys = jnp.sum(
        d_low[:, :, :, None] * queries.astype(jnp.float32)[:, :, None], axis=1
    ) * HEAD_DIM ** (-0.5)
    return from_lanes(jnp.stack([d_query, d_keys, d_values], axis=1))


def block_forward(weights, inputs, frame_count, first):
    weight_attn, weight_up, weight_down, gain_pair = weights
    videos = inputs.shape[0]
    flat = inputs.reshape(-1, D).astype(jnp.float32)
    normed = layer_norm(flat, gain_pair[0]).astype(jnp.bfloat16)
    mixed = jnp.dot(normed, weight_attn[:, : 3 * D], preferred_element_type=jnp.float32).astype(
        jnp.bfloat16
    )
    mixed = mixed.reshape(videos, SEQ, 3 * D)
    context, logsum = lax.cond(first, spatial_forward, temporal_forward, mixed, frame_count)
    middle = flat + jnp.dot(
        context.reshape(-1, D), weight_attn[:, 3 * D :], preferred_element_type=jnp.float32
    )
    normed_two = layer_norm(middle, gain_pair[1]).astype(jnp.bfloat16)
    hidden_pre = jnp.dot(normed_two, weight_up, preferred_element_type=jnp.float32)
    activated = jax.nn.gelu(hidden_pre).astype(jnp.bfloat16)
    output = middle + jnp.dot(activated, weight_down, preferred_element_type=jnp.float32)
    return (
        output.astype(jnp.bfloat16).reshape(videos, SEQ, D),
        (mixed, context, logsum, middle, hidden_pre),
    )


def block_backward(weights, inputs, saved, frame_count, first, d_out):
    weight_attn, weight_up, weight_down, gain_pair = weights
    mixed, context, logsum, middle, hidden_pre = saved
    videos = inputs.shape[0]
    flat = inputs.reshape(-1, D).astype(jnp.float32)
    d_two = d_out.astype(jnp.bfloat16)
    normed_two, norm_two_back = jax.vjp(layer_norm, middle, gain_pair[1])
    activated, gelu_back = jax.vjp(jax.nn.gelu, hidden_pre)
    grad_down = jnp.dot(activated.astype(jnp.bfloat16).T, d_two, preferred_element_type=jnp.float32)
    d_activated = jnp.dot(d_two, weight_down.T, preferred_element_type=jnp.float32)
    d_hidden = gelu_back(d_activated)[0].astype(jnp.bfloat16)
    grad_up = jnp.dot(
        normed_two.astype(jnp.bfloat16).T, d_hidden, preferred_element_type=jnp.float32
    )
    d_normed_two = jnp.dot(d_hidden, weight_up.T, preferred_element_type=jnp.float32)
    d_middle_norm, grad_gain_two = norm_two_back(d_normed_two)
    d_middle = d_out + d_middle_norm
    d_branch = d_middle.astype(jnp.bfloat16)
    grad_out = jnp.dot(context.reshape(-1, D).T, d_branch, preferred_element_type=jnp.float32)
    d_context = jnp.dot(
        d_branch, weight_attn[:, 3 * D :].T, preferred_element_type=jnp.float32
    ).astype(jnp.bfloat16)
    d_context = d_context.reshape(videos, SEQ, D)
    d_mixed = lax.cond(
        first, spatial_backward, temporal_backward, mixed, logsum, d_context, frame_count
    )
    d_mixed = d_mixed.reshape(-1, 3 * D).astype(jnp.bfloat16)
    normed, norm_back = jax.vjp(layer_norm, flat, gain_pair[0])
    grad_mix = jnp.dot(normed.astype(jnp.bfloat16).T, d_mixed, preferred_element_type=jnp.float32)
    d_normed = jnp.dot(d_mixed, weight_attn[:, : 3 * D].T, preferred_element_type=jnp.float32)
    d_flat, grad_gain_one = norm_back(d_normed)
    d_input = (d_middle + d_flat).astype(jnp.bfloat16).reshape(videos, SEQ, D)
    grads = (
        jnp.concatenate([grad_mix, grad_out], axis=1),
        grad_up,
        grad_down,
        jnp.stack([grad_gain_one, grad_gain_two]),
    )
    return (d_input, grads)


def valid_mask(frame_count):
    return (jnp.arange(SEQ)[None, :] // PATCHES < frame_count[:, None]).astype(jnp.float32)


def average(ema, weight, grad, rate):
    return rate * ema + (1.0 - rate) * (weight - LEARN_RATE * grad)


def gather_quant(proj, codebook):
    flat = jnp.concatenate([codebook.reshape(512), proj.reshape(32), jnp.zeros((480,), proj.dtype)])
    parts = gather_blocks(flat.astype(jnp.float32).reshape(8, 128)).reshape(128, 1024)
    parts = parts.astype(jnp.bfloat16)
    return (parts[:, 512:544].reshape(D, CODE_DIM), parts[:, :512])


def reduce_shards(grads, quant_grads):
    attn, up, down, gain = grads
    grad_proj, grad_code = quant_grads
    wide = [
        jnp.swapaxes(w.reshape(64, 8, 2, 1024), 1, 2).reshape(64, 16, 1024) for w in (attn, up)
    ]
    tall = jnp.swapaxes(down.reshape(64, 2, 16, 512), 1, 2).reshape(64, 16, 1024)
    few = jnp.concatenate(
        [
            grad_code[:64],
            grad_code[64:],
            jnp.swapaxes(gain.reshape(2, 64, 8), 0, 1).reshape(64, 16),
            grad_proj[:256].reshape(64, 32),
            grad_proj[256:].reshape(64, 32),
            jnp.zeros((64, 944), jnp.float32),
        ],
        axis=1,
    ).reshape(64, 16, 128)
    blocks = jnp.concatenate([wide[0], wide[1], tall, few], axis=2).astype(jnp.bfloat16)
    blocks = jnp.swapaxes(blocks.reshape(32, 2, 16, WIDE), 0, 1)
    total = scatter_blocks(blocks)
    rows = [
        jnp.swapaxes(total[:, i : i + 1024].reshape(2, 8, 1024), 0, 1).reshape(1, 8, 2048)
        for i in (0, 1024)
    ]
    down_rows = jnp.swapaxes(total[:, 2048:3072].reshape(16, 2, 512), 0, 1).reshape(1, 32, 512)
    few = total[:, 3072:].reshape(2048)
    gain_part = few[1024:1040].reshape(1, 2, 8)
    first_quant = jnp.concatenate([few[:512], few[1040:1072], jnp.zeros((480,), jnp.float32)])
    first_quant = lax.ppermute(first_quant.reshape(8, 128), "pipe", [(1, 0)]).reshape(1024)
    second_quant = jnp.concatenate([few[512:1024], few[1072:1104], jnp.zeros((480,), jnp.float32)])
    quant = jnp.where(lax.axis_index("pipe") == 0, first_quant, second_quant)
    return (
        rows[0],
        rows[1],
        down_rows,
        gain_part,
        quant[512:544].reshape(4, CODE_DIM),
        quant[:512].reshape(CODE_DIM, LOW_CODES),
    )


def per_device(
    video,
    cot_h,
    cot_q,
    frames,
    codes,
    w_attn,
    w_up,
    w_down,
    gains,
    proj,
    codebook,
    ema_attn,
    ema_up,
    ema_down,
    ema_gains,
    ema_proj,
    ema_code,
    decay,
):
    segment = lax.axis_index("pipe")
    first = segment == 0
    micro = video.shape[0]
    videos = video.shape[1]
    weights = (w_attn[0], w_up[0], w_down[0], gains[0])
    proj_all, code_table = gather_quant(proj, codebook)
    slots = micro + 2
    row_count = videos * SEQ

    def empty_saved():
        return (
            jnp.zeros((videos, SEQ, 3 * D), jnp.bfloat16),
            jnp.zeros((videos, SEQ, D), jnp.bfloat16),
            jnp.zeros((videos, SEQ, HEADS), jnp.float32),
            jnp.zeros((row_count, D), jnp.float32),
            jnp.zeros((row_count, FF), jnp.float32),
        )

    def empty_grads():
        return jax.tree.map(lambda w: jnp.zeros(w.shape, jnp.float32), weights)

    def empty_quant():
        return (jnp.zeros((D, CODE_DIM), jnp.float32), jnp.zeros((ROWS_OF_CODES, CODE_DIM * LOW_CODES), jnp.float32))

    def run_forward(inputs, frame_count):
        return block_forward(weights, inputs, frame_count, first)

    def skip_forward(inputs, frame_count):
        return (jnp.zeros_like(inputs), empty_saved())

    store_inputs = jnp.zeros((slots,) + video.shape[1:], jnp.bfloat16)
    store_outputs = jnp.zeros((slots,) + video.shape[1:], jnp.bfloat16)
    store_saved = jax.tree.map(lambda a: jnp.zeros((slots,) + a.shape, a.dtype), empty_saved())
    received = jnp.zeros_like(video[0])
    for tick in range(micro + 1):
        own = video[min(tick, micro - 1)]
        inputs = jnp.where(first, own, received)
        active = jnp.where(first, tick < micro, tick >= 1)
        index = jnp.clip(tick - segment, 0, micro - 1)
        frame_count = lax.dynamic_index_in_dim(frames, index, 0, keepdims=False)
        output, saved = lax.cond(active, run_forward, skip_forward, inputs, frame_count)
        which = tick - segment + 1
        store_inputs = lax.dynamic_update_index_in_dim(store_inputs, inputs, which, 0)
        store_outputs = lax.dynamic_update_index_in_dim(store_outputs, output, which, 0)
        store_saved = jax.tree.map(
            lambda buffer, value: lax.dynamic_update_index_in_dim(buffer, value, which, 0),
            store_saved,
            saved,
        )
        if tick < micro:
            received = from_behind(output, "pipe", 1)

    def from_next(out_low, code_now, cot_h_now, cot_q_now, valid, returned):
        return (returned.reshape(-1, D).astype(jnp.float32), empty_quant())

    def from_loss(out_low, code_now, cot_h_now, cot_q_now, valid, returned):
        rows = out_low.reshape(-1, D)
        mask = valid.reshape(-1, 1)
        latent = jnp.dot(rows, proj_all, preferred_element_type=jnp.float32)
        code = code_now.reshape(-1, 1)
        high = (code // LOW_CODES == jnp.arange(ROWS_OF_CODES)[None, :]).astype(jnp.bfloat16)
        low = (code % LOW_CODES == jnp.arange(LOW_CODES)[None, :])[:, None, :]
        near = jnp.dot(high, code_table, preferred_element_type=jnp.float32)
        chosen = jnp.sum(jnp.where(low, near.reshape(-1, CODE_DIM, LOW_CODES), 0.0), axis=2)
        cot_codes = jnp.swapaxes(cot_q_now, 1, 2).reshape(-1, CODE_DIM).astype(jnp.float32)
        d_latent = (cot_codes * mask + 2.0 * BETA * mask * (latent - chosen)).astype(jnp.bfloat16)
        d_chosen = (2.0 * mask * (chosen - latent)).astype(jnp.bfloat16)
        grad_proj = jnp.dot(rows.T, d_latent, preferred_element_type=jnp.float32)
        spread = jnp.where(low, d_chosen[:, :, None], 0).reshape(-1, CODE_DIM * LOW_CODES)
        grad_code = jnp.dot(high.T, spread, preferred_element_type=jnp.float32)
        d_rows = jnp.dot(d_latent, proj_all.T, preferred_element_type=jnp.float32)
        d_out = cot_h_now.reshape(-1, D).astype(jnp.float32) * mask + d_rows
        return (d_out, (grad_proj, grad_code))

    def run_backward(inputs, saved, out_low, frame_count, code_now, cot_h_now, cot_q_now, returned):
        valid = valid_mask(frame_count)
        d_out, quant_terms = lax.cond(
            first, from_next, from_loss, out_low, code_now, cot_h_now, cot_q_now, valid, returned
        )
        d_input, grads = block_backward(weights, inputs, saved, frame_count, first, d_out)
        return (d_input, grads, quant_terms)

    def skip_backward(
        inputs, saved, out_low, frame_count, code_now, cot_h_now, cot_q_now, returned
    ):
        return (jnp.zeros_like(inputs), empty_grads(), empty_quant())

    summed = empty_grads()
    quant_summed = empty_quant()
    store_back = jnp.zeros((slots,) + video.shape[1:], jnp.bfloat16)
    returned = jnp.zeros_like(video[0])
    for tick in range(micro + 1):
        index = jnp.clip(tick - 1 + segment, 0, micro - 1)
        slot = tick + segment
        active = jnp.where(first, tick >= 1, tick < micro)
        inputs = lax.dynamic_index_in_dim(store_inputs, slot, 0, keepdims=False)
        out_low = lax.dynamic_index_in_dim(store_outputs, slot, 0, keepdims=False)
        saved = jax.tree.map(
            lambda buffer: lax.dynamic_index_in_dim(buffer, slot, 0, keepdims=False), store_saved
        )
        frame_count = lax.dynamic_index_in_dim(frames, index, 0, keepdims=False)
        code_now = lax.dynamic_index_in_dim(codes, index, 0, keepdims=False)
        cot_h_now = lax.dynamic_index_in_dim(cot_h, index, 0, keepdims=False)
        cot_q_now = lax.dynamic_index_in_dim(cot_q, index, 0, keepdims=False)
        d_input, grads, quant_terms = lax.cond(
            active,
            run_backward,
            skip_backward,
            inputs,
            saved,
            out_low,
            frame_count,
            code_now,
            cot_h_now,
            cot_q_now,
            returned,
        )
        store_back = lax.dynamic_update_index_in_dim(store_back, d_input, slot, 0)
        quant_summed = jax.tree.map(lambda a, b: a + b, quant_summed, quant_terms)
        if tick < micro:
            returned = from_behind(d_input, "pipe", -1)
        summed = jax.tree.map(lambda a, b: a + b, summed, grads)
    g_attn, g_up, g_down, g_gains, g_proj, g_code = reduce_shards(summed, quant_summed)
    valid_all = (jnp.arange(SEQ)[None, None, :] // PATCHES < frames[:, :, None]).astype(
        jnp.float32
    )[..., None]
    acts = (store_outputs[1 : micro + 1].astype(jnp.float32) * valid_all).astype(jnp.bfloat16)[None]
    grad_in = store_back[1 : micro + 1][None]
    lane = lax.axis_index("dp")
    parts = lax.axis_size("dp")

    def own_rows(weight, axis):
        size = weight.shape[axis] // parts
        return lax.dynamic_slice_in_dim(weight, lane * size, size, axis).astype(jnp.float32)

    rate = lax.dynamic_index_in_dim(decay, segment, 0, keepdims=False)
    new_attn = average(ema_attn, own_rows(w_attn, 1), g_attn, rate)
    new_up = average(ema_up, own_rows(w_up, 1), g_up, rate)
    new_down = average(ema_down, own_rows(w_down, 1), g_down, rate)
    new_gains = average(ema_gains, own_rows(gains, 2), g_gains, rate)
    new_proj = average(ema_proj, proj.astype(jnp.float32), g_proj, decay[2])
    new_code = average(ema_code, codebook.astype(jnp.float32), g_code, decay[2])
    return (
        acts,
        grad_in,
        g_attn,
        g_up,
        g_down,
        g_gains,
        g_proj,
        g_code,
        new_attn,
        new_up,
        new_down,
        new_gains,
        new_proj,
        new_code,
    )


def solution(mesh):
    placed = (
        P(None, "dp", None, None),
        P(None, "dp", None, None),
        P(None, "dp", None, None),
        P(None, "dp"),
        P(None, "dp", None),
        P("pipe", None, None),
        P("pipe", None, None),
        P("pipe", None, None),
        P("pipe", None, None),
        P(("pipe", "dp"), None),
        P(None, ("pipe", "dp")),
        P("pipe", "dp", None),
        P("pipe", "dp", None),
        P("pipe", "dp", None),
        P("pipe", None, "dp"),
        P(("pipe", "dp"), None),
        P(None, ("pipe", "dp")),
        P(),
    )
    return jax.shard_map(
        per_device,
        mesh=mesh,
        in_specs=placed,
        out_specs=(
            P("pipe", None, "dp", None, None),
            P("pipe", None, "dp", None, None),
            P("pipe", "dp", None),
            P("pipe", "dp", None),
            P("pipe", "dp", None),
            P("pipe", None, "dp"),
            P(("pipe", "dp"), None),
            P(None, ("pipe", "dp")),
            P("pipe", "dp", None),
            P("pipe", "dp", None),
            P("pipe", "dp", None),
            P("pipe", None, "dp"),
            P(("pipe", "dp"), None),
            P(None, ("pipe", "dp")),
        ),
        check_vma=False,
    )
```

```python
import functools

import jax
import jax.numpy as jnp
from jax import lax
from jax.experimental import pallas as pl
from jax.experimental.pallas import tpu as pltpu
from jax.sharding import PartitionSpec as P

D = 512
HEADS = 8
HEAD_DIM = 64
FF = 2048
CODES = 8192
CODE_DIM = 8
LOW_CODES = 64
PATCHES = 64
FRAMES = 17
SEQ = 1088


EPSILON = 1e-05
BETA = 0.25
LEARN_RATE = 0.0001
MASKED = -1e30
MESH = pl.DeviceIdType.MESH
WIDE = 3200


def gather_kernel(block_ref, out_ref, landed, send_sems, recv_sems):
    pipe = lax.axis_index("pipe")
    dp = lax.axis_index("dp")
    own = pipe * 64 + dp

    def copy_to(step):
        target = lax.rem(dp + step, 64)
        return pltpu.make_async_remote_copy(
            src_ref=block_ref,
            dst_ref=landed.at[own],
            send_sem=send_sems.at[step],
            recv_sem=recv_sems.at[own],
            device_id=(1, target),
            device_id_type=MESH,
        )

    def start(step, carry):
        copy_to(step).start()
        return carry

    def finish(step, carry):
        copy_to(step).wait_send()
        return carry

    @pl.when(pipe == 0)
    def _():
        copy_to(0).start()

    lax.fori_loop(1, 64, start, 0)

    @pl.when(pipe == 0)
    def _():
        copy_to(0).wait_send()
        out_ref[...] = jnp.zeros_like(out_ref)

    lax.fori_loop(1, 64, finish, 0)

    @pl.when(pipe == 1)
    def _():
        landed[own] = block_ref[...]

        def arrive(step, carry):
            source = lax.rem(own + step, 128)
            pltpu.make_async_remote_copy(
                src_ref=block_ref,
                dst_ref=landed.at[source],
                send_sem=send_sems.at[0],
                recv_sem=recv_sems.at[source],
                device_id=(1, lax.rem(dp + 1, 64)),
                device_id_type=MESH,
            ).wait_recv()
            return carry

        lax.fori_loop(1, 128, arrive, 0)
        out_ref[...] = landed[...]


def gather_blocks(block):
    return pl.pallas_call(
        gather_kernel,
        out_shape=jax.ShapeDtypeStruct((128, 8, 128), jnp.float32),
        in_specs=[pl.BlockSpec(memory_space=pltpu.VMEM)],
        out_specs=pl.BlockSpec(memory_space=pltpu.VMEM),
        scratch_shapes=[
            pltpu.VMEM((128, 8, 128), jnp.float32),
            pltpu.SemaphoreType.DMA((64,)),
            pltpu.SemaphoreType.DMA((128,)),
        ],
        compiler_params=pltpu.CompilerParams(has_side_effects=True),
    )(block)


def chip_after(chip, step):
    x = lax.rem(lax.rem(chip, 4) + lax.rem(step, 4), 4)
    z = lax.rem(lax.rem(chip // 4, 2) + lax.rem(step // 4, 2), 2)
    y = lax.rem(chip // 8 + step // 8, 4)
    return (y * 2 + z) * 4 + x


def scatter_kernel(blocks, out_ref, mine, other, landed, local_sems, near_send, near_recv, far_send, far_recv):
    pipe = lax.axis_index("pipe")
    dp = lax.axis_index("dp")
    core = lax.rem(dp, 2)
    chip = dp // 2
    partner = dp + 1 - 2 * core

    def near(step):
        target = chip_after(chip, step)
        return pltpu.make_async_remote_copy(
            src_ref=blocks.at[target * 2 + 1 - core],
            dst_ref=other.at[target],
            send_sem=near_send.at[step],
            recv_sem=near_recv.at[step],
            device_id=(pipe, partner),
            device_id_type=MESH,
        )

    def local(step):
        target = chip_after(chip, step)
        return pltpu.make_async_copy(blocks.at[target * 2 + core], mine.at[target], local_sems.at[step])

    def far(step):
        target = chip_after(chip, step)
        return pltpu.make_async_remote_copy(
            src_ref=mine.at[target],
            dst_ref=landed.at[step],
            send_sem=far_send.at[step],
            recv_sem=far_recv.at[step],
            device_id=(pipe, target * 2 + core),
            device_id_type=MESH,
        )

    def begin(step, carry):
        at = lax.rem(step + 1, 32)
        near(at).start()
        local(at).start()
        return carry

    lax.fori_loop(0, 32, begin, 0)

    def pair(step, carry):
        target = chip_after(chip, step)
        local(step).wait()
        near(step).wait_recv()
        mine[target] = (mine[target].astype(jnp.float32) + other[target].astype(jnp.float32)).astype(jnp.bfloat16)
        far(step).start()
        return carry

    lax.fori_loop(1, 32, pair, 0)
    local(0).wait()
    near(0).wait_recv()
    out_ref[...] = mine[chip].astype(jnp.float32) + other[chip].astype(jnp.float32)

    def total(step, carry):
        far(step).wait_recv()
        out_ref[...] += landed[step].astype(jnp.float32)
        return carry

    lax.fori_loop(1, 32, total, 0)

    def finish(step, carry):
        near(step).wait_send()
        return carry

    lax.fori_loop(0, 32, finish, 0)

    def finish_far(step, carry):
        far(step).wait_send()
        return carry

    lax.fori_loop(1, 32, finish_far, 0)


def scatter_blocks(blocks):
    shape = (32, 16, WIDE)
    return pl.pallas_call(
        scatter_kernel,
        out_shape=jax.ShapeDtypeStruct((16, WIDE), jnp.float32),
        in_specs=[pl.BlockSpec(memory_space=pl.ANY)],
        out_specs=pl.BlockSpec(memory_space=pltpu.VMEM),
        scratch_shapes=[
            pltpu.VMEM(shape, jnp.bfloat16),
            pltpu.VMEM(shape, jnp.bfloat16),
            pltpu.VMEM(shape, jnp.bfloat16),
            pltpu.SemaphoreType.DMA((32,)),
            pltpu.SemaphoreType.DMA((32,)),
            pltpu.SemaphoreType.DMA((32,)),
            pltpu.SemaphoreType.DMA((32,)),
            pltpu.SemaphoreType.DMA((32,)),
        ],
        compiler_params=pltpu.CompilerParams(has_side_effects=True, vmem_limit_bytes=40 << 20),
    )(blocks)


BF = jnp.bfloat16
F32 = jnp.float32
SCALE = HEAD_DIM**-0.5
PAD = 1152
NN = (((1,), (0,)), ((), ()))
NT = (((1,), (1,)), ((), ()))
TN = (((0,), (0,)), ((), ()))
SPAN = 272
SPANS = SEQ // SPAN
WIDTH = 384
WIDTHS = PAD // WIDTH
COLUMNS = PAD // 128
ANY = pl.BlockSpec(memory_space=pl.ANY)
INSIDE = pl.BlockSpec(memory_space=pltpu.VMEM)
SCALARS = pl.BlockSpec(memory_space=pltpu.SMEM)


def dot(left, right, dims=NN):
    return lax.dot_general(left, right, dims, preferred_element_type=F32)


def normal(value):
    center = jnp.mean(value, axis=-1, keepdims=True)
    centred = value - center
    spread = jnp.mean(centred * centred, axis=-1, keepdims=True)
    rate = lax.rsqrt(spread + EPSILON)
    return centred * rate, rate


def normal_back(value, gain, d_normed):
    hat, rate = normal(value)
    scaled = d_normed * gain
    first = jnp.mean(scaled, axis=-1, keepdims=True)
    second = jnp.mean(scaled * hat, axis=-1, keepdims=True)
    terms = d_normed * hat
    return rate * (scaled - first - hat * second), fold_rows(terms), hat


def fold_rows(terms):
    return jnp.sum(terms.reshape(-1, 8, D), axis=0)


def gelu_pair(value):
    square = value * value
    inner = value * (0.7978845608028654 + 0.035677408136300125 * square)
    half = 0.5 + 0.5 * jnp.tanh(inner)
    out = value * half
    slope = half + out * (1.0 - half) * (1.5957691216057308 + 0.21406444881780075 * square)
    return out.astype(BF), slope.astype(BF)


def feed_forward(middle, gain, up, down, act_ref, slope_ref, rows):
    normed = (normal(middle)[0] * gain).astype(BF)
    total = middle
    for j in range(4):
        cols = slice(j * 512, (j + 1) * 512)
        act, slope = gelu_pair(dot(normed, up[:, cols]))
        act_ref[rows, cols] = act
        slope_ref[rows, cols] = slope
        total = total + dot(act, down[cols, :])
    return normed, total


def lane_is_low(shape):
    return lax.rem(lax.broadcasted_iota(jnp.int32, shape, len(shape) - 1), 128) < 64


def head_mask(shape):
    lane = lax.broadcasted_iota(jnp.int32, shape, 1)
    return [(lane >= 64 * h) & (lane < 64 * h + 64) for h in range(4)]


def spread_heads(value, masks):
    zero = jnp.zeros_like(value)
    return jnp.concatenate([jnp.where(m, value, zero) for m in masks], axis=0)


def fold_heads(value, masks):
    total = jnp.where(masks[0], value[:64], 0.0)
    for h in range(1, 4):
        total = total + jnp.where(masks[h], value[64 * h : 64 * h + 64], 0.0)
    return total


def per_head(value, low, reduce, neutral):
    parts = []
    for c in range(2):
        piece = value[:, 128 * c : 128 * c + 128]
        left = reduce(jnp.where(low, piece, neutral), axis=1, keepdims=True)
        right = reduce(jnp.where(low, neutral, piece), axis=1, keepdims=True)
        parts.append(jnp.where(low, left, right))
    return jnp.concatenate(parts, axis=1)


def spatial_frame(frame, mixed, probs_ref, context):
    rows = pl.ds(pl.multiple_of(frame * 64, 64), 64)
    low = lane_is_low((64, 128))
    masks = head_mask((64, 256))
    for g in range(2):
        cols = slice(g * 256, g * 256 + 256)
        query = mixed[rows, g * 256 : g * 256 + 256]
        keys = spread_heads(mixed[rows, 512 + g * 256 : 768 + g * 256], masks)
        values = spread_heads(mixed[rows, 1024 + g * 256 : 1280 + g * 256], masks)
        scores = dot(query, keys, NT) * SCALE
        power = jnp.exp(scores - per_head(scores, low, jnp.max, -jnp.inf))
        probs = (power / per_head(power, low, jnp.sum, 0.0)).astype(BF)
        probs_ref[rows, cols] = probs
        context[rows, cols] = dot(probs, values).astype(BF)


def spatial_frame_back(frame, mixed, probs_ref, d_context, d_mixed):
    rows = pl.ds(pl.multiple_of(frame * 64, 64), 64)
    low = lane_is_low((64, 128))
    masks = head_mask((64, 256))
    for g in range(2):
        cols = slice(g * 256, g * 256 + 256)
        query = mixed[rows, g * 256 : g * 256 + 256]
        keys = spread_heads(mixed[rows, 512 + g * 256 : 768 + g * 256], masks)
        values = spread_heads(mixed[rows, 1024 + g * 256 : 1280 + g * 256], masks)
        probs = probs_ref[rows, cols]
        d_out = d_context[rows, cols]
        wide = probs.astype(F32)
        d_probs = dot(d_out, values, NT)
        d_scores = (wide * (d_probs - per_head(d_probs * wide, low, jnp.sum, 0.0)) * SCALE).astype(BF)
        d_query = dot(d_scores, keys)
        d_keys = fold_heads(dot(d_scores, query, TN), masks)
        d_values = fold_heads(dot(probs, d_out, TN), masks)
        d_mixed[rows, g * 256 : g * 256 + 256] = d_query.astype(BF)
        d_mixed[rows, 512 + g * 256 : 768 + g * 256] = d_keys.astype(BF)
        d_mixed[rows, 1024 + g * 256 : 1280 + g * 256] = d_values.astype(BF)


def loop(count, body):
    def step(index, carry):
        body(index)
        return carry

    lax.fori_loop(0, count, step, 0)


def row_span(index, size):
    return pl.ds(pl.multiple_of(index * size, 16), size)


def valid_rows(start, size, count):
    row = lax.broadcasted_iota(jnp.int32, (size, 1), 0) + start
    return row < count * PATCHES


def first_forward_kernel(micro, *refs):
    (active, frames, video, w_attn, w_up, w_down, gains) = refs[:7]
    (acts, sent, s_mixed, s_context, s_probs, s_middle, s_act, s_slope) = refs[-21:-13]
    (x, attn, up, down, mixed, context, probs, middle, act, slope, out, masked, sems) = refs[-13:]

    @pl.when(active[0] == 1)
    def _():
        count = frames[micro, 0]
        loads = [
            pltpu.make_async_copy(video.at[micro, 0], x, sems.at[0]),
            pltpu.make_async_copy(w_attn, attn, sems.at[1]),
            pltpu.make_async_copy(w_up, up, sems.at[2]),
            pltpu.make_async_copy(w_down, down, sems.at[3]),
        ]
        for copy in loads:
            copy.start()
        loads[0].wait()
        loads[1].wait()

        def project(i):
            rows = row_span(i, SPAN)
            hat, _ = normal(x[rows, :].astype(F32))
            normed = (hat * gains[0:1, :]).astype(BF)
            for j in range(3):
                cols = slice(j * 512, (j + 1) * 512)
                mixed[rows, cols] = dot(normed, attn[:, cols]).astype(BF)

        loop(SPANS, project)
        stores = [pltpu.make_async_copy(mixed, s_mixed, sems.at[4])]
        stores[0].start()
        loop(FRAMES, lambda f: spatial_frame(f, mixed, probs, context))
        for k, (source, target) in enumerate(((context, s_context), (probs, s_probs))):
            stores.append(pltpu.make_async_copy(source, target, sems.at[5 + k]))
            stores[-1].start()
        loads[2].wait()
        loads[3].wait()

        def tail(i):
            rows = row_span(i, SPAN)
            here = x[rows, :].astype(F32) + dot(context[rows, :], attn[:, 1536:])
            middle[rows, :] = here
            _, total = feed_forward(here, gains[1:2, :], up, down, act, slope, rows)
            out[rows, :] = total.astype(BF)
            masked[rows, :] = jnp.where(valid_rows(i * SPAN, SPAN, count), total, 0.0).astype(BF)

        loop(SPANS, tail)
        late = ((out, sent), (masked, acts.at[micro]), (middle, s_middle), (act, s_act), (slope, s_slope))
        for k, (source, target) in enumerate(late):
            stores.append(pltpu.make_async_copy(source, target, sems.at[7 + k]))
            stores[-1].start()
        for copy in stores:
            copy.wait()


def saved_shapes():
    return [
        jax.ShapeDtypeStruct((SEQ, 3 * D), BF),
        jax.ShapeDtypeStruct((SEQ, D), BF),
        jax.ShapeDtypeStruct((SEQ, D), BF),
        jax.ShapeDtypeStruct((SEQ, D), F32),
        jax.ShapeDtypeStruct((SEQ, FF), BF),
        jax.ShapeDtypeStruct((SEQ, FF), BF),
    ]


def weight_scratch():
    return [pltpu.VMEM((D, 4 * D), BF), pltpu.VMEM((D, FF), BF), pltpu.VMEM((FF, D), BF)]


def first_forward(micro, active, frames, video, weights, acts=None):
    saved = saved_shapes()
    inputs = [active, frames, video, *weights] + ([] if acts is None else [acts])
    result = pl.pallas_call(
        functools.partial(first_forward_kernel, micro),
        out_shape=[jax.ShapeDtypeStruct((2, SEQ, D), BF), jax.ShapeDtypeStruct((SEQ, D), BF)] + saved,
        in_specs=([SCALARS, SCALARS, ANY, ANY, ANY, ANY, INSIDE, ANY])[: len(inputs)],
        out_specs=[ANY] * 8,
        input_output_aliases={} if acts is None else {7: 0},
        scratch_shapes=[pltpu.VMEM((SEQ, D), BF)] + weight_scratch()
        + [pltpu.VMEM(s.shape, s.dtype) for s in saved]
        + [pltpu.VMEM((SEQ, D), BF), pltpu.VMEM((SEQ, D), BF), pltpu.SemaphoreType.DMA((12,))],
        compiler_params=pltpu.CompilerParams(vmem_limit_bytes=60 << 20),
        name=f"first_forward_{micro}",
    )(*inputs)
    return result[0], result[1], result[2:]


def add_grad(total, fresh):
    def write(rows, cols, value):
        if fresh:
            total[rows, cols] = value
        else:
            total[rows, cols] = total[rows, cols] + value

    return write


def write_blocks(g_attn, g_up, g_down, few, block_out, blocks, sems):
    def piece(group):
        return pltpu.make_async_copy(
            block_out.at[group % 2], blocks.at[pl.ds(group * 16, 16)], sems.at[16 + group % 2]
        )

    for group in range(4):
        if group >= 2:
            piece(group - 2).wait()

        def one(i, group=group):
            j = group * 16 + i
            rows = pl.ds(pl.multiple_of(j * 8, 8), 8)
            for k, ref in enumerate((g_attn, g_up)):
                value = ref[rows, :]
                block_out[group % 2, i, :, k * 1024 : (k + 1) * 1024] = jnp.concatenate(
                    [value[:, :1024], value[:, 1024:]], axis=0
                ).astype(BF)
            value = g_down[pl.ds(pl.multiple_of(j * 32, 32), 32), :]
            block_out[group % 2, i, :, 2048:3072] = jnp.concatenate(
                [value[:16], value[16:]], axis=1
            ).astype(BF)
            block_out[group % 2, i, :, 3072:] = few[j].astype(BF)

        loop(16, one)
        piece(group).start()
    piece(2).wait()
    piece(3).wait()


def spread_gains(g_gains, few):
    dst = lax.broadcasted_iota(jnp.int32, (64, D), 0)
    lane = lax.broadcasted_iota(jnp.int32, (64, D), 1)
    source = lax.broadcasted_iota(jnp.int32, (D, 128), 0)
    place = lax.broadcasted_iota(jnp.int32, (D, 128), 1)
    total = jnp.zeros((64, 128), F32)
    for k in range(2):
        row = jnp.sum(g_gains[8 * k : 8 * k + 8, :], axis=0, keepdims=True)
        mine = jnp.where(lane // 8 == dst, row, 0.0)
        pick = (lax.rem(source, 8) + 8 * k == place).astype(F32)
        total = total + lax.dot_general(mine, pick, NN, precision=lax.Precision.HIGHEST, preferred_element_type=F32)
    few[:, 8, :] = total


def first_backward_kernel(micro, fresh, *refs):
    (active, video, w_attn, w_up, w_down, gains, d_in, s_mixed, s_context, s_probs, s_middle, s_act, s_slope) = refs[:13]
    if fresh:
        _, grad_in, new_attn, new_up, new_down, new_gains = refs[13:19]
        rest = refs[19:]
    else:
        _, _, old_attn, old_up, old_down, old_gains, grad_in, blocks = refs[13:21]
        rest = refs[21:]
    (x, attn, up, down, mixed, context, probs, middle, act, slope, d_two, normed, d_branch, d_mid, d_context,
     g_attn, g_up, g_down, g_gains, few, block_out, sems) = rest
    last = not fresh

    @pl.when(active[0] == 1)
    def _():
        pairs = [
            (d_in, d_two), (w_down, down), (s_slope, slope), (w_up, up), (s_middle, middle), (s_act, act),
            (w_attn, attn), (s_context, context), (s_probs, probs), (s_mixed, mixed), (video.at[micro, 0], x),
        ]
        if not fresh:
            pairs += [(old_down, g_down), (old_up, g_up), (old_attn, g_attn), (old_gains, g_gains)]
        loads = [pltpu.make_async_copy(s, t, sems.at[k]) for k, (s, t) in enumerate(pairs)]
        for copy in loads:
            copy.start()
        if fresh:
            g_gains[...] = jnp.zeros_like(g_gains)
        else:
            loads[14].wait()
        for k in range(5):
            loads[k].wait()
        gain = gains[1:2, :]

        def tail(i):
            rows = row_span(i, SPAN)
            d_low = d_two[rows, :]
            total = jnp.zeros((SPAN, D), F32)
            for j in range(4):
                cols = slice(j * 512, (j + 1) * 512)
                d_hidden = (dot(d_low, down[cols, :], NT) * slope[rows, cols].astype(F32)).astype(BF)
                slope[rows, cols] = d_hidden
                total = total + dot(d_hidden, up[:, cols], NT)
            here = middle[rows, :]
            d_here, g_rows, hat = normal_back(here, gain, total)
            g_gains[8:16, :] += g_rows
            normed[rows, :] = (hat * gain).astype(BF)
            d_here = d_low.astype(F32) + d_here
            d_mid[rows, :] = d_here
            d_branch[rows, :] = d_here.astype(BF)

        loop(SPANS, tail)
        loads[5].wait()
        if not fresh:
            loads[11].wait()
            loads[12].wait()
        put_down = add_grad(g_down, fresh)
        put_up = add_grad(g_up, fresh)
        put_attn = add_grad(g_attn, fresh)
        for j in range(4):
            cols = slice(j * 512, (j + 1) * 512)
            put_down(cols, slice(None), dot(act[:, cols], d_two[...], TN))
            put_up(slice(None), cols, dot(normed[...], slope[:, cols], TN))
        loads[6].wait()
        loads[7].wait()
        if not fresh:
            loads[13].wait()
        put_attn(slice(None), slice(1536, 2048), dot(context[...], d_branch[...], TN))

        def into_context(i):
            rows = row_span(i, SPAN)
            d_context[rows, :] = dot(d_branch[rows, :], attn[:, 1536:], NT).astype(BF)

        loop(SPANS, into_context)
        for k in range(8, 11):
            loads[k].wait()
        d_mixed = act
        loop(FRAMES, lambda f: spatial_frame_back(f, mixed, probs, d_context, d_mixed))
        gain_one = gains[0:1, :]

        def head(i):
            rows = row_span(i, SPAN)
            total = jnp.zeros((SPAN, D), F32)
            for j in range(3):
                cols = slice(j * 512, (j + 1) * 512)
                total = total + dot(d_mixed[rows, cols], attn[:, cols], NT)
            d_here, g_rows, hat = normal_back(x[rows, :].astype(F32), gain_one, total)
            g_gains[0:8, :] += g_rows
            normed[rows, :] = (hat * gain_one).astype(BF)
            d_branch[rows, :] = (d_mid[rows, :] + d_here).astype(BF)

        loop(SPANS, head)
        for j in range(3):
            cols = slice(j * 512, (j + 1) * 512)
            put_attn(slice(None), cols, dot(normed[...], d_mixed[:, cols], TN))
        targets = [(d_branch, grad_in.at[micro])]
        if fresh:
            targets += [(g_attn, new_attn), (g_up, new_up), (g_down, new_down), (g_gains, new_gains)]
        stores = [pltpu.make_async_copy(s, t, sems.at[15 + k]) for k, (s, t) in enumerate(targets)]
        for copy in stores:
            copy.start()
        if last:
            few[...] = jnp.zeros_like(few)
            spread_gains(g_gains, few)
            write_blocks(g_attn, g_up, g_down, few, block_out, blocks, sems)
        for copy in stores:
            copy.wait()


def grad_shapes():
    return [
        jax.ShapeDtypeStruct((D, 4 * D), F32),
        jax.ShapeDtypeStruct((D, FF), F32),
        jax.ShapeDtypeStruct((FF, D), F32),
        jax.ShapeDtypeStruct((16, D), F32),
    ]


def first_backward(micro, active, video, weights, d_in, saved, grad_in, blocks=None, grads=None):
    shapes = grad_shapes()
    kept = saved_shapes()
    rows = pltpu.VMEM((SEQ, D), BF)
    fresh = grads is None
    inputs = [active, video, *weights, d_in, *saved, grad_in]
    outputs = [jax.ShapeDtypeStruct(grad_in.shape, BF)]
    aliases = {13: 0}
    if fresh:
        outputs += shapes
    else:
        inputs += [blocks, *grads]
        outputs += [jax.ShapeDtypeStruct(blocks.shape, BF)]
        aliases = {13: 0, 14: 1}
    result = pl.pallas_call(
        functools.partial(first_backward_kernel, micro, fresh),
        out_shape=outputs,
        in_specs=[SCALARS, ANY, ANY, ANY, ANY, INSIDE] + [ANY] * (len(inputs) - 6),
        out_specs=[ANY] * len(outputs),
        input_output_aliases=aliases,
        scratch_shapes=[rows] + weight_scratch() + [pltpu.VMEM(s.shape, s.dtype) for s in kept]
        + [rows, rows, rows, pltpu.VMEM((SEQ, D), F32), rows]
        + [pltpu.VMEM(s.shape, s.dtype) for s in shapes]
        + [pltpu.VMEM((64, 16, 128), F32), pltpu.VMEM((2, 16, 16, WIDE), BF), pltpu.SemaphoreType.DMA((20,))],
        compiler_params=pltpu.CompilerParams(vmem_limit_bytes=63 << 20),
        name=f"first_backward_{micro}",
    )(*inputs)
    return result[0], (result[1:] if fresh else result[1])


def column(index):
    return slice(index * 128, index * 128 + 128)


def load_head(head, mixed, refs, scale):
    for part, (ref, turned) in enumerate(refs):
        rows = pl.ds(pl.multiple_of(part * D + head * HEAD_DIM, HEAD_DIM), HEAD_DIM)
        for c in range(COLUMNS):
            value = mixed[rows, column(c)].astype(F32)
            if part == 0 and scale:
                value = value * SCALE
            ref[:, column(c)] = value
            if turned is not None:
                turned[:, column(c)] = pltpu.roll(value, 64, 1)


def pair_rows(left, refs, a, rows_ref):
    for s, ref in enumerate(refs):
        for b in range(a + 1):
            rows_ref[9 * s + b : 9 * s + b + 1, :] = jnp.sum(left * ref[:, column(b)], axis=0, keepdims=True)


def weighted(rows_ref, refs, a):
    total = None
    for s, ref in enumerate(refs):
        for b in range(a + 1):
            term = rows_ref[9 * s + b : 9 * s + b + 1, :] * ref[:, column(b)]
            total = term if total is None else total + term
    return total


def temporal_head(head, order, mixed, probs, context, q, k, v, kt, vt, rows_ref):
    load_head(head, mixed, ((q, None), (k, kt), (v, vt)), True)
    out_rows = pl.ds(pl.multiple_of(head * HEAD_DIM, HEAD_DIM), HEAD_DIM)
    for a in range(COLUMNS):
        pair_rows(q[:, column(a)], (k, kt), a, rows_ref)
        scores = jnp.where(order[...] <= 2 * a, rows_ref[...], MASKED)
        power = jnp.exp(scores - jnp.max(scores, axis=0, keepdims=True))
        probs[head, a] = power / jnp.sum(power, axis=0, keepdims=True)
        context[out_rows, column(a)] = weighted(probs.at[head, a], (v, vt), a).astype(BF)


def temporal_head_back(head, mixed, probs, d_context, q, k, v, kt, vt, dc, rows_ref, ds):
    load_head(head, mixed, ((q, None), (k, kt), (v, vt)), False)
    in_rows = pl.ds(pl.multiple_of(head * HEAD_DIM, HEAD_DIM), HEAD_DIM)
    for c in range(COLUMNS):
        dc[:, column(c)] = d_context[in_rows, column(c)].astype(F32)
    for a in range(COLUMNS):
        pair_rows(dc[:, column(a)], (v, vt), a, rows_ref)
        p = probs[head, a]
        d_probs = jnp.where(p > 0.0, rows_ref[...], 0.0)
        delta = jnp.sum(d_probs * p, axis=0, keepdims=True)
        ds[a] = p * (d_probs - delta) * SCALE
        mixed[in_rows, column(a)] = weighted(ds.at[a], (k, kt), a).astype(BF)
    for part, (weight, source) in enumerate(((lambda a, r: ds[a, r : r + 1, :], q), (lambda a, r: probs[head, a, r : r + 1, :], dc))):
        rows = pl.ds(pl.multiple_of((part + 1) * D + head * HEAD_DIM, HEAD_DIM), HEAD_DIM)
        for b in range(COLUMNS):
            sums = []
            for s in range(2):
                total = None
                for a in range(b, COLUMNS):
                    term = weight(a, 9 * s + b) * source[:, column(a)]
                    total = term if total is None else total + term
                sums.append(total)
            mixed[rows, column(b)] = (sums[0] + pltpu.roll(sums[1], 64, 1)).astype(BF)


def frame_order(count):
    row = lax.broadcasted_iota(jnp.int32, (24, 128), 0)
    high = (lax.broadcasted_iota(jnp.int32, (24, 128), 1) >= 64).astype(jnp.int32)
    turned = row >= 9
    base = 2 * jnp.where(turned, row - 9, row)
    key_frame = base + jnp.where(turned, 1 - high, high)
    return jnp.where((row < 18) & (key_frame < count), key_frame - high, 1000)


def second_kernel(micro, fresh, *refs):
    (active, frames, received, w_out, w_turned, w_up, w_down, gains, cot_h, cot_q, codes, table, proj) = refs[:13]
    if fresh:
        _, acts, grad_in, sent_back, new_turned, new_out, new_up, new_down, new_gains, new_proj, new_code = refs[13:24]
        rest = refs[24:]
    else:
        (_, _, old_turned, old_out, old_up, old_down, old_gains, old_proj, old_code, acts, grad_in, sent_back, blocks) = refs[13:26]
        rest = refs[26:]
    (x, attn_out, turned, up, down, normed, normed_two, mixed, context, d_context, probs, middle, act, slope, out,
     masked, d_mid, d_two, cot, cot_codes, code_rows, g_turned, g_attn, g_up, g_down, g_gains, g_proj, g_code,
     q, k, v, kt, vt, dc, rows_ref, ds, order, few, block_out, sems) = rest
    last = not fresh

    @pl.when(active[0] == 1)
    def _():
        count = frames[micro, 0]
        real = pl.ds(0, SEQ)
        pairs = [
            (received, x.at[real]), (w_turned, turned), (w_out, attn_out), (w_up, up), (w_down, down),
            (codes.at[micro], code_rows.at[real]), (cot_q.at[micro], cot_codes.at[real]), (cot_h.at[micro, 0], cot.at[real]),
        ]
        if last:
            pairs += [
                (old_proj, g_proj), (old_code, g_code), (old_gains, g_gains), (old_down, g_down), (old_up, g_up),
                (old_out, g_attn.at[:, pl.ds(1536, 512)]), (old_turned, g_turned),
            ]
        loads = [pltpu.make_async_copy(s, t, sems.at[i]) for i, (s, t) in enumerate(pairs)]
        for copy in loads:
            copy.start()
        tail_rows = pl.ds(SEQ, PAD - SEQ)
        x[tail_rows, :] = jnp.zeros((PAD - SEQ, D), BF)
        cot[tail_rows, :] = jnp.zeros((PAD - SEQ, D), BF)
        cot_codes[tail_rows, :] = jnp.zeros((PAD - SEQ, 128), BF)
        code_rows[tail_rows, :] = jnp.zeros((PAD - SEQ, 128), jnp.int32)
        rows_ref[...] = jnp.zeros_like(rows_ref)
        order[...] = frame_order(count)
        if fresh:
            g_gains[...] = jnp.zeros_like(g_gains)
            g_proj[...] = jnp.zeros_like(g_proj)
            g_code[...] = jnp.zeros_like(g_code)
        gain_one, gain_two = gains[0:1, :], gains[1:2, :]
        loads[0].wait()
        loads[1].wait()
        for i in range(WIDTHS):
            rows = slice(i * WIDTH, (i + 1) * WIDTH)
            normed[rows, :] = (normal(x[rows, :].astype(F32))[0] * gain_one).astype(BF)
            for j in range(3):
                parts = slice(j * 512, (j + 1) * 512)
                mixed[parts, rows] = dot(turned[parts, :], normed[rows, :], NT).astype(BF)
        loop(HEADS, lambda h: temporal_head(h, order, mixed, probs, context, q, k, v, kt, vt, rows_ref))
        for i in range(2, 8 if fresh else 11):
            loads[i].wait()

        def forward_tail(i):
            rows = row_span(i, WIDTH)
            here = middle[rows, :]
            normed_low, total = feed_forward(here, gain_two, up, down, act, slope, rows)
            normed_two[rows, :] = normed_low
            valid = valid_rows(i * WIDTH, WIDTH, count)
            low = total.astype(BF)
            out[rows, :] = low
            masked[rows, :] = jnp.where(valid, total, 0.0).astype(BF)
            mask = valid.astype(F32)
            latent = dot(low, proj[...])
            code = code_rows[rows, :]
            lane = lax.broadcasted_iota(jnp.int32, (WIDTH, 128), 1)
            high = (lax.div(code, LOW_CODES) == lane).astype(BF)
            near = dot(high, table[...])
            spot = lax.rem(code, LOW_CODES) == lax.rem(lane, LOW_CODES)
            spots = jnp.concatenate([spot] * 4, axis=1)
            place = lax.div(lax.broadcasted_iota(jnp.int32, (512, 128), 0), LOW_CODES)
            pick = (place == lax.broadcasted_iota(jnp.int32, (512, 128), 1)).astype(BF)
            chosen = dot(jnp.where(spots, near, 0.0).astype(BF), pick)
            d_latent = (mask * (cot_codes[rows, :].astype(F32) + 2.0 * BETA * (latent - chosen))).astype(BF)
            d_chosen = (2.0 * mask * (chosen - latent)).astype(BF)
            g_proj[...] += dot(low, d_latent, TN)
            spread = jnp.where(spots, dot(d_chosen, pick, NT), 0.0).astype(BF)
            g_code[...] += dot(high, spread, TN)
            d_out = cot[rows, :].astype(F32) * mask + dot(d_latent, proj[...], NT)
            d_two[rows, :] = d_out.astype(BF)
            d_mid[rows, :] = d_out

        for i in range(WIDTHS):
            rows = slice(i * WIDTH, (i + 1) * WIDTH)
            middle[rows, :] = x[rows, :].astype(F32) + dot(context[:, rows], attn_out[...], TN)
        loop(WIDTHS, forward_tail)
        stores = [pltpu.make_async_copy(masked.at[real], acts.at[micro], sems.at[18])]
        stores[0].start()
        d_branch = out

        def backward_tail(i):
            rows = row_span(i, WIDTH)
            d_low = d_two[rows, :]
            total = jnp.zeros((WIDTH, D), F32)
            for j in range(4):
                cols = slice(j * 512, (j + 1) * 512)
                d_hidden = (dot(d_low, down[cols, :], NT) * slope[rows, cols].astype(F32)).astype(BF)
                slope[rows, cols] = d_hidden
                total = total + dot(d_hidden, up[:, cols], NT)
            d_here, g_rows, _ = normal_back(middle[rows, :], gain_two, total)
            g_gains[8:16, :] += g_rows
            d_here = d_mid[rows, :] + d_here
            d_mid[rows, :] = d_here
            d_branch[rows, :] = d_here.astype(BF)

        loop(WIDTHS, backward_tail)
        if last:
            for i in range(11, 15):
                loads[i].wait()
        put_down = add_grad(g_down, fresh)
        put_up = add_grad(g_up, fresh)
        put_attn = add_grad(g_attn, fresh)
        put_turned = add_grad(g_turned, fresh)
        every = slice(None)
        for j in range(4):
            cols = slice(j * 512, (j + 1) * 512)
            put_down(cols, every, dot(act[:, cols], d_two[...], TN))
            put_up(every, cols, dot(normed_two[...], slope[:, cols], TN))
        put_attn(every, slice(1536, 2048), dot(context[...], d_branch[...]))
        for i in range(WIDTHS):
            rows = slice(i * WIDTH, (i + 1) * WIDTH)
            d_context[:, rows] = dot(attn_out[...], d_branch[rows, :], NT).astype(BF)
        loop(
            HEADS,
            lambda h: temporal_head_back(h, mixed, probs, d_context, q, k, v, kt, vt, dc, rows_ref, ds),
        )
        for i in range(WIDTHS):
            rows = slice(i * WIDTH, (i + 1) * WIDTH)
            total = dot(mixed[:, rows], turned[...], TN)
            d_here, g_rows, _ = normal_back(x[rows, :].astype(F32), gain_one, total)
            g_gains[0:8, :] += g_rows
            d_two[rows, :] = (d_mid[rows, :] + d_here).astype(BF)
        targets = [(d_two.at[real], sent_back), (d_two.at[real], grad_in.at[micro])]
        for j in range(3):
            parts = slice(j * 512, (j + 1) * 512)
            put_turned(parts, every, dot(mixed[parts, :], normed[...]))
        if fresh:
            targets += [
                (g_turned, new_turned), (g_attn.at[:, pl.ds(1536, 512)], new_out), (g_up, new_up), (g_down, new_down),
                (g_gains, new_gains), (g_proj, new_proj), (g_code, new_code),
            ]
        stores += [pltpu.make_async_copy(s, t, sems.at[19 + i]) for i, (s, t) in enumerate(targets)]
        for copy in stores[1:]:
            copy.start()
        if last:
            for j in range(3):
                cols = slice(j * 512, (j + 1) * 512)
                g_attn[:, cols] = g_turned[cols, :].T
            few[...] = jnp.zeros_like(few)
            spread_gains(g_gains, few)
            for j in range(4):
                few[:, j, :] = g_code[0:64, column(j)]
                few[:, 4 + j, :] = g_code[64:128, column(j)]
            for j in range(4):
                first = g_proj[pl.ds(j, 64, stride=4), :]
                second = g_proj[pl.ds(256 + j, 64, stride=4), :]
                few[:, 9 + j, :] = first + pltpu.roll(second, 64, 1)
            write_blocks(g_attn, g_up, g_down, few, block_out, blocks, sems)
        for copy in stores:
            copy.wait()


def second_grad_shapes():
    return [
        jax.ShapeDtypeStruct((3 * D, D), F32),
        jax.ShapeDtypeStruct((D, D), F32),
        jax.ShapeDtypeStruct((D, FF), F32),
        jax.ShapeDtypeStruct((FF, D), F32),
        jax.ShapeDtypeStruct((16, D), F32),
        jax.ShapeDtypeStruct((D, 128), F32),
        jax.ShapeDtypeStruct((128, 512), F32),
    ]


def second_section(micro, active, frames, received, weights, cots, acts, grad_in=None, grads=None):
    fresh = grads is None
    inputs = [active, frames, received, *weights, *cots, acts]
    outputs = [
        jax.ShapeDtypeStruct(acts.shape, BF),
        jax.ShapeDtypeStruct(acts.shape, BF),
        jax.ShapeDtypeStruct((SEQ, D), BF),
    ]
    aliases = {13: 0}
    if fresh:
        outputs += second_grad_shapes()
    else:
        inputs += [grad_in, *grads]
        outputs += [jax.ShapeDtypeStruct((64, 16, WIDE), BF)]
        aliases = {13: 0, 14: 1}
    tokens = pltpu.VMEM((PAD, D), BF)
    tokens_wide = pltpu.VMEM((PAD, D), F32)
    flipped = pltpu.VMEM((D, PAD), BF)
    hidden = pltpu.VMEM((PAD, FF), BF)
    one_head = pltpu.VMEM((HEAD_DIM, PAD), F32)
    scratch = [
        tokens, pltpu.VMEM((D, D), BF), pltpu.VMEM((3 * D, D), BF), pltpu.VMEM((D, FF), BF), pltpu.VMEM((FF, D), BF),
        tokens, tokens, pltpu.VMEM((3 * D, PAD), BF), flipped, flipped, pltpu.VMEM((HEADS, COLUMNS, 24, 128), F32),
        tokens_wide, hidden, hidden, tokens, tokens, tokens_wide, tokens, tokens, pltpu.VMEM((PAD, 128), BF),
        pltpu.VMEM((PAD, 128), jnp.int32), pltpu.VMEM((3 * D, D), F32), pltpu.VMEM((D, 4 * D), F32),
        pltpu.VMEM((D, FF), F32), pltpu.VMEM((FF, D), F32), pltpu.VMEM((16, D), F32), pltpu.VMEM((D, 128), F32),
        pltpu.VMEM((128, 512), F32),
    ]
    scratch += [one_head] * 6 + [
        pltpu.VMEM((24, 128), F32), pltpu.VMEM((COLUMNS, 24, 128), F32), pltpu.VMEM((24, 128), jnp.int32),
        pltpu.VMEM((64, 16, 128), F32), pltpu.VMEM((2, 16, 16, WIDE), BF), pltpu.SemaphoreType.DMA((30,)),
    ]
    specs = [SCALARS, SCALARS, ANY, ANY, ANY, ANY, ANY, INSIDE, ANY, ANY, ANY, INSIDE, INSIDE]
    result = pl.pallas_call(
        functools.partial(second_kernel, micro, fresh),
        out_shape=outputs,
        in_specs=specs + [ANY] * (len(inputs) - 13),
        out_specs=[ANY] * len(outputs),
        input_output_aliases=aliases,
        scratch_shapes=scratch,
        compiler_params=pltpu.CompilerParams(vmem_limit_bytes=63 << 20),
        name=f"second_section_{micro}",
    )(*inputs)
    return result[0], result[1], result[2], (result[3:] if fresh else result[3])


def average(ema, weight, grad, rate):
    return rate * ema + (1.0 - rate) * (weight - LEARN_RATE * grad)


def per_device(
    video, cot_h, cot_q, frames, codes, w_attn, w_up, w_down, gains, proj, codebook,
    ema_attn, ema_up, ema_down, ema_gains, ema_proj, ema_code, decay,
):
    segment = lax.axis_index("pipe")
    in_first = (segment == 0).astype(jnp.int32).reshape(1)
    in_second = 1 - in_first
    weights = (w_attn[0], w_up[0], w_down[0], gains[0])

    acts, sent_0, saved_0 = first_forward(0, in_first, frames, video, weights)
    received_0 = lax.ppermute(sent_0, "pipe", [(0, 1)])
    acts, sent_1, saved_1 = first_forward(1, in_first, frames, video, weights, acts)
    received_1 = lax.ppermute(sent_1, "pipe", [(0, 1)])

    wide_attn, proj, codebook, cot_q, codes, _ = lax.optimization_barrier(
        (w_attn[0], proj, codebook, cot_q, codes, sent_1)
    )
    flat = jnp.concatenate([codebook.reshape(512), proj.reshape(32), jnp.zeros((480,), proj.dtype)])
    parts = gather_blocks(flat.astype(F32).reshape(8, 128)).reshape(128, 1024).astype(BF)
    table = parts[:, :512]
    proj_all = jnp.pad(parts[:, 512:544].reshape(D, CODE_DIM), ((0, 0), (0, 120)))
    cot_rows = jnp.pad(jnp.swapaxes(cot_q[:, 0], 1, 2), ((0, 0), (0, 0), (0, 120)))
    code_rows = jnp.broadcast_to(codes[:, 0, :, None], (2, SEQ, 128))
    second_weights = (wide_attn[:, 3 * D :], wide_attn[:, : 3 * D].T, w_up[0], w_down[0], gains[0])
    cots = (cot_h, cot_rows, code_rows, table, proj_all)

    acts, grad_in, back_0, grads = second_section(
        0, in_second, frames, received_0, second_weights, cots, acts
    )
    returned_0 = lax.ppermute(back_0, "pipe", [(1, 0)])
    acts, grad_in, back_1, blocks = second_section(
        1, in_second, frames, received_1, second_weights, cots, acts, grad_in, grads
    )
    returned_1 = lax.ppermute(back_1, "pipe", [(1, 0)])
    grad_in, first_grads = first_backward(0, in_first, video, weights, returned_0, saved_0, grad_in)
    grad_in, blocks = first_backward(
        1, in_first, video, weights, returned_1, saved_1, grad_in, blocks, first_grads
    )

    total = scatter_blocks(blocks)
    g_attn, g_up = (
        jnp.swapaxes(total[:, i : i + 1024].reshape(2, 8, 1024), 0, 1).reshape(1, 8, 2048)
        for i in (0, 1024)
    )
    g_down = jnp.swapaxes(total[:, 2048:3072].reshape(16, 2, 512), 0, 1).reshape(1, 32, 512)
    few = total[:, 3072:]
    g_gains = few[8, :16].reshape(1, 2, 8)
    few = jnp.where(segment == 0, lax.ppermute(few, "pipe", [(1, 0)]), jnp.concatenate([few[4:8], few[:4], few[8:]], axis=0))
    g_code = few[:4].reshape(CODE_DIM, LOW_CODES)
    g_proj = jnp.where(segment == 0, few[9:13, :8], few[9:13, 64:72])
    lane = lax.axis_index("dp")
    parts = lax.axis_size("dp")

    def own_rows(weight, axis):
        size = weight.shape[axis] // parts
        return lax.dynamic_slice_in_dim(weight, lane * size, size, axis).astype(F32)

    rate = lax.dynamic_index_in_dim(decay, segment, 0, keepdims=False)
    return (
        acts[None, :, None],
        grad_in[None, :, None],
        g_attn,
        g_up,
        g_down,
        g_gains,
        g_proj,
        g_code,
        average(ema_attn, own_rows(w_attn, 1), g_attn, rate),
        average(ema_up, own_rows(w_up, 1), g_up, rate),
        average(ema_down, own_rows(w_down, 1), g_down, rate),
        average(ema_gains, own_rows(gains, 2), g_gains, rate),
        average(ema_proj, proj.astype(F32), g_proj, decay[2]),
        average(ema_code, codebook.astype(F32), g_code, decay[2]),
    )


def solution(mesh):
    placed = (
        P(None, "dp", None, None),
        P(None, "dp", None, None),
        P(None, "dp", None, None),
        P(None, "dp"),
        P(None, "dp", None),
        P("pipe", None, None),
        P("pipe", None, None),
        P("pipe", None, None),
        P("pipe", None, None),
        P(("pipe", "dp"), None),
        P(None, ("pipe", "dp")),
        P("pipe", "dp", None),
        P("pipe", "dp", None),
        P("pipe", "dp", None),
        P("pipe", None, "dp"),
        P(("pipe", "dp"), None),
        P(None, ("pipe", "dp")),
        P(),
    )
    return jax.shard_map(
        per_device,
        mesh=mesh,
        in_specs=placed,
        out_specs=(
            P("pipe", None, "dp", None, None),
            P("pipe", None, "dp", None, None),
            P("pipe", "dp", None),
            P("pipe", "dp", None),
            P("pipe", "dp", None),
            P("pipe", None, "dp"),
            P(("pipe", "dp"), None),
            P(None, ("pipe", "dp")),
            P("pipe", "dp", None),
            P("pipe", "dp", None),
            P("pipe", "dp", None),
            P("pipe", None, "dp"),
            P(("pipe", "dp"), None),
            P(None, ("pipe", "dp")),
        ),
        check_vma=False,
    )
```

```python
import functools

import jax
import jax.numpy as jnp
from jax import lax
from jax.experimental import pallas as pl
from jax.experimental.pallas import tpu as pltpu
from jax.sharding import PartitionSpec as P

D = 512
HEADS = 8
HEAD_DIM = 64
FF = 2048
CODES = 8192
CODE_DIM = 8
LOW_CODES = 64
PATCHES = 64
FRAMES = 17
SEQ = 1088


EPSILON = 1e-05
BETA = 0.25
LEARN_RATE = 0.0001
MASKED = -1e30
MESH = pl.DeviceIdType.MESH
WIDE = 3200


def gather_kernel(block_ref, out_ref, landed, send_sems, recv_sems):
    pipe = lax.axis_index("pipe")
    dp = lax.axis_index("dp")
    own = pipe * 64 + dp

    def copy_to(step):
        target = lax.rem(dp + step, 64)
        return pltpu.make_async_remote_copy(
            src_ref=block_ref,
            dst_ref=landed.at[own],
            send_sem=send_sems.at[step],
            recv_sem=recv_sems.at[own],
            device_id=(1, target),
            device_id_type=MESH,
        )

    def start(step, carry):
        copy_to(step).start()
        return carry

    def finish(step, carry):
        copy_to(step).wait_send()
        return carry

    @pl.when(pipe == 0)
    def _():
        copy_to(0).start()

    lax.fori_loop(1, 64, start, 0)

    @pl.when(pipe == 0)
    def _():
        copy_to(0).wait_send()
        out_ref[...] = jnp.zeros_like(out_ref)

    lax.fori_loop(1, 64, finish, 0)

    @pl.when(pipe == 1)
    def _():
        landed[own] = block_ref[...]

        def arrive(step, carry):
            source = lax.rem(own + step, 128)
            pltpu.make_async_remote_copy(
                src_ref=block_ref,
                dst_ref=landed.at[source],
                send_sem=send_sems.at[0],
                recv_sem=recv_sems.at[source],
                device_id=(1, lax.rem(dp + 1, 64)),
                device_id_type=MESH,
            ).wait_recv()
            return carry

        lax.fori_loop(1, 128, arrive, 0)
        out_ref[...] = landed[...]


def gather_blocks(block):
    return pl.pallas_call(
        gather_kernel,
        out_shape=jax.ShapeDtypeStruct((128, 8, 128), jnp.float32),
        in_specs=[pl.BlockSpec(memory_space=pltpu.VMEM)],
        out_specs=pl.BlockSpec(memory_space=pltpu.VMEM),
        scratch_shapes=[
            pltpu.VMEM((128, 8, 128), jnp.float32),
            pltpu.SemaphoreType.DMA((64,)),
            pltpu.SemaphoreType.DMA((128,)),
        ],
        compiler_params=pltpu.CompilerParams(has_side_effects=True),
    )(block)


def chip_after(chip, step):
    x = lax.rem(lax.rem(chip, 4) + lax.rem(step, 4), 4)
    z = lax.rem(lax.rem(chip // 4, 2) + lax.rem(step // 4, 2), 2)
    y = lax.rem(chip // 8 + step // 8, 4)
    return (y * 2 + z) * 4 + x


def scatter_kernel(
    blocks, out_ref, few_ref, mine, other, landed, share, taken,
    local_sems, near_send, near_recv, far_send, far_recv, share_send, share_recv,
):
    pipe = lax.axis_index("pipe")
    dp = lax.axis_index("dp")
    core = lax.rem(dp, 2)
    chip = dp // 2
    partner = dp + 1 - 2 * core

    def near(step):
        target = chip_after(chip, step)
        return pltpu.make_async_remote_copy(
            src_ref=blocks.at[target * 2 + 1 - core],
            dst_ref=other.at[target],
            send_sem=near_send.at[step],
            recv_sem=near_recv.at[step],
            device_id=(pipe, partner),
            device_id_type=MESH,
        )

    def local(step):
        target = chip_after(chip, step)
        return pltpu.make_async_copy(blocks.at[target * 2 + core], mine.at[target], local_sems.at[step])

    def far(step):
        target = chip_after(chip, step)
        return pltpu.make_async_remote_copy(
            src_ref=mine.at[target],
            dst_ref=landed.at[step],
            send_sem=far_send.at[step],
            recv_sem=far_recv.at[step],
            device_id=(pipe, target * 2 + core),
            device_id_type=MESH,
        )

    def begin(step, carry):
        at = lax.rem(step + 1, 32)
        near(at).start()
        local(at).start()
        return carry

    lax.fori_loop(0, 32, begin, 0)

    def pair(step, carry):
        target = chip_after(chip, step)
        local(step).wait()
        near(step).wait_recv()
        mine[target] = (mine[target].astype(jnp.float32) + other[target].astype(jnp.float32)).astype(jnp.bfloat16)
        far(step).start()
        return carry

    lax.fori_loop(1, 32, pair, 0)
    local(0).wait()
    near(0).wait_recv()
    out_ref[...] = mine[chip].astype(jnp.float32) + other[chip].astype(jnp.float32)

    def total(step, carry):
        far(step).wait_recv()
        out_ref[...] += landed[step].astype(jnp.float32)
        return carry

    lax.fori_loop(1, 32, total, 0)
    share[...] = out_ref[:, 3072:]
    across = pltpu.make_async_remote_copy(
        src_ref=share,
        dst_ref=taken,
        send_sem=share_send,
        recv_sem=share_recv,
        device_id=(1 - pipe, dp),
        device_id_type=MESH,
    )

    @pl.when(pipe == 1)
    def _():
        across.start()
        few_ref[...] = share[...]
        across.wait_send()

    def finish(step, carry):
        near(step).wait_send()
        return carry

    lax.fori_loop(0, 32, finish, 0)

    def finish_far(step, carry):
        far(step).wait_send()
        return carry

    lax.fori_loop(1, 32, finish_far, 0)

    @pl.when(pipe == 0)
    def _():
        across.wait_recv()
        few_ref[...] = taken[...]


def scatter_blocks(blocks):
    shape = (32, 16, WIDE)
    return pl.pallas_call(
        scatter_kernel,
        out_shape=[
            jax.ShapeDtypeStruct((16, WIDE), jnp.float32),
            jax.ShapeDtypeStruct((16, 128), jnp.float32),
        ],
        in_specs=[pl.BlockSpec(memory_space=pl.ANY)],
        out_specs=[pl.BlockSpec(memory_space=pltpu.VMEM)] * 2,
        scratch_shapes=[
            pltpu.VMEM(shape, jnp.bfloat16),
            pltpu.VMEM(shape, jnp.bfloat16),
            pltpu.VMEM(shape, jnp.bfloat16),
            pltpu.VMEM((16, 128), jnp.float32),
            pltpu.VMEM((16, 128), jnp.float32),
            pltpu.SemaphoreType.DMA((32,)),
            pltpu.SemaphoreType.DMA((32,)),
            pltpu.SemaphoreType.DMA((32,)),
            pltpu.SemaphoreType.DMA((32,)),
            pltpu.SemaphoreType.DMA((32,)),
            pltpu.SemaphoreType.DMA,
            pltpu.SemaphoreType.DMA,
        ],
        compiler_params=pltpu.CompilerParams(has_side_effects=True, vmem_limit_bytes=60 << 20),
    )(blocks)


BF = jnp.bfloat16
F32 = jnp.float32
SCALE = HEAD_DIM**-0.5
PAD = 1152
NN = (((1,), (0,)), ((), ()))
NT = (((1,), (1,)), ((), ()))
TN = (((0,), (0,)), ((), ()))
SPAN = 272
SPANS = SEQ // SPAN
WIDTH = 384
WIDTHS = PAD // WIDTH
COLUMNS = PAD // 128
ANY = pl.BlockSpec(memory_space=pl.ANY)
INSIDE = pl.BlockSpec(memory_space=pltpu.VMEM)
SCALARS = pl.BlockSpec(memory_space=pltpu.SMEM)


def dot(left, right, dims=NN):
    return lax.dot_general(left, right, dims, preferred_element_type=F32)


def normal(value):
    center = jnp.mean(value, axis=-1, keepdims=True)
    centred = value - center
    spread = jnp.mean(centred * centred, axis=-1, keepdims=True)
    rate = lax.rsqrt(spread + EPSILON)
    return centred * rate, rate


def normal_back(value, gain, d_normed):
    hat, rate = normal(value)
    scaled = d_normed * gain
    first = jnp.mean(scaled, axis=-1, keepdims=True)
    second = jnp.mean(scaled * hat, axis=-1, keepdims=True)
    terms = d_normed * hat
    return rate * (scaled - first - hat * second), fold_rows(terms), hat


def fold_rows(terms):
    return jnp.sum(terms.reshape(-1, 8, D), axis=0)


def gelu_pair(value):
    square = value * value
    inner = value * (0.7978845608028654 + 0.035677408136300125 * square)
    half = 0.5 + 0.5 * jnp.tanh(inner)
    out = value * half
    slope = half + out * (1.0 - half) * (1.5957691216057308 + 0.21406444881780075 * square)
    return out.astype(BF), slope.astype(BF)


def feed_forward(middle, gain, up, down, act_ref, slope_ref, rows):
    normed = (normal(middle)[0] * gain).astype(BF)
    total = middle
    hidden = dot(normed, up[:, 0:512])
    for j in range(4):
        cols = slice(j * 512, (j + 1) * 512)
        after = dot(normed, up[:, cols.stop : cols.stop + 512]) if j < 3 else None
        act, slope = gelu_pair(hidden)
        act_ref[rows, cols] = act
        slope_ref[rows, cols] = slope
        total = total + dot(act, down[cols, :])
        hidden = after
    return normed, total


def lane_is_low(shape):
    return lax.rem(lax.broadcasted_iota(jnp.int32, shape, len(shape) - 1), 128) < 64


def head_mask(shape):
    lane = lax.broadcasted_iota(jnp.int32, shape, 1)
    return [(lane >= 64 * h) & (lane < 64 * h + 64) for h in range(4)]


def spread_heads(value, masks):
    zero = jnp.zeros_like(value)
    return jnp.concatenate([jnp.where(m, value, zero) for m in masks], axis=0)


def fold_heads(value, masks):
    total = jnp.where(masks[0], value[:64], 0.0)
    for h in range(1, 4):
        total = total + jnp.where(masks[h], value[64 * h : 64 * h + 64], 0.0)
    return total


def head_blocks():
    row = lax.broadcasted_iota(jnp.int32, (256, 256), 0)
    lane = lax.broadcasted_iota(jnp.int32, (256, 256), 1)
    return (lax.div(row, 64) == lax.div(lane, 64)).astype(BF)


def frame_groups():
    for f in range(FRAMES):
        for g in range(2):
            yield slice(f * 64, f * 64 + 64), g * 256


SLAB = 136


def window_forward(mixed, scores, probs, context):
    masks = head_mask((64, 256))
    for rows, at in frame_groups():
        keys = spread_heads(mixed[rows, 512 + at : 768 + at], masks)
        scores[rows, at : at + 256] = dot(mixed[rows, at : at + 256], keys, NT)
    low = lane_is_low((SLAB, 128))

    def soften(i):
        rows = row_span(i, SLAB)
        for c in range(4):
            cols = slice(c * 128, c * 128 + 128)
            piece = scores[rows, cols]
            left = jnp.max(jnp.where(low, piece, -jnp.inf), axis=1, keepdims=True)
            right = jnp.max(jnp.where(low, -jnp.inf, piece), axis=1, keepdims=True)
            scores[rows, cols] = jnp.exp((piece - jnp.where(low, left, right)) * SCALE)

    loop(SEQ // SLAB, soften)
    ones = head_blocks()
    for rows, at in frame_groups():
        cols = slice(at, at + 256)
        power = scores[rows, cols].astype(BF)
        inverse = 1.0 / dot(power, ones)
        values = spread_heads(mixed[rows, 1024 + at : 1280 + at], masks)
        context[rows, cols] = (dot(power, values) * inverse).astype(BF)
        probs[rows, cols] = (power.astype(F32) * inverse).astype(BF)


def window_backward(mixed, probs, d_context, d_probs, d_scores, d_mixed):
    masks = head_mask((64, 256))
    for rows, at in frame_groups():
        cols = slice(at, at + 256)
        values = spread_heads(mixed[rows, 1024 + at : 1280 + at], masks)
        d_probs[rows, cols] = dot(d_context[rows, cols], values, NT)
    ones = head_blocks()

    def soften(i):
        rows = row_span(i, SPAN)
        for g in range(2):
            cols = slice(g * 256, g * 256 + 256)
            wide = probs[rows, cols].astype(F32)
            here = d_probs[rows, cols]
            delta = dot((wide * here).astype(BF), ones)
            d_scores[rows, cols] = (wide * (here - delta) * SCALE).astype(BF)

    loop(SPANS, soften)
    for rows, at in frame_groups():
        cols = slice(at, at + 256)
        here = d_scores[rows, cols]
        keys = spread_heads(mixed[rows, 512 + at : 768 + at], masks)
        d_mixed[rows, at : at + 256] = dot(here, keys).astype(BF)
        d_keys = fold_heads(dot(here, mixed[rows, at : at + 256], TN), masks)
        d_mixed[rows, 512 + at : 768 + at] = d_keys.astype(BF)
        d_values = fold_heads(dot(probs[rows, cols], d_context[rows, cols], TN), masks)
        d_mixed[rows, 1024 + at : 1280 + at] = d_values.astype(BF)


def loop(count, body):
    def step(index, carry):
        body(index)
        return carry

    lax.fori_loop(0, count, step, 0)


def row_span(index, size):
    return pl.ds(pl.multiple_of(index * size, 16), size)


def valid_rows(start, size, count):
    row = lax.broadcasted_iota(jnp.int32, (size, 1), 0) + start
    return row < count * PATCHES


def first_forward_kernel(micro, *refs):
    (active, frames, video, w_attn, w_up, w_down, gains) = refs[:7]
    (acts, sent, s_mixed, s_context, s_probs, s_middle, s_act, s_slope) = refs[-21:-13]
    (x, attn, up, down, mixed, context, probs, middle, act, slope, out, masked, sems) = refs[-13:]

    @pl.when(active[0] == 1)
    def _():
        count = frames[micro, 0]
        loads = [
            pltpu.make_async_copy(video.at[micro, 0], x, sems.at[0]),
            pltpu.make_async_copy(w_attn, attn, sems.at[1]),
            pltpu.make_async_copy(w_up, up, sems.at[2]),
            pltpu.make_async_copy(w_down, down, sems.at[3]),
        ]
        for copy in loads:
            copy.start()
        loads[0].wait()
        loads[1].wait()

        def project(i):
            rows = row_span(i, SPAN)
            hat, _ = normal(x[rows, :].astype(F32))
            normed = (hat * gains[0:1, :]).astype(BF)
            for j in range(3):
                cols = slice(j * 512, (j + 1) * 512)
                mixed[rows, cols] = dot(normed, attn[:, cols]).astype(BF)

        loop(SPANS, project)
        stores = [pltpu.make_async_copy(mixed, s_mixed, sems.at[4])]
        stores[0].start()
        window_forward(mixed, middle, probs, context)
        for k, (source, target) in enumerate(((context, s_context), (probs, s_probs))):
            stores.append(pltpu.make_async_copy(source, target, sems.at[5 + k]))
            stores[-1].start()
        loads[2].wait()
        loads[3].wait()
        for i in range(SPANS):
            rows = slice(i * SPAN, (i + 1) * SPAN)
            here = x[rows, :].astype(F32) + dot(context[rows, :], attn[:, 1536:])
            middle[rows, :] = here
            _, total = feed_forward(here, gains[1:2, :], up, down, act, slope, rows)
            out[rows, :] = total.astype(BF)
            masked[rows, :] = jnp.where(valid_rows(i * SPAN, SPAN, count), total, 0.0).astype(BF)
            part = pl.ds(i * SPAN, SPAN)
            late = ((out, sent), (masked, acts.at[micro]), (middle, s_middle), (act, s_act), (slope, s_slope))
            for k, (source, target) in enumerate(late):
                stores.append(pltpu.make_async_copy(source.at[part], target.at[part], sems.at[7 + 5 * i + k]))
                stores[-1].start()
        for copy in stores:
            copy.wait()


def saved_shapes():
    return [
        jax.ShapeDtypeStruct((SEQ, 3 * D), BF),
        jax.ShapeDtypeStruct((SEQ, D), BF),
        jax.ShapeDtypeStruct((SEQ, D), BF),
        jax.ShapeDtypeStruct((SEQ, D), F32),
        jax.ShapeDtypeStruct((SEQ, FF), BF),
        jax.ShapeDtypeStruct((SEQ, FF), BF),
    ]


def weight_scratch():
    return [pltpu.VMEM((D, 4 * D), BF), pltpu.VMEM((D, FF), BF), pltpu.VMEM((FF, D), BF)]


def first_forward(micro, active, frames, video, weights, acts=None):
    saved = saved_shapes()
    inputs = [active, frames, video, *weights] + ([] if acts is None else [acts])
    result = pl.pallas_call(
        functools.partial(first_forward_kernel, micro),
        out_shape=[jax.ShapeDtypeStruct((2, SEQ, D), BF), jax.ShapeDtypeStruct((SEQ, D), BF)] + saved,
        in_specs=([SCALARS, SCALARS, ANY, ANY, ANY, ANY, INSIDE, ANY])[: len(inputs)],
        out_specs=[ANY] * 8,
        input_output_aliases={} if acts is None else {7: 0},
        scratch_shapes=[pltpu.VMEM((SEQ, D), BF)] + weight_scratch()
        + [pltpu.VMEM(s.shape, s.dtype) for s in saved]
        + [pltpu.VMEM((SEQ, D), BF), pltpu.VMEM((SEQ, D), BF), pltpu.SemaphoreType.DMA((27,))],
        compiler_params=pltpu.CompilerParams(vmem_limit_bytes=60 << 20),
        name=f"first_forward_{micro}",
    )(*inputs)
    return result[0], result[1], result[2:]


def put_wide(blocks, old, at, left, right):
    lanes = slice(at, at + 512)
    value = jnp.concatenate([left.reshape(64, 8, 512), right.reshape(64, 8, 512)], axis=1)
    if old is not None:
        value = value + old[:, :, lanes].astype(F32)
    blocks[:, :, lanes] = value.astype(BF)


def put_tall(blocks, old, part, value):
    value = value.reshape(16, 2, 16, 512)
    into = slice(part * 16, part * 16 + 16)
    for half in range(2):
        lanes = slice(2048 + half * 512, 2560 + half * 512)
        piece = value[:, half]
        if old is not None:
            piece = piece + old[into, :, lanes].astype(F32)
        blocks[into, :, lanes] = piece.astype(BF)


def send_lanes(source, target, at, size, sem):
    lanes = pl.ds(at, size)
    copy = pltpu.make_async_copy(source.at[:, :, lanes], target.at[:, :, lanes], sem)
    copy.start()
    return copy


def spread_gains(sums, few):
    dst = lax.broadcasted_iota(jnp.int32, (64, D), 0)
    lane = lax.broadcasted_iota(jnp.int32, (64, D), 1)
    source = lax.broadcasted_iota(jnp.int32, (D, 128), 0)
    place = lax.broadcasted_iota(jnp.int32, (D, 128), 1)
    total = jnp.zeros((64, 128), F32)
    for k in range(2):
        row = jnp.sum(sums[8 * k : 8 * k + 8, :], axis=0, keepdims=True)
        mine = jnp.where(lane // 8 == dst, row, 0.0)
        pick = (lax.rem(source, 8) + 8 * k == place).astype(F32)
        total = total + lax.dot_general(mine, pick, NN, precision=lax.Precision.HIGHEST, preferred_element_type=F32)
    few[:, 8, :] = total


def first_backward_kernel(micro, fresh, *refs):
    (active, video, w_attn, w_up, w_down, gains, d_in, s_mixed, s_context, s_probs, s_middle, s_act, s_slope) = refs[:13]
    if fresh:
        _, grad_in, blocks, new_gains = refs[13:17]
    else:
        _, _, old_blocks, old_gains, grad_in, blocks = refs[13:19]
    (x, attn, up, down, mixed, context, probs, middle, act, slope, d_two, normed, d_branch, d_mid, d_context,
     g_out, g_gains, more_gains, few, block_out, block_old, sems) = refs[-22:]
    old = None if fresh else block_old

    @pl.when(active[0] == 1)
    def _():
        pairs = [
            (d_in, d_two), (w_down, down), (s_slope, slope), (w_up, up), (s_middle, middle), (s_act, act),
            (w_attn, attn), (s_context, context), (s_probs, probs), (s_mixed, mixed), (video.at[micro, 0], x),
        ]
        if not fresh:
            pairs[6:6] = [(old_blocks, block_old), (old_gains, more_gains)]
        loads = [pltpu.make_async_copy(s, t, sems.at[k]) for k, (s, t) in enumerate(pairs)]
        for copy in loads:
            copy.start()
        g_gains[...] = jnp.zeros_like(g_gains)
        for k in range(5):
            loads[k].wait()
        gain = gains[1:2, :]

        def tail(i):
            rows = row_span(i, SPAN)
            d_low = d_two[rows, :]
            total = jnp.zeros((SPAN, D), F32)
            d_act = dot(d_low, down[0:512, :], NT)
            for j in range(4):
                cols = slice(j * 512, (j + 1) * 512)
                after = dot(d_low, down[cols.stop : cols.stop + 512, :], NT) if j < 3 else None
                d_hidden = (d_act * slope[rows, cols].astype(F32)).astype(BF)
                slope[rows, cols] = d_hidden
                total = total + dot(d_hidden, up[:, cols], NT)
                d_act = after
            here = middle[rows, :]
            d_here, g_rows, hat = normal_back(here, gain, total)
            g_gains[8:16, :] += g_rows
            normed[rows, :] = (hat * gain).astype(BF)
            d_here = d_low.astype(F32) + d_here
            d_mid[rows, :] = d_here
            d_branch[rows, :] = d_here.astype(BF)

        loop(SPANS, tail)
        for copy in loads[5 : 7 if fresh else 9]:
            copy.wait()
        for j in range(4):
            cols = slice(j * 512, (j + 1) * 512)
            put_tall(block_out, old, j, dot(act[:, cols], d_two[...], TN))
        stores = [send_lanes(block_out, blocks, 2048, 1024, sems.at[13])]
        for j in range(2):
            left, right = slope[:, j * 512 : j * 512 + 512], slope[:, 1024 + j * 512 : 1536 + j * 512]
            put_wide(block_out, old, 1024 + j * 512, dot(normed[...], left, TN), dot(normed[...], right, TN))
        stores.append(send_lanes(block_out, blocks, 1024, 1024, sems.at[14]))
        for copy in loads[7 if fresh else 9 :]:
            copy.wait()
        g_out[...] = dot(context[...], d_branch[...], TN)

        def into_context(i):
            rows = row_span(i, SPAN)
            d_context[rows, :] = dot(d_branch[rows, :], attn[:, 1536:], NT).astype(BF)

        loop(SPANS, into_context)
        d_mixed = act
        window_backward(mixed, probs, d_context, middle, normed, d_mixed)
        gain_one = gains[0:1, :]

        def head(i):
            rows = row_span(i, SPAN)
            total = jnp.zeros((SPAN, D), F32)
            for j in range(3):
                cols = slice(j * 512, (j + 1) * 512)
                total = total + dot(d_mixed[rows, cols], attn[:, cols], NT)
            d_here, g_rows, hat = normal_back(x[rows, :].astype(F32), gain_one, total)
            g_gains[0:8, :] += g_rows
            normed[rows, :] = (hat * gain_one).astype(BF)
            d_branch[rows, :] = (d_mid[rows, :] + d_here).astype(BF)

        loop(SPANS, head)
        stores.append(pltpu.make_async_copy(d_branch, grad_in.at[micro], sems.at[15]))
        stores[-1].start()
        if fresh:
            stores.append(pltpu.make_async_copy(g_gains, new_gains, sems.at[16]))
            stores[-1].start()
        else:
            few[...] = jnp.zeros_like(few)
            spread_gains(g_gains[...] + more_gains[...], few)
            block_out[:, :, 3072:] = few[...].astype(BF)
        put_wide(
            block_out, old, 0, dot(normed[...], d_mixed[:, :512], TN), dot(normed[...], d_mixed[:, 1024:1536], TN)
        )
        put_wide(block_out, old, 512, dot(normed[...], d_mixed[:, 512:1024], TN), g_out[...])
        stores.append(send_lanes(block_out, blocks, 0, 1024, sems.at[17]))
        if not fresh:
            stores.append(send_lanes(block_out, blocks, 3072, 128, sems.at[16]))
        for copy in stores:
            copy.wait()


BLOCKS = jax.ShapeDtypeStruct((64, 16, WIDE), BF)
GAINS = jax.ShapeDtypeStruct((16, D), F32)


def first_backward(micro, active, video, weights, d_in, saved, grad_in, blocks=None, before=None):
    kept = saved_shapes()
    rows = pltpu.VMEM((SEQ, D), BF)
    fresh = before is None
    inputs = [active, video, *weights, d_in, *saved, grad_in]
    outputs = [jax.ShapeDtypeStruct(grad_in.shape, BF), BLOCKS]
    aliases = {13: 0}
    if fresh:
        outputs += [GAINS]
    else:
        inputs += [blocks, *before]
        aliases = {13: 0, 14: 1}
    sums = pltpu.VMEM((16, D), F32)
    result = pl.pallas_call(
        functools.partial(first_backward_kernel, micro, fresh),
        out_shape=outputs,
        in_specs=[SCALARS, ANY, ANY, ANY, ANY, INSIDE] + [ANY] * (len(inputs) - 6),
        out_specs=[ANY] * len(outputs),
        input_output_aliases=aliases,
        scratch_shapes=[rows] + weight_scratch() + [pltpu.VMEM(s.shape, s.dtype) for s in kept]
        + [rows, rows, rows, pltpu.VMEM((SEQ, D), F32), rows, pltpu.VMEM((D, D), F32), sums, sums]
        + [pltpu.VMEM((64, 16, 128), F32), pltpu.VMEM((64, 16, WIDE), BF), pltpu.VMEM((64, 16, WIDE), BF)]
        + [pltpu.SemaphoreType.DMA((18,))],
        compiler_params=pltpu.CompilerParams(vmem_limit_bytes=62 << 20),
        name=f"first_backward_{micro}",
    )(*inputs)
    return result[0], *result[1:]


def column(index):
    return slice(index * 128, index * 128 + 128)


def load_head(head, mixed, refs, scale):
    for part, (ref, turned) in enumerate(refs):
        rows = pl.ds(pl.multiple_of(part * D + head * HEAD_DIM, HEAD_DIM), HEAD_DIM)
        for c in range(COLUMNS):
            value = mixed[rows, column(c)].astype(F32)
            if part == 0 and scale:
                value = value * SCALE
            ref[:, column(c)] = value
            if turned is not None:
                turned[:, column(c)] = pltpu.roll(value, 64, 1)


def pair_rows(left, refs, a, rows_ref):
    for s, ref in enumerate(refs):
        for b in range(a + 1):
            rows_ref[9 * s + b : 9 * s + b + 1, :] = jnp.sum(left * ref[:, column(b)], axis=0, keepdims=True)


def weighted(rows_ref, refs, a):
    total = None
    for s, ref in enumerate(refs):
        for b in range(a + 1):
            term = rows_ref[9 * s + b : 9 * s + b + 1, :] * ref[:, column(b)]
            total = term if total is None else total + term
    return total


def temporal_head(head, order, mixed, probs, context, q, k, v, kt, vt, rows_ref):
    load_head(head, mixed, ((q, None), (k, kt), (v, vt)), True)
    out_rows = pl.ds(pl.multiple_of(head * HEAD_DIM, HEAD_DIM), HEAD_DIM)
    for a in range(COLUMNS):
        pair_rows(q[:, column(a)], (k, kt), a, rows_ref)
        scores = jnp.where(order[...] <= 2 * a, rows_ref[...], MASKED)
        power = jnp.exp(scores - jnp.max(scores, axis=0, keepdims=True))
        probs[head, a] = power / jnp.sum(power, axis=0, keepdims=True)
        context[out_rows, column(a)] = weighted(probs.at[head, a], (v, vt), a).astype(BF)


def temporal_head_back(head, mixed, probs, d_context, q, k, v, kt, vt, dc, rows_ref, ds):
    load_head(head, mixed, ((q, None), (k, kt), (v, vt)), False)
    in_rows = pl.ds(pl.multiple_of(head * HEAD_DIM, HEAD_DIM), HEAD_DIM)
    for c in range(COLUMNS):
        dc[:, column(c)] = d_context[in_rows, column(c)].astype(F32)
    for a in range(COLUMNS):
        pair_rows(dc[:, column(a)], (v, vt), a, rows_ref)
        p = probs[head, a]
        d_probs = jnp.where(p > 0.0, rows_ref[...], 0.0)
        delta = jnp.sum(d_probs * p, axis=0, keepdims=True)
        ds[a] = p * (d_probs - delta) * SCALE
        mixed[in_rows, column(a)] = weighted(ds.at[a], (k, kt), a).astype(BF)
    for part, (weight, source) in enumerate(((lambda a, r: ds[a, r : r + 1, :], q), (lambda a, r: probs[head, a, r : r + 1, :], dc))):
        rows = pl.ds(pl.multiple_of((part + 1) * D + head * HEAD_DIM, HEAD_DIM), HEAD_DIM)
        for b in range(COLUMNS):
            sums = []
            for s in range(2):
                total = None
                for a in range(b, COLUMNS):
                    term = weight(a, 9 * s + b) * source[:, column(a)]
                    total = term if total is None else total + term
                sums.append(total)
            mixed[rows, column(b)] = (sums[0] + pltpu.roll(sums[1], 64, 1)).astype(BF)


def frame_order(count):
    row = lax.broadcasted_iota(jnp.int32, (24, 128), 0)
    high = (lax.broadcasted_iota(jnp.int32, (24, 128), 1) >= 64).astype(jnp.int32)
    turned = row >= 9
    base = 2 * jnp.where(turned, row - 9, row)
    key_frame = base + jnp.where(turned, 1 - high, high)
    return jnp.where((row < 18) & (key_frame < count), key_frame - high, 1000)


def second_kernel(micro, fresh, *refs):
    (active, frames, received, w_attn, w_turned, w_up, w_down, gains, cot_h, cot_q, codes, quant) = refs[:12]
    if fresh:
        _, acts, grad_in, sent_back = refs[12:16]
        old = []
    else:
        _, _, *old = refs[12:17]
        acts, grad_in, sent_back = refs[17:20]
    (s_act, s_hidden, s_normed, s_two, s_d_two, s_branch, s_context, s_mixed, new_gains, new_proj, new_code) = refs[-48:-37]
    (x, attn_out, turned, up, down, normed, normed_two, mixed, context, d_context, probs, middle, act, slope, out,
     masked, d_mid, d_two, cot, cot_codes, code_rows, table, proj_wide, proj, g_gains, g_proj, g_code,
     q, k, v, kt, vt, dc, rows_ref, ds, order, sems) = refs[-37:]

    @pl.when(active[0] == 1)
    def _():
        count = frames[micro, 0]
        real = pl.ds(0, SEQ)
        pairs = [
            (received, x.at[real]), (w_turned, turned), (w_attn.at[:, pl.ds(1536, 512)], attn_out), (w_up, up),
            (w_down, down), (codes.at[micro], code_rows.at[real]), (cot_q.at[micro], cot_codes.at[real]),
            (cot_h.at[micro, 0], cot.at[real]),
        ]
        pairs += list(zip(old, (g_gains, g_proj, g_code)))
        loads = [pltpu.make_async_copy(s, t, sems.at[i]) for i, (s, t) in enumerate(pairs)]
        for copy in loads:
            copy.start()
        stores = []

        def save(source, target):
            stores.append(pltpu.make_async_copy(source, target, sems.at[11 + len(stores)]))
            stores[-1].start()

        tail_rows = pl.ds(SEQ, PAD - SEQ)
        x[tail_rows, :] = jnp.zeros((PAD - SEQ, D), BF)
        cot[tail_rows, :] = jnp.zeros((PAD - SEQ, D), BF)
        cot_codes[tail_rows, :] = jnp.zeros((PAD - SEQ, 128), BF)
        code_rows[tail_rows, :] = jnp.zeros((PAD - SEQ, 128), jnp.int32)
        rows_ref[...] = jnp.zeros_like(rows_ref)
        order[...] = frame_order(count)
        if fresh:
            g_gains[...] = jnp.zeros_like(g_gains)
            g_proj[...] = jnp.zeros_like(g_proj)
            g_code[...] = jnp.zeros_like(g_code)
        for j in range(4):
            table[:, column(j)] = quant[:, j, :].astype(BF)
            proj_wide[pl.ds(j, 128, stride=4), :] = quant[:, 4 + j, :]
        proj[...] = proj_wide[...].astype(BF)
        gain_one, gain_two = gains[0:1, :], gains[1:2, :]
        loads[0].wait()
        loads[1].wait()
        for i in range(WIDTHS):
            rows = slice(i * WIDTH, (i + 1) * WIDTH)
            normed[rows, :] = (normal(x[rows, :].astype(F32))[0] * gain_one).astype(BF)
            for j in range(3):
                parts = slice(j * 512, (j + 1) * 512)
                mixed[parts, rows] = dot(turned[parts, :], normed[rows, :], NT).astype(BF)
        save(normed, s_normed)
        loop(HEADS, lambda h: temporal_head(h, order, mixed, probs, context, q, k, v, kt, vt, rows_ref))
        save(context, s_context)
        for copy in loads[2:]:
            copy.wait()
        for i in range(WIDTHS):
            rows = slice(i * WIDTH, (i + 1) * WIDTH)
            middle[rows, :] = x[rows, :].astype(F32) + dot(context[:, rows], attn_out[...], TN)

        def forward_tail(i):
            rows = row_span(i, WIDTH)
            here = middle[rows, :]
            normed_low, total = feed_forward(here, gain_two, up, down, act, slope, rows)
            normed_two[rows, :] = normed_low
            valid = valid_rows(i * WIDTH, WIDTH, count)
            low = total.astype(BF)
            out[rows, :] = low
            masked[rows, :] = jnp.where(valid, total, 0.0).astype(BF)
            mask = valid.astype(F32)
            latent = dot(low, proj[...])
            code = code_rows[rows, :]
            lane = lax.broadcasted_iota(jnp.int32, (WIDTH, 128), 1)
            high = (lax.div(code, LOW_CODES) == lane).astype(BF)
            near = dot(high, table[...])
            spot = lax.rem(code, LOW_CODES) == lax.rem(lane, LOW_CODES)
            spots = jnp.concatenate([spot] * 4, axis=1)
            place = lax.div(lax.broadcasted_iota(jnp.int32, (512, 128), 0), LOW_CODES)
            pick = (place == lax.broadcasted_iota(jnp.int32, (512, 128), 1)).astype(BF)
            chosen = dot(jnp.where(spots, near, 0.0).astype(BF), pick)
            d_latent = (mask * (cot_codes[rows, :].astype(F32) + 2.0 * BETA * (latent - chosen))).astype(BF)
            d_chosen = (2.0 * mask * (chosen - latent)).astype(BF)
            g_proj[...] += dot(low, d_latent, TN)
            spread = jnp.where(spots, dot(d_chosen, pick, NT), 0.0).astype(BF)
            g_code[...] += dot(high, spread, TN)
            d_out = cot[rows, :].astype(F32) * mask + dot(d_latent, proj[...], NT)
            d_two[rows, :] = d_out.astype(BF)
            d_mid[rows, :] = d_out

        loop(WIDTHS, forward_tail)
        save(masked.at[real], acts.at[micro])
        save(act, s_act)
        save(normed_two, s_two)
        save(d_two, s_d_two)
        save(g_proj, new_proj)
        save(g_code, new_code)
        d_branch = out

        def backward_tail(i):
            rows = row_span(i, WIDTH)
            d_low = d_two[rows, :]
            total = jnp.zeros((WIDTH, D), F32)
            d_act = dot(d_low, down[0:512, :], NT)
            for j in range(4):
                cols = slice(j * 512, (j + 1) * 512)
                after = dot(d_low, down[cols.stop : cols.stop + 512, :], NT) if j < 3 else None
                d_hidden = (d_act * slope[rows, cols].astype(F32)).astype(BF)
                slope[rows, cols] = d_hidden
                total = total + dot(d_hidden, up[:, cols], NT)
                d_act = after
            d_here, g_rows, _ = normal_back(middle[rows, :], gain_two, total)
            g_gains[8:16, :] += g_rows
            d_here = d_mid[rows, :] + d_here
            d_mid[rows, :] = d_here
            d_branch[rows, :] = d_here.astype(BF)

        loop(WIDTHS, backward_tail)
        save(slope, s_hidden)
        save(d_branch, s_branch)
        for i in range(WIDTHS):
            rows = slice(i * WIDTH, (i + 1) * WIDTH)
            d_context[:, rows] = dot(attn_out[...], d_branch[rows, :], NT).astype(BF)
        loop(
            HEADS,
            lambda h: temporal_head_back(h, mixed, probs, d_context, q, k, v, kt, vt, dc, rows_ref, ds),
        )
        save(mixed, s_mixed)
        d_x = cot
        for i in range(WIDTHS):
            rows = slice(i * WIDTH, (i + 1) * WIDTH)
            total = dot(mixed[:, rows], turned[...], TN)
            d_here, g_rows, _ = normal_back(x[rows, :].astype(F32), gain_one, total)
            g_gains[0:8, :] += g_rows
            d_x[rows, :] = (d_mid[rows, :] + d_here).astype(BF)
        save(d_x.at[real], sent_back)
        save(d_x.at[real], grad_in.at[micro])
        save(g_gains, new_gains)
        for copy in stores:
            copy.wait()


TOKENS = jax.ShapeDtypeStruct((PAD, D), BF)
HIDDEN = jax.ShapeDtypeStruct((PAD, FF), BF)
KEPT = [
    HIDDEN, HIDDEN, TOKENS, TOKENS, TOKENS, TOKENS,
    jax.ShapeDtypeStruct((D, PAD), BF), jax.ShapeDtypeStruct((3 * D, PAD), BF),
]
SMALL = [
    GAINS,
    jax.ShapeDtypeStruct((D, 128), F32),
    jax.ShapeDtypeStruct((128, 512), F32),
]


def second_section(micro, active, frames, received, weights, cots, acts, grad_in=None, small=None):
    fresh = small is None
    inputs = [active, frames, received, *weights, *cots, acts]
    outputs = [
        jax.ShapeDtypeStruct(acts.shape, BF),
        jax.ShapeDtypeStruct(acts.shape, BF),
        jax.ShapeDtypeStruct((SEQ, D), BF),
    ] + KEPT + SMALL
    aliases = {12: 0}
    if not fresh:
        inputs += [grad_in, *small]
        aliases = {12: 0, 13: 1}
    tokens = pltpu.VMEM((PAD, D), BF)
    tokens_wide = pltpu.VMEM((PAD, D), F32)
    flipped = pltpu.VMEM((D, PAD), BF)
    hidden = pltpu.VMEM((PAD, FF), BF)
    one_head = pltpu.VMEM((HEAD_DIM, PAD), F32)
    scratch = [
        tokens, pltpu.VMEM((D, D), BF), pltpu.VMEM((3 * D, D), BF), pltpu.VMEM((D, FF), BF), pltpu.VMEM((FF, D), BF),
        tokens, tokens, pltpu.VMEM((3 * D, PAD), BF), flipped, flipped, pltpu.VMEM((HEADS, COLUMNS, 24, 128), F32),
        tokens_wide, hidden, hidden, tokens, tokens, tokens_wide, tokens, tokens, pltpu.VMEM((PAD, 128), BF),
        pltpu.VMEM((PAD, 128), jnp.int32), pltpu.VMEM((128, 512), BF), pltpu.VMEM((D, 128), F32),
        pltpu.VMEM((D, 128), BF),
    ]
    scratch += [pltpu.VMEM(s.shape, s.dtype) for s in SMALL] + [one_head] * 6 + [
        pltpu.VMEM((24, 128), F32), pltpu.VMEM((COLUMNS, 24, 128), F32), pltpu.VMEM((24, 128), jnp.int32),
        pltpu.SemaphoreType.DMA((28,)),
    ]
    specs = [SCALARS, SCALARS, ANY, ANY, ANY, ANY, ANY, INSIDE, ANY, ANY, ANY, INSIDE]
    result = pl.pallas_call(
        functools.partial(second_kernel, micro, fresh),
        out_shape=outputs,
        in_specs=specs + [ANY] * (len(inputs) - 12),
        out_specs=[ANY] * len(outputs),
        input_output_aliases=aliases,
        scratch_shapes=scratch,
        compiler_params=pltpu.CompilerParams(vmem_limit_bytes=62 << 20),
        name=f"second_section_{micro}",
    )(*inputs)
    return result[0], result[1], result[2], result[3:11], result[11:]


def second_grads_kernel(active, *refs):
    kept = (refs[:8], refs[8:16])
    s_gains, s_proj, s_code, blocks = refs[16:20]
    (act, hidden, normed, normed_two, d_two, d_branch, context, mixed, g_gains, g_proj, g_code, few, block_out, sems) = refs[20:]
    held = (act, hidden, normed, normed_two, d_two, d_branch, context, mixed)

    @pl.when(active[0] == 1)
    def _():
        loads = {}
        for k in (0, 4, 1, 3, 6, 5, 7, 2):
            for m in range(2):
                at = pl.ds(m * PAD, PAD)
                into = held[k].at[:, at] if k >= 6 else held[k].at[at]
                loads[k, m] = pltpu.make_async_copy(kept[m][k], into, sems.at[2 * k + m])
                loads[k, m].start()
        tiny = [
            pltpu.make_async_copy(s, t, sems.at[16 + i])
            for i, (s, t) in enumerate(((s_gains, g_gains), (s_proj, g_proj), (s_code, g_code)))
        ]
        for copy in tiny:
            copy.start()

        def need(*keys):
            for k in keys:
                for m in range(2):
                    loads[k, m].wait()

        need(0, 4)
        for j in range(4):
            put_tall(block_out, None, j, dot(act[:, j * 512 : j * 512 + 512], d_two[...], TN))
        stores = [send_lanes(block_out, blocks, 2048, 1024, sems.at[19])]
        need(1, 3)
        for j in range(2):
            left, right = hidden[:, j * 512 : j * 512 + 512], hidden[:, 1024 + j * 512 : 1536 + j * 512]
            put_wide(
                block_out, None, 1024 + j * 512, dot(normed_two[...], left, TN), dot(normed_two[...], right, TN)
            )
        stores.append(send_lanes(block_out, blocks, 1024, 1024, sems.at[20]))
        need(6, 5, 7, 2)
        parts = [dot(mixed[j * 512 : j * 512 + 512, :], normed[...]).T for j in range(3)]
        put_wide(block_out, None, 0, parts[0], parts[2])
        put_wide(block_out, None, 512, parts[1], dot(context[...], d_branch[...]))
        stores.append(send_lanes(block_out, blocks, 0, 1024, sems.at[21]))
        for copy in tiny:
            copy.wait()
        few[...] = jnp.zeros_like(few)
        spread_gains(g_gains[...], few)
        for j in range(4):
            few[:, j, :] = g_code[0:64, column(j)]
            few[:, 4 + j, :] = g_code[64:128, column(j)]
        for j in range(4):
            first = g_proj[pl.ds(j, 64, stride=4), :]
            second = g_proj[pl.ds(256 + j, 64, stride=4), :]
            few[:, 9 + j, :] = first + pltpu.roll(second, 64, 1)
        block_out[:, :, 3072:] = few[...].astype(BF)
        stores.append(send_lanes(block_out, blocks, 3072, 128, sems.at[22]))
        for copy in stores:
            copy.wait()


def second_grads(active, kept_0, kept_1, small):
    twice = [
        pltpu.VMEM((s.shape[0], 2 * PAD) if s.shape[1] == PAD else (2 * PAD, s.shape[1]), BF) for s in KEPT
    ]
    return pl.pallas_call(
        second_grads_kernel,
        out_shape=BLOCKS,
        in_specs=[SCALARS] + [ANY] * 19,
        out_specs=ANY,
        scratch_shapes=twice + [pltpu.VMEM(s.shape, s.dtype) for s in SMALL]
        + [pltpu.VMEM((64, 16, 128), F32), pltpu.VMEM((64, 16, WIDE), BF), pltpu.SemaphoreType.DMA((23,))],
        compiler_params=pltpu.CompilerParams(vmem_limit_bytes=62 << 20),
        name="second_grads",
    )(active, *kept_0, *kept_1, *small)


def average(ema, weight, grad, rate):
    return rate * ema + (1.0 - rate) * (weight - LEARN_RATE * grad)


def average_kernel(first, rates, total, few, *refs):
    weights, emas, grads, news = refs[:6], refs[6:12], refs[12:18], refs[18:24]
    grads[0][0, :, :1024] = total[0:8, 0:1024]
    grads[0][0, :, 1024:] = total[8:16, 0:1024]
    grads[1][0, :, :1024] = total[0:8, 1024:2048]
    grads[1][0, :, 1024:] = total[8:16, 1024:2048]
    grads[2][0, 0:16, :] = total[:, 2048:2560]
    grads[2][0, 16:32, :] = total[:, 2560:3072]
    gain = total[8:9, 3072:3200]
    grads[3][0, 0:1, :] = gain[:, 0:8]
    grads[3][0, 1:2, :] = pltpu.roll(gain, 120, 1)[:, 0:8]
    is_first = first[0] == 1
    proj = few[9:13, :]
    grads[4][...] = jnp.where(is_first, proj, pltpu.roll(proj, 64, 1))[:, 0:8]
    code = jnp.where(is_first, few[0:4, :], few[4:8, :])
    turned = pltpu.roll(code, 64, 1)
    for r in range(4):
        grads[5][2 * r : 2 * r + 1, :] = code[r : r + 1, 0:64]
        grads[5][2 * r + 1 : 2 * r + 2, :] = turned[r : r + 1, 0:64]
    for i in range(6):
        rate = rates[0] if i < 4 else rates[1]
        news[i][...] = average(emas[i][...], weights[i][...].astype(F32), grads[i][...], rate)


def averages(first, rates, total, few, weights, emas):
    shapes = [jax.ShapeDtypeStruct(e.shape, F32) for e in emas]
    return pl.pallas_call(
        average_kernel,
        out_shape=shapes * 2,
        in_specs=[SCALARS, SCALARS] + [INSIDE] * 14,
        out_specs=[INSIDE] * 12,
        name="averages",
    )(first, rates, total, few, *weights, *emas)


def per_device(
    video, cot_h, cot_q, frames, codes, w_attn, w_up, w_down, gains, proj, codebook,
    ema_attn, ema_up, ema_down, ema_gains, ema_proj, ema_code, decay,
):
    segment = lax.axis_index("pipe")
    in_first = (segment == 0).astype(jnp.int32).reshape(1)
    in_second = 1 - in_first
    weights = (w_attn[0], w_up[0], w_down[0], gains[0])

    acts, sent_0, saved_0 = first_forward(0, in_first, frames, video, weights)
    received_0 = lax.ppermute(sent_0, "pipe", [(0, 1)])

    wide_attn, proj_own, code_own, cot_q, codes, _ = lax.optimization_barrier(
        (w_attn[0], proj, codebook, cot_q, codes, sent_0)
    )
    cot_rows = jnp.pad(jnp.swapaxes(cot_q[:, 0], 1, 2), ((0, 0), (0, 0), (0, 120)))
    code_rows = jnp.broadcast_to(codes[:, 0, :, None], (2, SEQ, 128))
    turned = wide_attn[:, : 3 * D].T
    block = jnp.concatenate([code_own.reshape(4, 128), jnp.pad(proj_own, ((0, 0), (0, 120)))], axis=0)
    block = block.astype(F32)
    quant = gather_blocks(block)

    second_weights = (w_attn[0], turned, w_up[0], w_down[0], gains[0])
    cots = (cot_h, cot_rows, code_rows, quant)
    video_1, _ = lax.optimization_barrier((video, quant))
    acts, sent_1, saved_1 = first_forward(1, in_first, frames, video_1, weights, acts)
    received_1 = lax.ppermute(sent_1, "pipe", [(0, 1)])

    acts, grad_in, back_0, kept_0, small = second_section(
        0, in_second, frames, received_0, second_weights, cots, acts
    )
    returned_0 = lax.ppermute(back_0, "pipe", [(1, 0)])
    acts, grad_in, back_1, kept_1, small = second_section(
        1, in_second, frames, received_1, second_weights, cots, acts, grad_in, small
    )
    returned_1 = lax.ppermute(back_1, "pipe", [(1, 0)])
    blocks = second_grads(in_second, kept_0, kept_1, small)

    returned_0, blocks = lax.optimization_barrier((returned_0, blocks))
    grad_in, *before = first_backward(0, in_first, video, weights, returned_0, saved_0, grad_in)

    lane = lax.axis_index("dp")
    parts = lax.axis_size("dp")
    w_attn_late, w_up_late, w_down_late, gains_late, decay, _ = lax.optimization_barrier(
        (w_attn, w_up, w_down, gains, decay, before[1])
    )

    def own_rows(weight, axis):
        size = weight.shape[axis] // parts
        return lax.dynamic_slice_in_dim(weight, lane * size, size, axis).astype(F32)

    own = (
        own_rows(w_attn_late, 1), own_rows(w_up_late, 1), own_rows(w_down_late, 1), own_rows(gains_late, 2), proj,
        codebook,
    )
    rates = jnp.stack([lax.dynamic_index_in_dim(decay, segment, 0, keepdims=False), decay[2]])
    returned_1, own, rates = lax.optimization_barrier((returned_1, own, rates))
    grad_in, blocks = first_backward(
        1, in_first, video, weights, returned_1, saved_1, grad_in, blocks, before
    )
    total, few = scatter_blocks(blocks)
    results = averages(
        in_first, rates, total, few, own, (ema_attn, ema_up, ema_down, ema_gains, ema_proj, ema_code)
    )
    return (acts[None, :, None], grad_in[None, :, None], *results)


def solution(mesh):
    placed = (
        P(None, "dp", None, None),
        P(None, "dp", None, None),
        P(None, "dp", None, None),
        P(None, "dp"),
        P(None, "dp", None),
        P("pipe", None, None),
        P("pipe", None, None),
        P("pipe", None, None),
        P("pipe", None, None),
        P(("pipe", "dp"), None),
        P(None, ("pipe", "dp")),
        P("pipe", "dp", None),
        P("pipe", "dp", None),
        P("pipe", "dp", None),
        P("pipe", None, "dp"),
        P(("pipe", "dp"), None),
        P(None, ("pipe", "dp")),
        P(),
    )
    return jax.shard_map(
        per_device,
        mesh=mesh,
        in_specs=placed,
        out_specs=(
            P("pipe", None, "dp", None, None),
            P("pipe", None, "dp", None, None),
            P("pipe", "dp", None),
            P("pipe", "dp", None),
            P("pipe", "dp", None),
            P("pipe", None, "dp"),
            P(("pipe", "dp"), None),
            P(None, ("pipe", "dp")),
            P("pipe", "dp", None),
            P("pipe", "dp", None),
            P("pipe", "dp", None),
            P("pipe", None, "dp"),
            P(("pipe", "dp"), None),
            P(None, ("pipe", "dp")),
        ),
        check_vma=False,
    )
```

```python
import functools

import jax
import jax.numpy as jnp
from jax import lax
from jax.experimental import pallas as pl
from jax.experimental.pallas import tpu as pltpu
from jax.sharding import PartitionSpec as P

D = 512
HEADS = 8
HEAD_DIM = 64
FF = 2048
CODES = 8192
CODE_DIM = 8
LOW_CODES = 64
PATCHES = 64
FRAMES = 17
SEQ = 1088


EPSILON = 1e-05
BETA = 0.25
LEARN_RATE = 0.0001
MASKED = -1e30
MESH = pl.DeviceIdType.MESH
WIDE = 3200
CUT = 1664
LEFT = pl.ds(0, CUT)
RIGHT = pl.ds(CUT, WIDE - CUT)


def gather_kernel(block_ref, out_ref, landed, send_sems, recv_sems):
    pipe = lax.axis_index("pipe")
    dp = lax.axis_index("dp")

    def copy_of(step):
        return pltpu.make_async_remote_copy(
            src_ref=block_ref,
            dst_ref=landed.at[step],
            send_sem=send_sems.at[step],
            recv_sem=recv_sems.at[step],
            device_id=(1, lax.rem(dp + step, 64)),
            device_id_type=MESH,
        )

    @pl.when(pipe == 1)
    def _():
        barrier = pltpu.get_barrier_semaphore()

        def greet(step, carry):
            pl.semaphore_signal(barrier, inc=1, device_id=(1, lax.rem(dp + step, 64)), device_id_type=MESH)
            return carry

        lax.fori_loop(1, 64, greet, 0)
        pl.semaphore_wait(barrier, 63)

        def start(step, carry):
            copy_of(step).start()
            return carry

        lax.fori_loop(1, 64, start, 0)
        for half in range(2):
            out_ref[half * 64 + dp] = block_ref[half]

        def arrive(step, carry):
            copy_of(step).wait_recv()
            source = lax.rem(dp + 64 - step, 64)
            for half in range(2):
                out_ref[half * 64 + source] = landed[step, half]
            return carry

        lax.fori_loop(1, 64, arrive, 0)

        def finish(step, carry):
            copy_of(step).wait_send()
            return carry

        lax.fori_loop(1, 64, finish, 0)


def gather_blocks(block):
    return pl.pallas_call(
        gather_kernel,
        out_shape=jax.ShapeDtypeStruct((128, 8, 128), jnp.float32),
        in_specs=[pl.BlockSpec(memory_space=pltpu.VMEM)],
        out_specs=pl.BlockSpec(memory_space=pltpu.VMEM),
        scratch_shapes=[
            pltpu.VMEM((64, 2, 8, 128), jnp.float32),
            pltpu.SemaphoreType.DMA((64,)),
            pltpu.SemaphoreType.DMA((64,)),
        ],
        compiler_params=pltpu.CompilerParams(collective_id=1, has_side_effects=True),
        name="gather_quantizer",
    )(block)


def scatter_kernel(
    blocks, out_ref, few_ref, mine, other, land_a, land_b, next_a, next_b, land_c, land_d, last_out, last_in, share, taken,
    local_sem, near_send, near_recv, one_send, one_recv, two_send, two_recv, last_send, last_recv, share_send, share_recv,
):
    pipe = lax.axis_index("pipe")
    dp = lax.axis_index("dp")
    core = lax.rem(dp, 2)
    x = lax.rem(dp // 2, 4)
    z = lax.rem(dp // 8, 2)
    y = dp // 16
    full = slice(None)

    def at(yy, zz, xx, cc):
        return (pipe, ((yy * 2 + zz) * 4 + xx) * 2 + cc)

    def x_after(step):
        return lax.rem(x + step, 4)

    def y_after(step):
        return lax.rem(y + step, 4)

    def remote(source, target, send, recv, device):
        return pltpu.make_async_remote_copy(
            src_ref=source, dst_ref=target, send_sem=send, recv_sem=recv, device_id=device, device_id_type=MESH
        )

    own = pltpu.make_async_copy(blocks.at[:, :, :, core], mine, local_sem)
    own.start()
    barrier = pltpu.get_barrier_semaphore()
    peers = [at(y, z, x, 1 - core), at(y, 1 - z, x, core), (1 - pipe, dp)]
    peers += [at(y, z, x_after(d), core) for d in (1, 2, 3)]
    peers += [at(y_after(d), z, x, core) for d in (1, 2, 3)]
    for peer in peers:
        pl.semaphore_signal(barrier, inc=1, device_id=peer, device_id_type=MESH)
    pl.semaphore_wait(barrier, 9)

    def near_a(d):
        t = x_after(d)
        return remote(
            blocks.at[:, :, t, 1 - core, :, LEFT], other.at[:, :, t, :, LEFT], near_send.at[2 * d], near_recv.at[2 * d],
            at(y, z, x, 1 - core),
        )

    def near_b(d):
        t = y_after(d)
        return remote(
            blocks.at[t, :, :, 1 - core, :, RIGHT], other.at[t, :, :, :, RIGHT], near_send.at[2 * d + 1],
            near_recv.at[2 * d + 1], at(y, z, x, 1 - core),
        )

    def one_a(d):
        return remote(
            mine.at[:, :, x_after(d), :, LEFT], land_a.at[d - 1], one_send.at[2 * d - 2], one_recv.at[2 * d - 2],
            at(y, z, x_after(d), core),
        )

    def one_b(d):
        return remote(
            mine.at[y_after(d), :, :, :, RIGHT], land_b.at[d - 1], one_send.at[2 * d - 1], one_recv.at[2 * d - 1],
            at(y_after(d), z, x, core),
        )

    def two_a(d):
        return remote(
            next_a.at[y_after(d)], land_c.at[d - 1], two_send.at[2 * d - 2], two_recv.at[2 * d - 2],
            at(y_after(d), z, x, core),
        )

    def two_b(d):
        return remote(
            next_b.at[x_after(d)], land_d.at[d - 1], two_send.at[2 * d - 1], two_recv.at[2 * d - 1],
            at(y, z, x_after(d), core),
        )

    order = (2, 1, 3, 0)
    for d in order:
        near_a(d).start()
        near_b(d).start()
    own.wait()

    def wide(ref, *index):
        return ref[index].astype(jnp.float32)

    for d in order[:3]:
        near_a(d).wait_recv()

        def pair_a(i, carry, t=x_after(d)):
            yy, zz = i // 2, lax.rem(i, 2)
            where = (yy, zz, t, full, LEFT)
            mine[where] = (wide(mine, *where) + wide(other, *where)).astype(jnp.bfloat16)
            return carry

        lax.fori_loop(0, 8, pair_a, 0)
        one_a(d).start()
        near_b(d).wait_recv()

        def pair_b(i, carry, t=y_after(d)):
            zz, xx = i // 4, lax.rem(i, 4)
            where = (t, zz, xx, full, RIGHT)
            mine[where] = (wide(mine, *where) + wide(other, *where)).astype(jnp.bfloat16)
            return carry

        lax.fori_loop(0, 8, pair_b, 0)
        one_b(d).start()
    near_a(0).wait_recv()
    near_b(0).wait_recv()
    for d in (1, 3, 2):
        one_a(d).wait_recv()
        one_b(d).wait_recv()

    def sum_a(yy, zz):
        where = (yy, zz, x, full, LEFT)
        total = wide(mine, *where) + wide(other, *where)
        for k in range(3):
            total = total + wide(land_a, k, yy, zz)
        return total

    def sum_b(zz, xx):
        where = (y, zz, xx, full, RIGHT)
        total = wide(mine, *where) + wide(other, *where)
        for k in range(3):
            total = total + wide(land_b, k, zz, xx)
        return total

    for d in order[:3]:
        for zz in range(2):
            next_a[y_after(d), zz] = sum_a(y_after(d), zz).astype(jnp.bfloat16)
        two_a(d).start()
        for zz in range(2):
            next_b[x_after(d), zz] = sum_b(zz, x_after(d)).astype(jnp.bfloat16)
        two_b(d).start()
    away, here = [sum_a(y, 1 - z), sum_b(1 - z, x)], [sum_a(y, z), sum_b(z, x)]
    for d in (1, 3, 2):
        two_a(d).wait_recv()
        two_b(d).wait_recv()
    for k in range(3):
        for part, land in enumerate((land_c, land_d)):
            away[part] = away[part] + wide(land, k, 1 - z)
            here[part] = here[part] + wide(land, k, z)
    last_out[:, LEFT] = away[0].astype(jnp.bfloat16)
    last_out[:, RIGHT] = away[1].astype(jnp.bfloat16)
    last = remote(last_out, last_in, last_send, last_recv, at(y, 1 - z, x, core))
    last.start()
    last.wait_recv()
    out_ref[:, LEFT] = here[0] + wide(last_in, full, LEFT)
    out_ref[:, RIGHT] = here[1] + wide(last_in, full, RIGHT)
    share[...] = out_ref[:, 3072:]
    across = remote(share, taken, share_send, share_recv, (1 - pipe, dp))

    @pl.when(pipe == 1)
    def _():
        across.start()
        few_ref[...] = share[...]
        across.wait_send()

    for d in order:
        near_a(d).wait_send()
        near_b(d).wait_send()
    for d in order[:3]:
        one_a(d).wait_send()
        one_b(d).wait_send()
        two_a(d).wait_send()
        two_b(d).wait_send()
    last.wait_send()

    @pl.when(pipe == 0)
    def _():
        across.wait_recv()
        few_ref[...] = taken[...]


def scatter_blocks(blocks):
    half = (4, 2, 4, 16, WIDE)
    low = jnp.bfloat16
    sems = pltpu.SemaphoreType.DMA
    return pl.pallas_call(
        scatter_kernel,
        out_shape=[
            jax.ShapeDtypeStruct((16, WIDE), jnp.float32),
            jax.ShapeDtypeStruct((16, 128), jnp.float32),
        ],
        in_specs=[pl.BlockSpec(memory_space=pl.ANY)],
        out_specs=[pl.BlockSpec(memory_space=pltpu.VMEM)] * 2,
        scratch_shapes=[
            pltpu.VMEM(half, low),
            pltpu.VMEM(half, low),
            pltpu.VMEM((3, 4, 2, 16, CUT), low),
            pltpu.VMEM((3, 2, 4, 16, WIDE - CUT), low),
            pltpu.VMEM((4, 2, 16, CUT), low),
            pltpu.VMEM((4, 2, 16, WIDE - CUT), low),
            pltpu.VMEM((3, 2, 16, CUT), low),
            pltpu.VMEM((3, 2, 16, WIDE - CUT), low),
            pltpu.VMEM((16, WIDE), low),
            pltpu.VMEM((16, WIDE), low),
            pltpu.VMEM((16, 128), jnp.float32),
            pltpu.VMEM((16, 128), jnp.float32),
            sems, sems((8,)), sems((8,)), sems((6,)), sems((6,)), sems((6,)), sems((6,)), sems, sems, sems, sems,
        ],
        compiler_params=pltpu.CompilerParams(
            collective_id=0, has_side_effects=True, vmem_limit_bytes=60 << 20
        ),
        name="scatter_gradients",
    )(blocks.reshape(4, 2, 4, 2, 16, WIDE))


BF = jnp.bfloat16
F32 = jnp.float32
SCALE = HEAD_DIM**-0.5
PAD = 1152
NN = (((1,), (0,)), ((), ()))
NT = (((1,), (1,)), ((), ()))
TN = (((0,), (0,)), ((), ()))
SPAN = 272
SPANS = SEQ // SPAN
WIDTH = 384
WIDTHS = PAD // WIDTH
COLUMNS = PAD // 128
ANY = pl.BlockSpec(memory_space=pl.ANY)
INSIDE = pl.BlockSpec(memory_space=pltpu.VMEM)
SCALARS = pl.BlockSpec(memory_space=pltpu.SMEM)


def dot(left, right, dims=NN):
    return lax.dot_general(left, right, dims, preferred_element_type=F32)


def normal(value):
    center = jnp.mean(value, axis=-1, keepdims=True)
    centred = value - center
    spread = jnp.mean(centred * centred, axis=-1, keepdims=True)
    rate = lax.rsqrt(spread + EPSILON)
    return centred * rate, rate


def normal_back(value, gain, d_normed):
    hat, rate = normal(value)
    scaled = d_normed * gain
    first = jnp.mean(scaled, axis=-1, keepdims=True)
    second = jnp.mean(scaled * hat, axis=-1, keepdims=True)
    terms = d_normed * hat
    return rate * (scaled - first - hat * second), fold_rows(terms), hat


def fold_rows(terms):
    return jnp.sum(terms.reshape(-1, 8, D), axis=0)


def gelu_pair(value):
    square = value * value
    inner = value * (0.7978845608028654 + 0.035677408136300125 * square)
    half = 0.5 + 0.5 * jnp.tanh(inner)
    out = value * half
    slope = half + out * (1.0 - half) * (1.5957691216057308 + 0.21406444881780075 * square)
    return out.astype(BF), slope.astype(BF)


def feed_forward(middle, gain, up, down, act_ref, slope_ref, rows):
    normed = (normal(middle)[0] * gain).astype(BF)
    total = middle
    hidden = dot(normed, up[:, 0:512])
    for j in range(4):
        cols = slice(j * 512, (j + 1) * 512)
        after = dot(normed, up[:, cols.stop : cols.stop + 512]) if j < 3 else None
        act, slope = gelu_pair(hidden)
        act_ref[rows, cols] = act
        slope_ref[rows, cols] = slope
        total = total + dot(act, down[cols, :])
        hidden = after
    return normed, total


def lane_is_low(shape):
    return lax.rem(lax.broadcasted_iota(jnp.int32, shape, len(shape) - 1), 128) < 64


def head_mask(shape):
    lane = lax.broadcasted_iota(jnp.int32, shape, 1)
    return [(lane >= 64 * h) & (lane < 64 * h + 64) for h in range(4)]


def spread_heads(value, masks):
    zero = jnp.zeros_like(value)
    return jnp.concatenate([jnp.where(m, value, zero) for m in masks], axis=0)


def fold_heads(value, masks):
    total = jnp.where(masks[0], value[:64], 0.0)
    for h in range(1, 4):
        total = total + jnp.where(masks[h], value[64 * h : 64 * h + 64], 0.0)
    return total


def head_blocks():
    row = lax.broadcasted_iota(jnp.int32, (256, 256), 0)
    lane = lax.broadcasted_iota(jnp.int32, (256, 256), 1)
    return (lax.div(row, 64) == lax.div(lane, 64)).astype(BF)


def frame_groups():
    for f in range(FRAMES):
        for g in range(2):
            yield slice(f * 64, f * 64 + 64), g * 256


SLAB = 136


def window_forward(mixed, scores, probs, context):
    masks = head_mask((64, 256))
    for rows, at in frame_groups():
        keys = spread_heads(mixed[rows, 512 + at : 768 + at], masks)
        scores[rows, at : at + 256] = dot(mixed[rows, at : at + 256], keys, NT)
    low = lane_is_low((SLAB, 128))

    def soften(i):
        rows = row_span(i, SLAB)
        for c in range(4):
            cols = slice(c * 128, c * 128 + 128)
            piece = scores[rows, cols]
            left = jnp.max(jnp.where(low, piece, -jnp.inf), axis=1, keepdims=True)
            right = jnp.max(jnp.where(low, -jnp.inf, piece), axis=1, keepdims=True)
            scores[rows, cols] = jnp.exp((piece - jnp.where(low, left, right)) * SCALE)

    loop(SEQ // SLAB, soften)
    ones = head_blocks()
    for rows, at in frame_groups():
        cols = slice(at, at + 256)
        power = scores[rows, cols].astype(BF)
        inverse = 1.0 / dot(power, ones)
        values = spread_heads(mixed[rows, 1024 + at : 1280 + at], masks)
        context[rows, cols] = (dot(power, values) * inverse).astype(BF)
        probs[rows, cols] = (power.astype(F32) * inverse).astype(BF)


def window_backward(mixed, probs, d_context, d_probs, d_scores, d_mixed):
    masks = head_mask((64, 256))
    for rows, at in frame_groups():
        cols = slice(at, at + 256)
        values = spread_heads(mixed[rows, 1024 + at : 1280 + at], masks)
        d_probs[rows, cols] = dot(d_context[rows, cols], values, NT)
    ones = head_blocks()

    def soften(i):
        rows = row_span(i, SPAN)
        for g in range(2):
            cols = slice(g * 256, g * 256 + 256)
            wide = probs[rows, cols].astype(F32)
            here = d_probs[rows, cols]
            delta = dot((wide * here).astype(BF), ones)
            d_scores[rows, cols] = (wide * (here - delta) * SCALE).astype(BF)

    loop(SPANS, soften)
    for rows, at in frame_groups():
        cols = slice(at, at + 256)
        here = d_scores[rows, cols]
        keys = spread_heads(mixed[rows, 512 + at : 768 + at], masks)
        d_mixed[rows, at : at + 256] = dot(here, keys).astype(BF)
        d_keys = fold_heads(dot(here, mixed[rows, at : at + 256], TN), masks)
        d_mixed[rows, 512 + at : 768 + at] = d_keys.astype(BF)
        d_values = fold_heads(dot(probs[rows, cols], d_context[rows, cols], TN), masks)
        d_mixed[rows, 1024 + at : 1280 + at] = d_values.astype(BF)


def loop(count, body):
    def step(index, carry):
        body(index)
        return carry

    lax.fori_loop(0, count, step, 0)


def row_span(index, size):
    return pl.ds(pl.multiple_of(index * size, 16), size)


def valid_rows(start, size, count):
    row = lax.broadcasted_iota(jnp.int32, (size, 1), 0) + start
    return row < count * PATCHES


def first_forward_kernel(micro, *refs):
    (active, frames, video, w_attn, w_up, w_down, gains) = refs[:7]
    (acts, sent, s_mixed, s_context, s_probs, s_middle, s_act, s_slope) = refs[-21:-13]
    (x, attn, up, down, mixed, context, probs, middle, act, slope, out, masked, sems) = refs[-13:]

    @pl.when(active[0] == 1)
    def _():
        count = frames[micro, 0]
        loads = [
            pltpu.make_async_copy(video.at[micro, 0], x, sems.at[0]),
            pltpu.make_async_copy(w_attn, attn, sems.at[1]),
            pltpu.make_async_copy(w_up, up, sems.at[2]),
            pltpu.make_async_copy(w_down, down, sems.at[3]),
        ]
        for copy in loads:
            copy.start()
        loads[0].wait()
        loads[1].wait()

        def project(i):
            rows = row_span(i, SPAN)
            hat, _ = normal(x[rows, :].astype(F32))
            normed = (hat * gains[0:1, :]).astype(BF)
            for j in range(3):
                cols = slice(j * 512, (j + 1) * 512)
                mixed[rows, cols] = dot(normed, attn[:, cols]).astype(BF)

        loop(SPANS, project)
        stores = [pltpu.make_async_copy(mixed, s_mixed, sems.at[4])]
        stores[0].start()
        window_forward(mixed, middle, probs, context)
        for k, (source, target) in enumerate(((context, s_context), (probs, s_probs))):
            stores.append(pltpu.make_async_copy(source, target, sems.at[5 + k]))
            stores[-1].start()
        loads[2].wait()
        loads[3].wait()
        late = ((out, sent), (masked, acts.at[micro]), (middle, s_middle), (act, s_act), (slope, s_slope))

        def late_stores(i):
            rows = row_span(i, SPAN)
            return [
                pltpu.make_async_copy(source.at[rows], target.at[rows], sems.at[7 + k * SPANS + i])
                for k, (source, target) in enumerate(late)
            ]

        def tail(i):
            rows = row_span(i, SPAN)
            here = x[rows, :].astype(F32) + dot(context[rows, :], attn[:, 1536:])
            middle[rows, :] = here
            _, total = feed_forward(here, gains[1:2, :], up, down, act, slope, rows)
            out[rows, :] = total.astype(BF)
            masked[rows, :] = jnp.where(valid_rows(i * SPAN, SPAN, count), total, 0.0).astype(BF)
            for copy in late_stores(i):
                copy.start()

        loop(SPANS, tail)

        def settle(i):
            for copy in late_stores(i):
                copy.wait()

        loop(SPANS, settle)
        for copy in stores:
            copy.wait()


def saved_shapes():
    return [
        jax.ShapeDtypeStruct((SEQ, 3 * D), BF),
        jax.ShapeDtypeStruct((SEQ, D), BF),
        jax.ShapeDtypeStruct((SEQ, D), BF),
        jax.ShapeDtypeStruct((SEQ, D), F32),
        jax.ShapeDtypeStruct((SEQ, FF), BF),
        jax.ShapeDtypeStruct((SEQ, FF), BF),
    ]


def weight_scratch():
    return [pltpu.VMEM((D, 4 * D), BF), pltpu.VMEM((D, FF), BF), pltpu.VMEM((FF, D), BF)]


def first_forward(micro, active, frames, video, weights, acts=None):
    saved = saved_shapes()
    inputs = [active, frames, video, *weights] + ([] if acts is None else [acts])
    result = pl.pallas_call(
        functools.partial(first_forward_kernel, micro),
        out_shape=[jax.ShapeDtypeStruct((2, SEQ, D), BF), jax.ShapeDtypeStruct((SEQ, D), BF)] + saved,
        in_specs=([SCALARS, SCALARS, ANY, ANY, ANY, ANY, INSIDE, ANY])[: len(inputs)],
        out_specs=[ANY] * 8,
        input_output_aliases={} if acts is None else {7: 0},
        scratch_shapes=[pltpu.VMEM((SEQ, D), BF)] + weight_scratch()
        + [pltpu.VMEM(s.shape, s.dtype) for s in saved]
        + [pltpu.VMEM((SEQ, D), BF), pltpu.VMEM((SEQ, D), BF), pltpu.SemaphoreType.DMA((27,))],
        compiler_params=pltpu.CompilerParams(vmem_limit_bytes=60 << 20),
        name=f"first_forward_{micro}",
    )(*inputs)
    return result[0], result[1], result[2:]


def lanes_at(start, size=512):
    return pl.ds(pl.multiple_of(start, 128), size)


def put_wide(blocks, old, at, left, right):
    lanes = lanes_at(at)
    value = jnp.concatenate([left.reshape(64, 8, 512), right.reshape(64, 8, 512)], axis=1)
    if old is not None:
        value = value + old[:, :, lanes].astype(F32)
    blocks[:, :, lanes] = value.astype(BF)


def put_tall(blocks, old, part, value):
    value = value.reshape(16, 2, 16, 512)
    into = pl.ds(part * 16, 16)
    for half in range(2):
        lanes = slice(2048 + half * 512, 2560 + half * 512)
        piece = value[:, half]
        if old is not None:
            piece = piece + old[into, :, lanes].astype(F32)
        blocks[into, :, lanes] = piece.astype(BF)


def send_lanes(source, target, at, size, sem):
    lanes = pl.ds(at, size)
    copy = pltpu.make_async_copy(source.at[:, :, lanes], target.at[:, :, lanes], sem)
    copy.start()
    return copy


def spread_gains(sums, few):
    dst = lax.broadcasted_iota(jnp.int32, (64, D), 0)
    lane = lax.broadcasted_iota(jnp.int32, (64, D), 1)
    source = lax.broadcasted_iota(jnp.int32, (D, 128), 0)
    place = lax.broadcasted_iota(jnp.int32, (D, 128), 1)
    total = jnp.zeros((64, 128), F32)
    for k in range(2):
        row = jnp.sum(sums[8 * k : 8 * k + 8, :], axis=0, keepdims=True)
        mine = jnp.where(lane // 8 == dst, row, 0.0)
        pick = (lax.rem(source, 8) + 8 * k == place).astype(F32)
        total = total + lax.dot_general(mine, pick, NN, precision=lax.Precision.HIGHEST, preferred_element_type=F32)
    few[:, 8, :] = total


def first_backward_kernel(micro, fresh, *refs):
    (active, video, w_attn, w_up, w_down, gains, d_in, s_mixed, s_context, s_probs, s_middle, s_act, s_slope) = refs[:13]
    if fresh:
        _, grad_in, blocks, new_gains = refs[13:17]
    else:
        _, _, old_blocks, old_gains, grad_in, blocks = refs[13:19]
    (x, attn, up, down, mixed, context, probs, middle, act, slope, d_two, normed, d_branch, d_mid, d_context,
     g_out, g_gains, more_gains, few, block_out, block_old, sems) = refs[-22:]
    old = None if fresh else block_old

    @pl.when(active[0] == 1)
    def _():
        pairs = [
            (d_in, d_two), (w_down, down), (s_slope, slope), (w_up, up), (s_middle, middle), (s_act, act),
            (w_attn, attn), (s_context, context), (s_probs, probs), (s_mixed, mixed), (video.at[micro, 0], x),
        ]
        if not fresh:
            pairs[6:6] = [(old_blocks, block_old), (old_gains, more_gains)]
        loads = [pltpu.make_async_copy(s, t, sems.at[k]) for k, (s, t) in enumerate(pairs)]
        for copy in loads:
            copy.start()
        g_gains[...] = jnp.zeros_like(g_gains)
        for k in range(5):
            loads[k].wait()
        gain = gains[1:2, :]

        def tail(i):
            rows = row_span(i, SPAN)
            d_low = d_two[rows, :]
            total = jnp.zeros((SPAN, D), F32)
            d_act = dot(d_low, down[0:512, :], NT)
            for j in range(4):
                cols = slice(j * 512, (j + 1) * 512)
                after = dot(d_low, down[cols.stop : cols.stop + 512, :], NT) if j < 3 else None
                d_hidden = (d_act * slope[rows, cols].astype(F32)).astype(BF)
                slope[rows, cols] = d_hidden
                total = total + dot(d_hidden, up[:, cols], NT)
                d_act = after
            here = middle[rows, :]
            d_here, g_rows, hat = normal_back(here, gain, total)
            g_gains[8:16, :] += g_rows
            normed[rows, :] = (hat * gain).astype(BF)
            d_here = d_low.astype(F32) + d_here
            d_mid[rows, :] = d_here
            d_branch[rows, :] = d_here.astype(BF)

        loop(SPANS, tail)
        for copy in loads[5 : 7 if fresh else 9]:
            copy.wait()
        loop(4, lambda j: put_tall(block_out, old, j, dot(act[:, lanes_at(j * 512)], d_two[...], TN)))
        stores = [send_lanes(block_out, blocks, 2048, 1024, sems.at[13])]

        def put_up(j):
            left, right = slope[:, lanes_at(j * 512)], slope[:, lanes_at(1024 + j * 512)]
            put_wide(block_out, old, 1024 + j * 512, dot(normed[...], left, TN), dot(normed[...], right, TN))

        loop(2, put_up)
        stores.append(send_lanes(block_out, blocks, 1024, 1024, sems.at[14]))
        for copy in loads[7 if fresh else 9 :]:
            copy.wait()
        g_out[...] = dot(context[...], d_branch[...], TN)

        def into_context(i):
            rows = row_span(i, SPAN)
            d_context[rows, :] = dot(d_branch[rows, :], attn[:, 1536:], NT).astype(BF)

        loop(SPANS, into_context)
        d_mixed = act
        window_backward(mixed, probs, d_context, middle, normed, d_mixed)
        gain_one = gains[0:1, :]

        def head(i):
            rows = row_span(i, SPAN)
            total = jnp.zeros((SPAN, D), F32)
            for j in range(3):
                cols = slice(j * 512, (j + 1) * 512)
                total = total + dot(d_mixed[rows, cols], attn[:, cols], NT)
            d_here, g_rows, hat = normal_back(x[rows, :].astype(F32), gain_one, total)
            g_gains[0:8, :] += g_rows
            normed[rows, :] = (hat * gain_one).astype(BF)
            d_branch[rows, :] = (d_mid[rows, :] + d_here).astype(BF)

        loop(SPANS, head)
        stores.append(pltpu.make_async_copy(d_branch, grad_in.at[micro], sems.at[15]))
        stores[-1].start()
        if fresh:
            stores.append(pltpu.make_async_copy(g_gains, new_gains, sems.at[16]))
            stores[-1].start()
        else:
            few[...] = jnp.zeros_like(few)
            spread_gains(g_gains[...] + more_gains[...], few)
            block_out[:, :, 3072:] = few[...].astype(BF)
        put_wide(
            block_out, old, 0, dot(normed[...], d_mixed[:, :512], TN), dot(normed[...], d_mixed[:, 1024:1536], TN)
        )
        put_wide(block_out, old, 512, dot(normed[...], d_mixed[:, 512:1024], TN), g_out[...])
        stores.append(send_lanes(block_out, blocks, 0, 1024, sems.at[17]))
        if not fresh:
            stores.append(send_lanes(block_out, blocks, 3072, 128, sems.at[16]))
        for copy in stores:
            copy.wait()


BLOCKS = jax.ShapeDtypeStruct((64, 16, WIDE), BF)
GAINS = jax.ShapeDtypeStruct((16, D), F32)


def first_backward(micro, active, video, weights, d_in, saved, grad_in, blocks=None, before=None):
    kept = saved_shapes()
    rows = pltpu.VMEM((SEQ, D), BF)
    fresh = before is None
    inputs = [active, video, *weights, d_in, *saved, grad_in]
    outputs = [jax.ShapeDtypeStruct(grad_in.shape, BF), BLOCKS]
    aliases = {13: 0}
    if fresh:
        outputs += [GAINS]
    else:
        inputs += [blocks, *before]
        aliases = {13: 0, 14: 1}
    sums = pltpu.VMEM((16, D), F32)
    result = pl.pallas_call(
        functools.partial(first_backward_kernel, micro, fresh),
        out_shape=outputs,
        in_specs=[SCALARS, ANY, ANY, ANY, ANY, INSIDE] + [ANY] * (len(inputs) - 6),
        out_specs=[ANY] * len(outputs),
        input_output_aliases=aliases,
        scratch_shapes=[rows] + weight_scratch() + [pltpu.VMEM(s.shape, s.dtype) for s in kept]
        + [rows, rows, rows, pltpu.VMEM((SEQ, D), F32), rows, pltpu.VMEM((D, D), F32), sums, sums]
        + [pltpu.VMEM((64, 16, 128), F32), pltpu.VMEM((64, 16, WIDE), BF), pltpu.VMEM((64, 16, WIDE), BF)]
        + [pltpu.SemaphoreType.DMA((18,))],
        compiler_params=pltpu.CompilerParams(vmem_limit_bytes=62 << 20),
        name=f"first_backward_{micro}",
    )(*inputs)
    return result[0], *result[1:]


def column(index):
    return slice(index * 128, index * 128 + 128)


def load_head(head, mixed, refs, scale):
    for part, (ref, turned) in enumerate(refs):
        rows = pl.ds(pl.multiple_of(part * D + head * HEAD_DIM, HEAD_DIM), HEAD_DIM)
        for c in range(COLUMNS):
            value = mixed[rows, column(c)].astype(F32)
            if part == 0 and scale:
                value = value * SCALE
            ref[:, column(c)] = value
            if turned is not None:
                turned[:, column(c)] = pltpu.roll(value, 64, 1)


def pair_rows(left, refs, a, rows_ref):
    for s, ref in enumerate(refs):
        for b in range(a + 1):
            rows_ref[9 * s + b : 9 * s + b + 1, :] = jnp.sum(left * ref[:, column(b)], axis=0, keepdims=True)


def weighted(rows_ref, refs, a):
    total = None
    for s, ref in enumerate(refs):
        for b in range(a + 1):
            term = rows_ref[9 * s + b : 9 * s + b + 1, :] * ref[:, column(b)]
            total = term if total is None else total + term
    return total


def temporal_head(head, order, mixed, probs, context, q, k, v, kt, vt, rows_ref):
    load_head(head, mixed, ((q, None), (k, kt), (v, vt)), True)
    out_rows = pl.ds(pl.multiple_of(head * HEAD_DIM, HEAD_DIM), HEAD_DIM)
    for a in range(COLUMNS):
        pair_rows(q[:, column(a)], (k, kt), a, rows_ref)
        scores = jnp.where(order[...] <= 2 * a, rows_ref[...], MASKED)
        power = jnp.exp(scores - jnp.max(scores, axis=0, keepdims=True))
        probs[head, a] = power / jnp.sum(power, axis=0, keepdims=True)
        context[out_rows, column(a)] = weighted(probs.at[head, a], (v, vt), a).astype(BF)


def temporal_head_back(head, mixed, probs, d_context, q, k, v, kt, vt, dc, rows_ref, ds):
    load_head(head, mixed, ((q, None), (k, kt), (v, vt)), False)
    in_rows = pl.ds(pl.multiple_of(head * HEAD_DIM, HEAD_DIM), HEAD_DIM)
    for c in range(COLUMNS):
        dc[:, column(c)] = d_context[in_rows, column(c)].astype(F32)
    for a in range(COLUMNS):
        pair_rows(dc[:, column(a)], (v, vt), a, rows_ref)
        p = probs[head, a]
        d_probs = jnp.where(p > 0.0, rows_ref[...], 0.0)
        delta = jnp.sum(d_probs * p, axis=0, keepdims=True)
        ds[a] = p * (d_probs - delta) * SCALE
        mixed[in_rows, column(a)] = weighted(ds.at[a], (k, kt), a).astype(BF)
    for part, (weight, source) in enumerate(((lambda a, r: ds[a, r : r + 1, :], q), (lambda a, r: probs[head, a, r : r + 1, :], dc))):
        rows = pl.ds(pl.multiple_of((part + 1) * D + head * HEAD_DIM, HEAD_DIM), HEAD_DIM)
        for b in range(COLUMNS):
            sums = []
            for s in range(2):
                total = None
                for a in range(b, COLUMNS):
                    term = weight(a, 9 * s + b) * source[:, column(a)]
                    total = term if total is None else total + term
                sums.append(total)
            mixed[rows, column(b)] = (sums[0] + pltpu.roll(sums[1], 64, 1)).astype(BF)


def frame_order(count):
    row = lax.broadcasted_iota(jnp.int32, (24, 128), 0)
    high = (lax.broadcasted_iota(jnp.int32, (24, 128), 1) >= 64).astype(jnp.int32)
    turned = row >= 9
    base = 2 * jnp.where(turned, row - 9, row)
    key_frame = base + jnp.where(turned, 1 - high, high)
    return jnp.where((row < 18) & (key_frame < count), key_frame - high, 1000)


def second_kernel(micro, fresh, *refs):
    (active, frames, received, w_attn, w_turned, w_up, w_down, gains, cot_h, cot_q, codes, quant) = refs[:12]
    if fresh:
        _, acts, grad_in, sent_back = refs[12:16]
        old = []
    else:
        _, _, *old = refs[12:17]
        acts, grad_in, sent_back = refs[17:20]
    (s_act, s_hidden, s_normed, s_two, s_d_two, s_branch, s_context, s_mixed, new_gains, new_proj, new_code) = refs[-48:-37]
    (x, attn_out, turned, up, down, normed, normed_two, mixed, context, d_context, probs, middle, act, slope, out,
     masked, d_mid, d_two, cot, cot_codes, code_rows, table, proj_wide, proj, g_gains, g_proj, g_code,
     q, k, v, kt, vt, dc, rows_ref, ds, order, sems) = refs[-37:]

    @pl.when(active[0] == 1)
    def _():
        count = frames[micro, 0]
        real = pl.ds(0, SEQ)
        pairs = [
            (received, x.at[real]), (w_turned, turned), (w_attn.at[:, pl.ds(1536, 512)], attn_out), (w_up, up),
            (w_down, down), (codes.at[micro], code_rows.at[real]), (cot_q.at[micro], cot_codes.at[real]),
            (cot_h.at[micro, 0], cot.at[real]),
        ]
        pairs += list(zip(old, (g_gains, g_proj, g_code)))
        loads = [pltpu.make_async_copy(s, t, sems.at[i]) for i, (s, t) in enumerate(pairs)]
        for copy in loads:
            copy.start()
        stores = []

        def save(source, target):
            stores.append(pltpu.make_async_copy(source, target, sems.at[11 + len(stores)]))
            stores[-1].start()

        tail_rows = pl.ds(SEQ, PAD - SEQ)
        x[tail_rows, :] = jnp.zeros((PAD - SEQ, D), BF)
        cot[tail_rows, :] = jnp.zeros((PAD - SEQ, D), BF)
        cot_codes[tail_rows, :] = jnp.zeros((PAD - SEQ, 128), BF)
        code_rows[tail_rows, :] = jnp.zeros((PAD - SEQ, 128), jnp.int32)
        rows_ref[...] = jnp.zeros_like(rows_ref)
        order[...] = frame_order(count)
        if fresh:
            g_gains[...] = jnp.zeros_like(g_gains)
            g_proj[...] = jnp.zeros_like(g_proj)
            g_code[...] = jnp.zeros_like(g_code)
        for j in range(4):
            table[:, column(j)] = quant[:, j, :].astype(BF)
            proj_wide[pl.ds(j, 128, stride=4), :] = quant[:, 4 + j, :]
        proj[...] = proj_wide[...].astype(BF)
        gain_one, gain_two = gains[0:1, :], gains[1:2, :]
        loads[0].wait()
        loads[1].wait()

        def project(i):
            rows, lanes = row_span(i, WIDTH), lanes_at(i * WIDTH, WIDTH)
            normed[rows, :] = (normal(x[rows, :].astype(F32))[0] * gain_one).astype(BF)
            for j in range(3):
                parts = slice(j * 512, (j + 1) * 512)
                mixed[parts, lanes] = dot(turned[parts, :], normed[rows, :], NT).astype(BF)

        loop(WIDTHS, project)
        save(normed, s_normed)
        loop(HEADS, lambda h: temporal_head(h, order, mixed, probs, context, q, k, v, kt, vt, rows_ref))
        save(context, s_context)
        for copy in loads[2:]:
            copy.wait()

        def forward_tail(i):
            rows = row_span(i, WIDTH)
            here = x[rows, :].astype(F32) + dot(context[:, lanes_at(i * WIDTH, WIDTH)], attn_out[...], TN)
            middle[rows, :] = here
            normed_low, total = feed_forward(here, gain_two, up, down, act, slope, rows)
            normed_two[rows, :] = normed_low
            valid = valid_rows(i * WIDTH, WIDTH, count)
            low = total.astype(BF)
            out[rows, :] = low
            masked[rows, :] = jnp.where(valid, total, 0.0).astype(BF)
            mask = valid.astype(F32)
            latent = dot(low, proj[...])
            code = code_rows[rows, :]
            lane = lax.broadcasted_iota(jnp.int32, (WIDTH, 128), 1)
            high = (lax.div(code, LOW_CODES) == lane).astype(BF)
            near = dot(high, table[...])
            spot = lax.rem(code, LOW_CODES) == lax.rem(lane, LOW_CODES)
            spots = jnp.concatenate([spot] * 4, axis=1)
            place = lax.div(lax.broadcasted_iota(jnp.int32, (512, 128), 0), LOW_CODES)
            pick = (place == lax.broadcasted_iota(jnp.int32, (512, 128), 1)).astype(BF)
            chosen = dot(jnp.where(spots, near, 0.0).astype(BF), pick)
            d_latent = (mask * (cot_codes[rows, :].astype(F32) + 2.0 * BETA * (latent - chosen))).astype(BF)
            d_chosen = (2.0 * mask * (chosen - latent)).astype(BF)
            g_proj[...] += dot(low, d_latent, TN)
            spread = jnp.where(spots, dot(d_chosen, pick, NT), 0.0).astype(BF)
            g_code[...] += dot(high, spread, TN)
            d_out = cot[rows, :].astype(F32) * mask + dot(d_latent, proj[...], NT)
            d_two[rows, :] = d_out.astype(BF)
            d_mid[rows, :] = d_out

        loop(WIDTHS, forward_tail)
        save(masked.at[real], acts.at[micro])
        save(act, s_act)
        save(normed_two, s_two)
        save(d_two, s_d_two)
        save(g_proj, new_proj)
        save(g_code, new_code)
        d_branch = out

        def backward_tail(i):
            rows = row_span(i, WIDTH)
            d_low = d_two[rows, :]
            total = jnp.zeros((WIDTH, D), F32)
            d_act = dot(d_low, down[0:512, :], NT)
            for j in range(4):
                cols = slice(j * 512, (j + 1) * 512)
                after = dot(d_low, down[cols.stop : cols.stop + 512, :], NT) if j < 3 else None
                d_hidden = (d_act * slope[rows, cols].astype(F32)).astype(BF)
                slope[rows, cols] = d_hidden
                total = total + dot(d_hidden, up[:, cols], NT)
                d_act = after
            d_here, g_rows, _ = normal_back(middle[rows, :], gain_two, total)
            g_gains[8:16, :] += g_rows
            d_here = d_mid[rows, :] + d_here
            d_mid[rows, :] = d_here
            d_low = d_here.astype(BF)
            d_branch[rows, :] = d_low
            d_context[:, lanes_at(i * WIDTH, WIDTH)] = dot(attn_out[...], d_low, NT).astype(BF)

        loop(WIDTHS, backward_tail)
        save(slope, s_hidden)
        save(d_branch, s_branch)
        loop(
            HEADS,
            lambda h: temporal_head_back(h, mixed, probs, d_context, q, k, v, kt, vt, dc, rows_ref, ds),
        )
        save(mixed, s_mixed)
        d_x = cot

        def finish(i):
            rows = row_span(i, WIDTH)
            total = dot(mixed[:, lanes_at(i * WIDTH, WIDTH)], turned[...], TN)
            d_here, g_rows, _ = normal_back(x[rows, :].astype(F32), gain_one, total)
            g_gains[0:8, :] += g_rows
            d_x[rows, :] = (d_mid[rows, :] + d_here).astype(BF)

        loop(WIDTHS, finish)
        save(d_x.at[real], sent_back)
        save(d_x.at[real], grad_in.at[micro])
        save(g_gains, new_gains)
        for copy in stores:
            copy.wait()


TOKENS = jax.ShapeDtypeStruct((PAD, D), BF)
HIDDEN = jax.ShapeDtypeStruct((PAD, FF), BF)
KEPT = [
    HIDDEN, HIDDEN, TOKENS, TOKENS, TOKENS, TOKENS,
    jax.ShapeDtypeStruct((D, PAD), BF), jax.ShapeDtypeStruct((3 * D, PAD), BF),
]
SMALL = [
    GAINS,
    jax.ShapeDtypeStruct((D, 128), F32),
    jax.ShapeDtypeStruct((128, 512), F32),
]


def second_section(micro, active, frames, received, weights, cots, acts, grad_in=None, small=None):
    fresh = small is None
    inputs = [active, frames, received, *weights, *cots, acts]
    outputs = [
        jax.ShapeDtypeStruct(acts.shape, BF),
        jax.ShapeDtypeStruct(acts.shape, BF),
        jax.ShapeDtypeStruct((SEQ, D), BF),
    ] + KEPT + SMALL
    aliases = {12: 0}
    if not fresh:
        inputs += [grad_in, *small]
        aliases = {12: 0, 13: 1}
    tokens = pltpu.VMEM((PAD, D), BF)
    tokens_wide = pltpu.VMEM((PAD, D), F32)
    flipped = pltpu.VMEM((D, PAD), BF)
    hidden = pltpu.VMEM((PAD, FF), BF)
    one_head = pltpu.VMEM((HEAD_DIM, PAD), F32)
    scratch = [
        tokens, pltpu.VMEM((D, D), BF), pltpu.VMEM((3 * D, D), BF), pltpu.VMEM((D, FF), BF), pltpu.VMEM((FF, D), BF),
        tokens, tokens, pltpu.VMEM((3 * D, PAD), BF), flipped, flipped, pltpu.VMEM((HEADS, COLUMNS, 24, 128), F32),
        tokens_wide, hidden, hidden, tokens, tokens, tokens_wide, tokens, tokens, pltpu.VMEM((PAD, 128), BF),
        pltpu.VMEM((PAD, 128), jnp.int32), pltpu.VMEM((128, 512), BF), pltpu.VMEM((D, 128), F32),
        pltpu.VMEM((D, 128), BF),
    ]
    scratch += [pltpu.VMEM(s.shape, s.dtype) for s in SMALL] + [one_head] * 6 + [
        pltpu.VMEM((24, 128), F32), pltpu.VMEM((COLUMNS, 24, 128), F32), pltpu.VMEM((24, 128), jnp.int32),
        pltpu.SemaphoreType.DMA((28,)),
    ]
    specs = [SCALARS, SCALARS, ANY, ANY, ANY, ANY, ANY, INSIDE, ANY, ANY, ANY, INSIDE]
    result = pl.pallas_call(
        functools.partial(second_kernel, micro, fresh),
        out_shape=outputs,
        in_specs=specs + [ANY] * (len(inputs) - 12),
        out_specs=[ANY] * len(outputs),
        input_output_aliases=aliases,
        scratch_shapes=scratch,
        compiler_params=pltpu.CompilerParams(vmem_limit_bytes=62 << 20),
        name=f"second_section_{micro}",
    )(*inputs)
    return result[0], result[1], result[2], result[3:11], result[11:]


def second_grads_kernel(active, *refs):
    kept = (refs[:8], refs[8:16])
    s_gains, s_proj, s_code, blocks = refs[16:20]
    (act, hidden, normed, normed_two, d_two, d_branch, context, mixed, g_gains, g_proj, g_code, few, block_out, sems) = refs[20:]
    held = (act, hidden, normed, normed_two, d_two, d_branch, context, mixed)

    @pl.when(active[0] == 1)
    def _():
        loads = {}
        for k in (0, 4, 1, 3, 6, 5, 7, 2):
            for m in range(2):
                at = pl.ds(m * PAD, PAD)
                into = held[k].at[:, at] if k >= 6 else held[k].at[at]
                loads[k, m] = pltpu.make_async_copy(kept[m][k], into, sems.at[2 * k + m])
                loads[k, m].start()
        tiny = [
            pltpu.make_async_copy(s, t, sems.at[16 + i])
            for i, (s, t) in enumerate(((s_gains, g_gains), (s_proj, g_proj), (s_code, g_code)))
        ]
        for copy in tiny:
            copy.start()

        def need(*keys):
            for k in keys:
                for m in range(2):
                    loads[k, m].wait()

        need(0, 4)
        for j in range(4):
            put_tall(block_out, None, j, dot(act[:, j * 512 : j * 512 + 512], d_two[...], TN))
        stores = [send_lanes(block_out, blocks, 2048, 1024, sems.at[19])]
        need(1, 3)
        for j in range(2):
            left, right = hidden[:, j * 512 : j * 512 + 512], hidden[:, 1024 + j * 512 : 1536 + j * 512]
            put_wide(
                block_out, None, 1024 + j * 512, dot(normed_two[...], left, TN), dot(normed_two[...], right, TN)
            )
        stores.append(send_lanes(block_out, blocks, 1024, 1024, sems.at[20]))
        need(6, 5, 7, 2)
        parts = [dot(mixed[j * 512 : j * 512 + 512, :], normed[...]).T for j in range(3)]
        put_wide(block_out, None, 0, parts[0], parts[2])
        put_wide(block_out, None, 512, parts[1], dot(context[...], d_branch[...]))
        stores.append(send_lanes(block_out, blocks, 0, 1024, sems.at[21]))
        for copy in tiny:
            copy.wait()
        few[...] = jnp.zeros_like(few)
        spread_gains(g_gains[...], few)
        for j in range(4):
            few[:, j, :] = g_code[0:64, column(j)]
            few[:, 4 + j, :] = g_code[64:128, column(j)]
        for j in range(4):
            first = g_proj[pl.ds(j, 64, stride=4), :]
            second = g_proj[pl.ds(256 + j, 64, stride=4), :]
            few[:, 9 + j, :] = first + pltpu.roll(second, 64, 1)
        block_out[:, :, 3072:] = few[...].astype(BF)
        stores.append(send_lanes(block_out, blocks, 3072, 128, sems.at[22]))
        for copy in stores:
            copy.wait()


def second_grads(active, kept_0, kept_1, small):
    twice = [
        pltpu.VMEM((s.shape[0], 2 * PAD) if s.shape[1] == PAD else (2 * PAD, s.shape[1]), BF) for s in KEPT
    ]
    return pl.pallas_call(
        second_grads_kernel,
        out_shape=BLOCKS,
        in_specs=[SCALARS] + [ANY] * 19,
        out_specs=ANY,
        scratch_shapes=twice + [pltpu.VMEM(s.shape, s.dtype) for s in SMALL]
        + [pltpu.VMEM((64, 16, 128), F32), pltpu.VMEM((64, 16, WIDE), BF), pltpu.SemaphoreType.DMA((23,))],
        compiler_params=pltpu.CompilerParams(vmem_limit_bytes=62 << 20),
        name="second_grads",
    )(active, *kept_0, *kept_1, *small)


def average(ema, weight, grad, rate):
    return rate * ema + (1.0 - rate) * (weight - LEARN_RATE * grad)


def average_kernel(first, rates, total, few, *refs):
    weights, emas, grads, news = refs[:6], refs[6:12], refs[12:18], refs[18:24]
    grads[0][0, :, :1024] = total[0:8, 0:1024]
    grads[0][0, :, 1024:] = total[8:16, 0:1024]
    grads[1][0, :, :1024] = total[0:8, 1024:2048]
    grads[1][0, :, 1024:] = total[8:16, 1024:2048]
    grads[2][0, 0:16, :] = total[:, 2048:2560]
    grads[2][0, 16:32, :] = total[:, 2560:3072]
    gain = total[8:9, 3072:3200]
    grads[3][0, 0:1, :] = gain[:, 0:8]
    grads[3][0, 1:2, :] = pltpu.roll(gain, 120, 1)[:, 0:8]
    is_first = first[0] == 1
    proj = few[9:13, :]
    grads[4][...] = jnp.where(is_first, proj, pltpu.roll(proj, 64, 1))[:, 0:8]
    code = jnp.where(is_first, few[0:4, :], few[4:8, :])
    turned = pltpu.roll(code, 64, 1)
    for r in range(4):
        grads[5][2 * r : 2 * r + 1, :] = code[r : r + 1, 0:64]
        grads[5][2 * r + 1 : 2 * r + 2, :] = turned[r : r + 1, 0:64]
    for i in range(6):
        rate = rates[0] if i < 4 else rates[1]
        news[i][...] = average(emas[i][...], weights[i][...].astype(F32), grads[i][...], rate)


def averages(first, rates, total, few, weights, emas):
    shapes = [jax.ShapeDtypeStruct(e.shape, F32) for e in emas]
    return pl.pallas_call(
        average_kernel,
        out_shape=shapes * 2,
        in_specs=[SCALARS, SCALARS] + [INSIDE] * 14,
        out_specs=[INSIDE] * 12,
        name="averages",
    )(first, rates, total, few, *weights, *emas)


def per_device(
    video, cot_h, cot_q, frames, codes, w_attn, w_up, w_down, gains, proj, codebook,
    ema_attn, ema_up, ema_down, ema_gains, ema_proj, ema_code, decay,
):
    segment = lax.axis_index("pipe")
    in_first = (segment == 0).astype(jnp.int32).reshape(1)
    in_second = 1 - in_first
    weights = (w_attn[0], w_up[0], w_down[0], gains[0])

    block = jnp.concatenate([codebook.reshape(4, 128), jnp.pad(proj, ((0, 0), (0, 120)))], axis=0)
    block = block.astype(F32)
    acts, sent_0, saved_0 = first_forward(0, in_first, frames, video, weights)
    sent_0, block = lax.optimization_barrier((sent_0, block))
    block_first = lax.ppermute(block, "pipe", [(0, 1)])
    received_0 = lax.ppermute(sent_0, "pipe", [(0, 1)])

    w_attn_late, w_up_late, w_down_late, gains_late, cot_q, codes, decay, _ = lax.optimization_barrier(
        (w_attn, w_up, w_down, gains, cot_q, codes, decay, sent_0)
    )
    cot_rows = jnp.pad(jnp.swapaxes(cot_q[:, 0], 1, 2), ((0, 0), (0, 0), (0, 120)))
    code_rows = jnp.broadcast_to(codes[:, 0, :, None], (2, SEQ, 128))
    turned = w_attn_late[0, :, : 3 * D].T
    lane = lax.axis_index("dp")
    parts = lax.axis_size("dp")

    def own_rows(weight, axis):
        size = weight.shape[axis] // parts
        return lax.dynamic_slice_in_dim(weight, lane * size, size, axis).astype(F32)

    own = (
        own_rows(w_attn_late, 1), own_rows(w_up_late, 1), own_rows(w_down_late, 1), own_rows(gains_late, 2), proj,
        codebook,
    )
    rates = jnp.stack([lax.dynamic_index_in_dim(decay, segment, 0, keepdims=False), decay[2]])
    cot_rows, code_rows, turned, own, rates, block_first = lax.optimization_barrier(
        (cot_rows, code_rows, turned, own, rates, block_first)
    )
    quant = gather_blocks(jnp.stack([block_first, block]))
    second_weights = (w_attn[0], turned, w_up[0], w_down[0], gains[0])
    cots = (cot_h, cot_rows, code_rows, quant)
    video_1, _ = lax.optimization_barrier((video, quant))
    acts, sent_1, saved_1 = first_forward(1, in_first, frames, video_1, weights, acts)
    received_1 = lax.ppermute(sent_1, "pipe", [(0, 1)])

    acts, grad_in, back_0, kept_0, small = second_section(
        0, in_second, frames, received_0, second_weights, cots, acts
    )
    returned_0 = lax.ppermute(back_0, "pipe", [(1, 0)])
    acts, grad_in, back_1, kept_1, small = second_section(
        1, in_second, frames, received_1, second_weights, cots, acts, grad_in, small
    )
    returned_1 = lax.ppermute(back_1, "pipe", [(1, 0)])
    blocks = second_grads(in_second, kept_0, kept_1, small)

    returned_0, blocks = lax.optimization_barrier((returned_0, blocks))
    grad_in, *before = first_backward(0, in_first, video, weights, returned_0, saved_0, grad_in)

    grad_in, blocks = first_backward(
        1, in_first, video, weights, returned_1, saved_1, grad_in, blocks, before
    )
    total, few = scatter_blocks(blocks)
    results = averages(
        in_first, rates, total, few, own, (ema_attn, ema_up, ema_down, ema_gains, ema_proj, ema_code)
    )
    return (acts[None, :, None], grad_in[None, :, None], *results)


def solution(mesh):
    placed = (
        P(None, "dp", None, None),
        P(None, "dp", None, None),
        P(None, "dp", None, None),
        P(None, "dp"),
        P(None, "dp", None),
        P("pipe", None, None),
        P("pipe", None, None),
        P("pipe", None, None),
        P("pipe", None, None),
        P(("pipe", "dp"), None),
        P(None, ("pipe", "dp")),
        P("pipe", "dp", None),
        P("pipe", "dp", None),
        P("pipe", "dp", None),
        P("pipe", None, "dp"),
        P(("pipe", "dp"), None),
        P(None, ("pipe", "dp")),
        P(),
    )
    return jax.shard_map(
        per_device,
        mesh=mesh,
        in_specs=placed,
        out_specs=(
            P("pipe", None, "dp", None, None),
            P("pipe", None, "dp", None, None),
            P("pipe", "dp", None),
            P("pipe", "dp", None),
            P("pipe", "dp", None),
            P("pipe", None, "dp"),
            P(("pipe", "dp"), None),
            P(None, ("pipe", "dp")),
            P("pipe", "dp", None),
            P("pipe", "dp", None),
            P("pipe", "dp", None),
            P("pipe", None, "dp"),
            P(("pipe", "dp"), None),
            P(None, ("pipe", "dp")),
        ),
        check_vma=False,
    )
```

```python
import functools

import jax
import jax.numpy as jnp
from jax import lax
from jax.experimental import pallas as pl
from jax.experimental.pallas import tpu as pltpu
from jax.sharding import PartitionSpec as P

D = 512
HEADS = 8
HEAD_DIM = 64
FF = 2048
CODES = 8192
CODE_DIM = 8
LOW_CODES = 64
PATCHES = 64
FRAMES = 17
SEQ = 1088


EPSILON = 1e-05
BETA = 0.25
LEARN_RATE = 0.0001
MASKED = -1e30
MESH = pl.DeviceIdType.MESH
WIDE = 3200
CUT = 1664
LEFT = pl.ds(0, CUT)
RIGHT = pl.ds(CUT, WIDE - CUT)


def gather_kernel(block_ref, out_ref, landed, send_sems, recv_sems):
    pipe = lax.axis_index("pipe")
    dp = lax.axis_index("dp")

    def copy_of(step):
        return pltpu.make_async_remote_copy(
            src_ref=block_ref,
            dst_ref=landed.at[step],
            send_sem=send_sems.at[step],
            recv_sem=recv_sems.at[step],
            device_id=(1, lax.rem(dp + step, 64)),
            device_id_type=MESH,
        )

    @pl.when(pipe == 1)
    def _():
        barrier = pltpu.get_barrier_semaphore()

        def greet(step, carry):
            pl.semaphore_signal(barrier, inc=1, device_id=(1, lax.rem(dp + step, 64)), device_id_type=MESH)
            return carry

        lax.fori_loop(1, 64, greet, 0)
        pl.semaphore_wait(barrier, 63)

        def start(step, carry):
            copy_of(step).start()
            return carry

        lax.fori_loop(1, 64, start, 0)
        for half in range(2):
            out_ref[half * 64 + dp] = block_ref[half]

        def arrive(step, carry):
            copy_of(step).wait_recv()
            source = lax.rem(dp + 64 - step, 64)
            for half in range(2):
                out_ref[half * 64 + source] = landed[step, half]
            return carry

        lax.fori_loop(1, 64, arrive, 0)

        def finish(step, carry):
            copy_of(step).wait_send()
            return carry

        lax.fori_loop(1, 64, finish, 0)


def gather_blocks(block):
    return pl.pallas_call(
        gather_kernel,
        out_shape=jax.ShapeDtypeStruct((128, 8, 128), jnp.float32),
        in_specs=[pl.BlockSpec(memory_space=pltpu.VMEM)],
        out_specs=pl.BlockSpec(memory_space=pltpu.VMEM),
        scratch_shapes=[
            pltpu.VMEM((64, 2, 8, 128), jnp.float32),
            pltpu.SemaphoreType.DMA((64,)),
            pltpu.SemaphoreType.DMA((64,)),
        ],
        compiler_params=pltpu.CompilerParams(collective_id=1, has_side_effects=True),
        name="gather_quantizer",
    )(block)


def scatter_kernel(
    blocks, out_ref, few_ref, mine, other, land_a, land_b, next_a, next_b, land_c, land_d, last_out, last_in, share, taken,
    local_sem, near_send, near_recv, one_send, one_recv, two_send, two_recv, last_send, last_recv, share_send, share_recv,
):
    pipe = lax.axis_index("pipe")
    dp = lax.axis_index("dp")
    core = lax.rem(dp, 2)
    x = lax.rem(dp // 2, 4)
    z = lax.rem(dp // 8, 2)
    y = dp // 16
    full = slice(None)

    def at(yy, zz, xx, cc):
        return (pipe, ((yy * 2 + zz) * 4 + xx) * 2 + cc)

    def x_after(step):
        return lax.rem(x + step, 4)

    def y_after(step):
        return lax.rem(y + step, 4)

    def remote(source, target, send, recv, device):
        return pltpu.make_async_remote_copy(
            src_ref=source, dst_ref=target, send_sem=send, recv_sem=recv, device_id=device, device_id_type=MESH
        )

    own = pltpu.make_async_copy(blocks.at[:, :, :, core], mine, local_sem)
    own.start()
    barrier = pltpu.get_barrier_semaphore()
    peers = [at(y, z, x, 1 - core), at(y, 1 - z, x, core), (1 - pipe, dp)]
    peers += [at(y, z, x_after(d), core) for d in (1, 2, 3)]
    peers += [at(y_after(d), z, x, core) for d in (1, 2, 3)]
    for peer in peers:
        pl.semaphore_signal(barrier, inc=1, device_id=peer, device_id_type=MESH)
    pl.semaphore_wait(barrier, 9)

    def near_a(d):
        t = x_after(d)
        return remote(
            blocks.at[:, :, t, 1 - core, :, LEFT], other.at[:, :, t, :, LEFT], near_send.at[2 * d], near_recv.at[2 * d],
            at(y, z, x, 1 - core),
        )

    def near_b(d):
        t = y_after(d)
        return remote(
            blocks.at[t, :, :, 1 - core, :, RIGHT], other.at[t, :, :, :, RIGHT], near_send.at[2 * d + 1],
            near_recv.at[2 * d + 1], at(y, z, x, 1 - core),
        )

    def one_a(d):
        return remote(
            mine.at[:, :, x_after(d), :, LEFT], land_a.at[d - 1], one_send.at[2 * d - 2], one_recv.at[2 * d - 2],
            at(y, z, x_after(d), core),
        )

    def one_b(d):
        return remote(
            mine.at[y_after(d), :, :, :, RIGHT], land_b.at[d - 1], one_send.at[2 * d - 1], one_recv.at[2 * d - 1],
            at(y_after(d), z, x, core),
        )

    def two_a(d):
        return remote(
            next_a.at[y_after(d)], land_c.at[d - 1], two_send.at[2 * d - 2], two_recv.at[2 * d - 2],
            at(y_after(d), z, x, core),
        )

    def two_b(d):
        return remote(
            next_b.at[x_after(d)], land_d.at[d - 1], two_send.at[2 * d - 1], two_recv.at[2 * d - 1],
            at(y, z, x_after(d), core),
        )

    order = (2, 1, 3, 0)
    for d in order:
        near_a(d).start()
        near_b(d).start()
    own.wait()

    def wide(ref, *index):
        return ref[index].astype(jnp.float32)

    for d in order[:3]:
        near_a(d).wait_recv()

        def pair_a(i, carry, t=x_after(d)):
            yy, zz = i // 2, lax.rem(i, 2)
            where = (yy, zz, t, full, LEFT)
            mine[where] = (wide(mine, *where) + wide(other, *where)).astype(jnp.bfloat16)
            return carry

        lax.fori_loop(0, 8, pair_a, 0)
        one_a(d).start()
        near_b(d).wait_recv()

        def pair_b(i, carry, t=y_after(d)):
            zz, xx = i // 4, lax.rem(i, 4)
            where = (t, zz, xx, full, RIGHT)
            mine[where] = (wide(mine, *where) + wide(other, *where)).astype(jnp.bfloat16)
            return carry

        lax.fori_loop(0, 8, pair_b, 0)
        one_b(d).start()
    near_a(0).wait_recv()
    near_b(0).wait_recv()
    for d in (1, 3, 2):
        one_a(d).wait_recv()
        one_b(d).wait_recv()

    def sum_a(yy, zz):
        where = (yy, zz, x, full, LEFT)
        total = wide(mine, *where) + wide(other, *where)
        for k in range(3):
            total = total + wide(land_a, k, yy, zz)
        return total

    def sum_b(zz, xx):
        where = (y, zz, xx, full, RIGHT)
        total = wide(mine, *where) + wide(other, *where)
        for k in range(3):
            total = total + wide(land_b, k, zz, xx)
        return total

    for d in order[:3]:
        for zz in range(2):
            next_a[y_after(d), zz] = sum_a(y_after(d), zz).astype(jnp.bfloat16)
        two_a(d).start()
        for zz in range(2):
            next_b[x_after(d), zz] = sum_b(zz, x_after(d)).astype(jnp.bfloat16)
        two_b(d).start()
    away, here = [sum_a(y, 1 - z), sum_b(1 - z, x)], [sum_a(y, z), sum_b(z, x)]
    for d in (1, 3, 2):
        two_a(d).wait_recv()
        two_b(d).wait_recv()
    for k in range(3):
        for part, land in enumerate((land_c, land_d)):
            away[part] = away[part] + wide(land, k, 1 - z)
            here[part] = here[part] + wide(land, k, z)
    last_out[:, LEFT] = away[0].astype(jnp.bfloat16)
    last_out[:, RIGHT] = away[1].astype(jnp.bfloat16)
    last = remote(last_out, last_in, last_send, last_recv, at(y, 1 - z, x, core))
    last.start()
    last.wait_recv()
    out_ref[:, LEFT] = here[0] + wide(last_in, full, LEFT)
    out_ref[:, RIGHT] = here[1] + wide(last_in, full, RIGHT)
    share[...] = out_ref[:, 3072:]
    across = remote(share, taken, share_send, share_recv, (1 - pipe, dp))

    @pl.when(pipe == 1)
    def _():
        across.start()
        few_ref[...] = share[...]
        across.wait_send()

    for d in order:
        near_a(d).wait_send()
        near_b(d).wait_send()
    for d in order[:3]:
        one_a(d).wait_send()
        one_b(d).wait_send()
        two_a(d).wait_send()
        two_b(d).wait_send()
    last.wait_send()

    @pl.when(pipe == 0)
    def _():
        across.wait_recv()
        few_ref[...] = taken[...]


def scatter_blocks(blocks):
    half = (4, 2, 4, 16, WIDE)
    low = jnp.bfloat16
    sems = pltpu.SemaphoreType.DMA
    return pl.pallas_call(
        scatter_kernel,
        out_shape=[
            jax.ShapeDtypeStruct((16, WIDE), jnp.float32),
            jax.ShapeDtypeStruct((16, 128), jnp.float32),
        ],
        in_specs=[pl.BlockSpec(memory_space=pl.ANY)],
        out_specs=[pl.BlockSpec(memory_space=pltpu.VMEM)] * 2,
        scratch_shapes=[
            pltpu.VMEM(half, low),
            pltpu.VMEM(half, low),
            pltpu.VMEM((3, 4, 2, 16, CUT), low),
            pltpu.VMEM((3, 2, 4, 16, WIDE - CUT), low),
            pltpu.VMEM((4, 2, 16, CUT), low),
            pltpu.VMEM((4, 2, 16, WIDE - CUT), low),
            pltpu.VMEM((3, 2, 16, CUT), low),
            pltpu.VMEM((3, 2, 16, WIDE - CUT), low),
            pltpu.VMEM((16, WIDE), low),
            pltpu.VMEM((16, WIDE), low),
            pltpu.VMEM((16, 128), jnp.float32),
            pltpu.VMEM((16, 128), jnp.float32),
            sems, sems((8,)), sems((8,)), sems((6,)), sems((6,)), sems((6,)), sems((6,)), sems, sems, sems, sems,
        ],
        compiler_params=pltpu.CompilerParams(
            collective_id=0, has_side_effects=True, vmem_limit_bytes=60 << 20
        ),
        name="scatter_gradients",
    )(blocks.reshape(4, 2, 4, 2, 16, WIDE))


BF = jnp.bfloat16
F32 = jnp.float32
SCALE = HEAD_DIM**-0.5
PAD = 1152
NN = (((1,), (0,)), ((), ()))
NT = (((1,), (1,)), ((), ()))
TN = (((0,), (0,)), ((), ()))
SPAN = 544
SPANS = SEQ // SPAN
WIDTH = 384
WIDTHS = PAD // WIDTH
COLUMNS = PAD // 128
ANY = pl.BlockSpec(memory_space=pl.ANY)
INSIDE = pl.BlockSpec(memory_space=pltpu.VMEM)
SCALARS = pl.BlockSpec(memory_space=pltpu.SMEM)


def cost(micros):
    return pl.CostEstimate(flops=int(micros * 1.1e9), bytes_accessed=int(micros * 1e6), transcendentals=0)


def dot(left, right, dims=NN):
    return lax.dot_general(left, right, dims, preferred_element_type=F32)


def normal(value):
    center = jnp.mean(value, axis=-1, keepdims=True)
    centred = value - center
    spread = jnp.mean(centred * centred, axis=-1, keepdims=True)
    rate = lax.rsqrt(spread + EPSILON)
    return centred * rate, rate


def normal_back(value, gain, d_normed):
    hat, rate = normal(value)
    scaled = d_normed * gain
    first = jnp.mean(scaled, axis=-1, keepdims=True)
    second = jnp.mean(scaled * hat, axis=-1, keepdims=True)
    terms = d_normed * hat
    return rate * (scaled - first - hat * second), fold_rows(terms), hat


def fold_rows(terms):
    return jnp.sum(terms.reshape(-1, 8, D), axis=0)


def gelu_pair(value):
    square = value * value
    inner = value * (0.7978845608028654 + 0.035677408136300125 * square)
    half = 0.5 + 0.5 * jnp.tanh(inner)
    out = value * half
    slope = half + out * (1.0 - half) * (1.5957691216057308 + 0.21406444881780075 * square)
    return out.astype(BF), slope.astype(BF)


def feed_forward(middle, gain, up, down, act_ref, slope_ref, rows):
    normed = (normal(middle)[0] * gain).astype(BF)
    total = middle
    hidden = dot(normed, up[:, 0:512])
    for j in range(4):
        cols = slice(j * 512, (j + 1) * 512)
        after = dot(normed, up[:, cols.stop : cols.stop + 512]) if j < 3 else None
        act, slope = gelu_pair(hidden)
        act_ref[rows, cols] = act
        slope_ref[rows, cols] = slope
        total = total + dot(act, down[cols, :])
        hidden = after
    return normed, total


def lane_is_low(shape):
    return lax.rem(lax.broadcasted_iota(jnp.int32, shape, len(shape) - 1), 128) < 64


def head_mask(shape):
    lane = lax.broadcasted_iota(jnp.int32, shape, 1)
    return [(lane >= 64 * h) & (lane < 64 * h + 64) for h in range(4)]


def spread_heads(value, masks):
    zero = jnp.zeros_like(value)
    return jnp.concatenate([jnp.where(m, value, zero) for m in masks], axis=0)


def fold_heads(value, masks):
    total = jnp.where(masks[0], value[:64], 0.0)
    for h in range(1, 4):
        total = total + jnp.where(masks[h], value[64 * h : 64 * h + 64], 0.0)
    return total


def head_blocks():
    row = lax.broadcasted_iota(jnp.int32, (256, 256), 0)
    lane = lax.broadcasted_iota(jnp.int32, (256, 256), 1)
    return (lax.div(row, 64) == lax.div(lane, 64)).astype(BF)


def frame_groups(frames=FRAMES):
    for f in range(frames):
        for g in range(2):
            yield slice(f * 64, f * 64 + 64), g * 256


def window_forward(frames, mixed, scores, probs, context):
    masks = head_mask((64, 256))
    slab = frames * 64 // (8 if frames == FRAMES else 4)
    for rows, at in frame_groups(frames):
        keys = spread_heads(mixed[rows, 512 + at : 768 + at], masks)
        scores[rows, at : at + 256] = dot(mixed[rows, at : at + 256], keys, NT)
    low = lane_is_low((slab, 128))

    def soften(i):
        rows = row_span(i, slab)
        for c in range(4):
            cols = slice(c * 128, c * 128 + 128)
            piece = scores[rows, cols]
            left = jnp.max(jnp.where(low, piece, -jnp.inf), axis=1, keepdims=True)
            right = jnp.max(jnp.where(low, -jnp.inf, piece), axis=1, keepdims=True)
            scores[rows, cols] = jnp.exp((piece - jnp.where(low, left, right)) * SCALE)

    loop(frames * 64 // slab, soften)
    ones = head_blocks()
    for rows, at in frame_groups(frames):
        cols = slice(at, at + 256)
        power = scores[rows, cols].astype(BF)
        inverse = 1.0 / dot(power, ones)
        values = spread_heads(mixed[rows, 1024 + at : 1280 + at], masks)
        context[rows, cols] = (dot(power, values) * inverse).astype(BF)
        probs[rows, cols] = (power.astype(F32) * inverse).astype(BF)


def window_backward(mixed, probs, d_context, d_probs, d_scores, d_mixed):
    masks = head_mask((64, 256))
    for rows, at in frame_groups():
        cols = slice(at, at + 256)
        values = spread_heads(mixed[rows, 1024 + at : 1280 + at], masks)
        d_probs[rows, cols] = dot(d_context[rows, cols], values, NT)
    ones = head_blocks()

    def soften(i):
        rows = row_span(i, SPAN)
        for g in range(2):
            cols = slice(g * 256, g * 256 + 256)
            wide = probs[rows, cols].astype(F32)
            here = d_probs[rows, cols]
            delta = dot((wide * here).astype(BF), ones)
            d_scores[rows, cols] = (wide * (here - delta) * SCALE).astype(BF)

    loop(SPANS, soften)
    for rows, at in frame_groups():
        cols = slice(at, at + 256)
        here = d_scores[rows, cols]
        keys = spread_heads(mixed[rows, 512 + at : 768 + at], masks)
        d_mixed[rows, at : at + 256] = dot(here, keys).astype(BF)
        d_keys = fold_heads(dot(here, mixed[rows, at : at + 256], TN), masks)
        d_mixed[rows, 512 + at : 768 + at] = d_keys.astype(BF)
        d_values = fold_heads(dot(probs[rows, cols], d_context[rows, cols], TN), masks)
        d_mixed[rows, 1024 + at : 1280 + at] = d_values.astype(BF)


def loop(count, body):
    def step(index, carry):
        body(index)
        return carry

    lax.fori_loop(0, count, step, 0)


def row_span(index, size):
    return pl.ds(pl.multiple_of(index * size, 16), size)


def valid_rows(start, size, count):
    row = lax.broadcasted_iota(jnp.int32, (size, 1), 0) + start
    return row < count * PATCHES


def first_forward_kernel(micro, begin, amount, *refs):
    (active, frames, video, w_attn, w_up, w_down, gains) = refs[:7]
    (acts, sent, s_mixed, s_context, s_probs, s_middle, s_act, s_slope) = refs[-21:-13]
    (x, attn, up, down, mixed, context, probs, middle, act, slope, out, masked, sems) = refs[-13:]
    start, size = begin * PATCHES, amount * PATCHES
    span = size // 2

    @pl.when(active[0] == 1)
    def _():
        count = frames[micro, 0]
        loads = [
            pltpu.make_async_copy(video.at[micro, 0, pl.ds(start, size)], x, sems.at[0]),
            pltpu.make_async_copy(w_attn, attn, sems.at[1]),
            pltpu.make_async_copy(w_up, up, sems.at[2]),
            pltpu.make_async_copy(w_down, down, sems.at[3]),
        ]
        for copy in loads:
            copy.start()
        loads[0].wait()
        loads[1].wait()

        def project(i):
            rows = row_span(i, span)
            hat, _ = normal(x[rows, :].astype(F32))
            normed = (hat * gains[0:1, :]).astype(BF)
            for j in range(3):
                cols = slice(j * 512, (j + 1) * 512)
                mixed[rows, cols] = dot(normed, attn[:, cols]).astype(BF)

        loop(2, project)
        stores = [pltpu.make_async_copy(mixed, s_mixed, sems.at[4])]
        stores[0].start()
        window_forward(amount, mixed, middle, probs, context)
        for k, (source, target) in enumerate(((context, s_context), (probs, s_probs))):
            stores.append(pltpu.make_async_copy(source, target, sems.at[5 + k]))
            stores[-1].start()
        loads[2].wait()
        loads[3].wait()
        real = acts.at[micro, pl.ds(start, size)]
        late = ((out, sent), (masked, real), (middle, s_middle), (act, s_act), (slope, s_slope))

        def late_stores(i):
            rows = row_span(i, span)
            return [
                pltpu.make_async_copy(source.at[rows], target.at[rows], sems.at[7 + k * 2 + i])
                for k, (source, target) in enumerate(late)
            ]

        def tail(i):
            rows = row_span(i, span)
            here = x[rows, :].astype(F32) + dot(context[rows, :], attn[:, 1536:])
            middle[rows, :] = here
            _, total = feed_forward(here, gains[1:2, :], up, down, act, slope, rows)
            out[rows, :] = total.astype(BF)
            masked[rows, :] = jnp.where(valid_rows(start + i * span, span, count), total, 0.0).astype(BF)
            for copy in late_stores(i):
                copy.start()

        loop(2, tail)

        def settle(i):
            for copy in late_stores(i):
                copy.wait()

        loop(2, settle)
        for copy in stores:
            copy.wait()


def saved_shapes(size=SEQ):
    return [
        jax.ShapeDtypeStruct((size, 3 * D), BF),
        jax.ShapeDtypeStruct((size, D), BF),
        jax.ShapeDtypeStruct((size, D), BF),
        jax.ShapeDtypeStruct((size, D), F32),
        jax.ShapeDtypeStruct((size, FF), BF),
        jax.ShapeDtypeStruct((size, FF), BF),
    ]


def weight_scratch():
    return [pltpu.VMEM((D, 4 * D), BF), pltpu.VMEM((D, FF), BF), pltpu.VMEM((FF, D), BF)]


def first_forward(micro, active, frames, video, weights, acts=None, begin=0, amount=FRAMES):
    size = amount * PATCHES
    saved = saved_shapes(size)
    inputs = [active, frames, video, *weights] + ([] if acts is None else [acts])
    tokens = pltpu.VMEM((size, D), BF)
    result = pl.pallas_call(
        functools.partial(first_forward_kernel, micro, begin, amount),
        out_shape=[jax.ShapeDtypeStruct((2, SEQ, D), BF), jax.ShapeDtypeStruct((size, D), BF)] + saved,
        in_specs=([SCALARS, SCALARS, ANY, ANY, ANY, ANY, INSIDE, ANY])[: len(inputs)],
        out_specs=[ANY] * 8,
        input_output_aliases={} if acts is None else {7: 0},
        scratch_shapes=[tokens] + weight_scratch() + [pltpu.VMEM(s.shape, s.dtype) for s in saved]
        + [tokens, tokens, pltpu.SemaphoreType.DMA((17,))],
        compiler_params=pltpu.CompilerParams(vmem_limit_bytes=60 << 20),
        cost_estimate=cost(22 * amount // FRAMES),
        name=f"first_forward_{micro}_{begin}",
    )(*inputs)
    return result[0], result[1], result[2:]


def lanes_at(start, size=512):
    return pl.ds(pl.multiple_of(start, 128), size)


def put_wide(blocks, old, at, left, right):
    lanes = lanes_at(at)
    value = jnp.concatenate([left.reshape(64, 8, 512), right.reshape(64, 8, 512)], axis=1)
    if old is not None:
        value = value + old[:, :, lanes].astype(F32)
    blocks[:, :, lanes] = value.astype(BF)


def put_tall(blocks, old, part, value):
    value = value.reshape(16, 2, 16, 512)
    into = pl.ds(part * 16, 16)
    for half in range(2):
        lanes = slice(2048 + half * 512, 2560 + half * 512)
        piece = value[:, half]
        if old is not None:
            piece = piece + old[into, :, lanes].astype(F32)
        blocks[into, :, lanes] = piece.astype(BF)


def send_lanes(source, target, at, size, sem):
    lanes = pl.ds(at, size)
    copy = pltpu.make_async_copy(source.at[:, :, lanes], target.at[:, :, lanes], sem)
    copy.start()
    return copy


def spread_gains(sums, few):
    dst = lax.broadcasted_iota(jnp.int32, (64, D), 0)
    lane = lax.broadcasted_iota(jnp.int32, (64, D), 1)
    source = lax.broadcasted_iota(jnp.int32, (D, 128), 0)
    place = lax.broadcasted_iota(jnp.int32, (D, 128), 1)
    total = jnp.zeros((64, 128), F32)
    for k in range(2):
        row = jnp.sum(sums[8 * k : 8 * k + 8, :], axis=0, keepdims=True)
        mine = jnp.where(lane // 8 == dst, row, 0.0)
        pick = (lax.rem(source, 8) + 8 * k == place).astype(F32)
        total = total + lax.dot_general(mine, pick, NN, precision=lax.Precision.HIGHEST, preferred_element_type=F32)
    few[:, 8, :] = total


def first_backward_kernel(micro, fresh, cuts, *refs):
    parts = len(cuts)
    (active, video, w_attn, w_up, w_down, gains, d_in) = refs[:7]
    saved = [refs[7 + 6 * p : 13 + 6 * p] for p in range(parts)]
    rest = refs[7 + 6 * parts :]
    if fresh:
        _, grad_in, blocks, new_gains = rest[:4]
    else:
        _, _, old_blocks, old_gains, grad_in, blocks = rest[:6]
    (x, attn, up, down, mixed, context, probs, middle, act, slope, d_two, normed, d_branch, d_mid, d_context,
     g_out, g_gains, more_gains, few, block_out, block_old, sems) = refs[-22:]
    old = None if fresh else block_old

    @pl.when(active[0] == 1)
    def _():
        loads = {}

        def load(name, source, target):
            copy = pltpu.make_async_copy(source, target, sems.at[18 + sum(len(c) for c in loads.values())])
            copy.start()
            loads.setdefault(name, []).append(copy)

        def need(*names):
            for name in names:
                for copy in loads[name]:
                    copy.wait()

        def load_saved(name, k, target, start, size):
            for p, (first, amount) in enumerate(cuts):
                low, high = max(start, first), min(start + size, first + amount)
                if low < high:
                    load(name, saved[p][k].at[pl.ds(low - first, high - low)], target.at[pl.ds(low, high - low)])

        load("d_in", d_in, d_two)
        load("down", w_down, down)
        load_saved("slope0", 5, slope, 0, SPAN)
        load("up", w_up, up)
        load_saved("middle0", 3, middle, 0, SPAN)
        load_saved("slope1", 5, slope, SPAN, SPAN)
        load_saved("middle1", 3, middle, SPAN, SPAN)
        load_saved("act", 4, act, 0, SEQ)
        if not fresh:
            load("old", old_blocks, block_old)
            load("old", old_gains, more_gains)
        load("attn", w_attn, attn)
        load_saved("context", 1, context, 0, SEQ)
        load_saved("probs", 2, probs, 0, SEQ)
        load_saved("mixed", 0, mixed, 0, SEQ)
        load("x", video.at[micro, 0], x)
        g_gains[...] = jnp.zeros_like(g_gains)
        gain = gains[1:2, :]
        need("d_in", "down")
        for i in range(SPANS):
            rows = slice(i * SPAN, (i + 1) * SPAN)
            d_low = d_two[rows, :]
            total = jnp.zeros((SPAN, D), F32)
            d_act = dot(d_low, down[0:512, :], NT)
            need(f"slope{i}")
            for j in range(4):
                cols = slice(j * 512, (j + 1) * 512)
                after = dot(d_low, down[cols.stop : cols.stop + 512, :], NT) if j < 3 else None
                d_hidden = (d_act * slope[rows, cols].astype(F32)).astype(BF)
                slope[rows, cols] = d_hidden
                if i + j == 0:
                    need("up")
                total = total + dot(d_hidden, up[:, cols], NT)
                d_act = after
            need(f"middle{i}")
            here = middle[rows, :]
            d_here, g_rows, hat = normal_back(here, gain, total)
            g_gains[8:16, :] += g_rows
            normed[rows, :] = (hat * gain).astype(BF)
            d_here = d_low.astype(F32) + d_here
            d_mid[rows, :] = d_here
            d_branch[rows, :] = d_here.astype(BF)
        need("act")
        if not fresh:
            need("old")
        loop(4, lambda j: put_tall(block_out, old, j, dot(act[:, lanes_at(j * 512)], d_two[...], TN)))
        stores = [send_lanes(block_out, blocks, 2048, 1024, sems.at[13])]

        def put_up(j):
            left, right = slope[:, lanes_at(j * 512)], slope[:, lanes_at(1024 + j * 512)]
            put_wide(block_out, old, 1024 + j * 512, dot(normed[...], left, TN), dot(normed[...], right, TN))

        loop(2, put_up)
        stores.append(send_lanes(block_out, blocks, 1024, 1024, sems.at[14]))
        need("attn", "context", "probs", "mixed", "x")
        g_out[...] = dot(context[...], d_branch[...], TN)

        def into_context(i):
            rows = row_span(i, SPAN)
            d_context[rows, :] = dot(d_branch[rows, :], attn[:, 1536:], NT).astype(BF)

        loop(SPANS, into_context)
        d_mixed = act
        window_backward(mixed, probs, d_context, middle, normed, d_mixed)
        gain_one = gains[0:1, :]

        def head(i):
            rows = row_span(i, SPAN)
            total = jnp.zeros((SPAN, D), F32)
            for j in range(3):
                cols = slice(j * 512, (j + 1) * 512)
                total = total + dot(d_mixed[rows, cols], attn[:, cols], NT)
            d_here, g_rows, hat = normal_back(x[rows, :].astype(F32), gain_one, total)
            g_gains[0:8, :] += g_rows
            normed[rows, :] = (hat * gain_one).astype(BF)
            d_branch[rows, :] = (d_mid[rows, :] + d_here).astype(BF)

        loop(SPANS, head)
        stores.append(pltpu.make_async_copy(d_branch, grad_in.at[micro], sems.at[15]))
        stores[-1].start()
        if fresh:
            stores.append(pltpu.make_async_copy(g_gains, new_gains, sems.at[16]))
            stores[-1].start()
        else:
            few[...] = jnp.zeros_like(few)
            spread_gains(g_gains[...] + more_gains[...], few)
            block_out[:, :, 3072:] = few[...].astype(BF)
        put_wide(
            block_out, old, 0, dot(normed[...], d_mixed[:, :512], TN), dot(normed[...], d_mixed[:, 1024:1536], TN)
        )
        put_wide(block_out, old, 512, dot(normed[...], d_mixed[:, 512:1024], TN), g_out[...])
        stores.append(send_lanes(block_out, blocks, 0, 1024, sems.at[17]))
        if not fresh:
            stores.append(send_lanes(block_out, blocks, 3072, 128, sems.at[16]))
        for copy in stores:
            copy.wait()


BLOCKS = jax.ShapeDtypeStruct((64, 16, WIDE), BF)
GAINS = jax.ShapeDtypeStruct((16, D), F32)


def first_backward(micro, active, video, weights, d_in, cuts, saved, grad_in, blocks=None, before=None):
    kept = saved_shapes()
    rows = pltpu.VMEM((SEQ, D), BF)
    fresh = before is None
    inputs = [active, video, *weights, d_in, *saved, grad_in]
    outputs = [jax.ShapeDtypeStruct(grad_in.shape, BF), BLOCKS]
    place = len(inputs) - 1
    aliases = {place: 0}
    if fresh:
        outputs += [GAINS]
    else:
        inputs += [blocks, *before]
        aliases = {place: 0, place + 1: 1}
    sums = pltpu.VMEM((16, D), F32)
    result = pl.pallas_call(
        functools.partial(first_backward_kernel, micro, fresh, cuts),
        out_shape=outputs,
        in_specs=[SCALARS, ANY, ANY, ANY, ANY, INSIDE] + [ANY] * (len(inputs) - 6),
        out_specs=[ANY] * len(outputs),
        input_output_aliases=aliases,
        scratch_shapes=[rows] + weight_scratch() + [pltpu.VMEM(s.shape, s.dtype) for s in kept]
        + [rows, rows, rows, pltpu.VMEM((SEQ, D), F32), rows, pltpu.VMEM((D, D), F32), sums, sums]
        + [pltpu.VMEM((64, 16, 128), F32), pltpu.VMEM((64, 16, WIDE), BF), pltpu.VMEM((64, 16, WIDE), BF)]
        + [pltpu.SemaphoreType.DMA((44,))],
        compiler_params=pltpu.CompilerParams(vmem_limit_bytes=127 << 19),
        cost_estimate=cost(32),
        name=f"first_backward_{micro}",
    )(*inputs)
    return result[0], *result[1:]


TALL = 1152
AHEAD = 3
BEHIND = 1


def column(index):
    return slice(index * 128, index * 128 + 128)


def load_head(head, mixed, refs, scale):
    for part, (ref, turned) in enumerate(refs):
        rows = pl.ds(pl.multiple_of(part * D + head * HEAD_DIM, HEAD_DIM), HEAD_DIM)
        for c in range(COLUMNS):
            value = mixed[rows, column(c)].astype(F32)
            if part == 0 and scale:
                value = value * SCALE
            ref[:, column(c)] = value
            if turned is not None:
                turned[:, column(c)] = pltpu.roll(value, 64, 1)


def column_sets(size):
    first = COLUMNS % size
    sets = [list(range(first))] if first else []
    return sets + [list(range(i, i + size)) for i in range(first, COLUMNS, size)]


def pair_rows(lefts, refs, rows_refs):
    for s, ref in enumerate(refs):
        for b in range(max(lefts) + 1):
            right = ref[:, column(b)]
            for i, (a, left) in enumerate(lefts.items()):
                if b <= a:
                    rows_refs[i, 9 * s + b : 9 * s + b + 1, :] = jnp.sum(left * right, axis=0, keepdims=True)


def weighted(rows_of, refs, columns):
    totals = {a: None for a in columns}
    for s, ref in enumerate(refs):
        for b in range(max(columns) + 1):
            right = ref[:, column(b)]
            for a in columns:
                if b <= a:
                    term = rows_of(a, 9 * s + b) * right
                    totals[a] = term if totals[a] is None else totals[a] + term
    return totals


def temporal_head(head, order, mixed, probs, context, q, k, v, kt, vt, rows_ref):
    load_head(head, mixed, ((q, None), (k, kt), (v, vt)), True)
    out_rows = pl.ds(pl.multiple_of(head * HEAD_DIM, HEAD_DIM), HEAD_DIM)
    for columns in column_sets(AHEAD):
        pair_rows({a: q[:, column(a)] for a in columns}, (k, kt), rows_ref)
        for i, a in enumerate(columns):
            scores = jnp.where(order[...] <= 2 * a, rows_ref[i], MASKED)
            power = jnp.exp(scores - jnp.max(scores, axis=0, keepdims=True))
            probs[head, a] = power / jnp.sum(power, axis=0, keepdims=True)
        totals = weighted(lambda a, r: probs[head, a, r : r + 1, :], (v, vt), columns)
        for a in columns:
            context[out_rows, column(a)] = totals[a].astype(BF)


def temporal_head_back(head, mixed, probs, d_context, q, k, v, kt, vt, dc, rows_ref, ds):
    load_head(head, mixed, ((q, None), (k, kt), (v, vt)), False)
    in_rows = pl.ds(pl.multiple_of(head * HEAD_DIM, HEAD_DIM), HEAD_DIM)
    for c in range(COLUMNS):
        dc[:, column(c)] = d_context[in_rows, column(c)].astype(F32)
    for columns in column_sets(AHEAD):
        pair_rows({a: dc[:, column(a)] for a in columns}, (v, vt), rows_ref)
        for i, a in enumerate(columns):
            p = probs[head, a]
            d_probs = jnp.where(p > 0.0, rows_ref[i], 0.0)
            delta = jnp.sum(d_probs * p, axis=0, keepdims=True)
            ds[a] = p * (d_probs - delta) * SCALE
        totals = weighted(lambda a, r: ds[a, r : r + 1, :], (k, kt), columns)
        for a in columns:
            mixed[in_rows, column(a)] = totals[a].astype(BF)
    for part, (weight, source) in enumerate(
        ((lambda a, r: ds[a, r : r + 1, :], q), (lambda a, r: probs[head, a, r : r + 1, :], dc))
    ):
        rows = pl.ds(pl.multiple_of((part + 1) * D + head * HEAD_DIM, HEAD_DIM), HEAD_DIM)
        for columns in column_sets(BEHIND):
            sums = {}
            for a in range(min(columns), COLUMNS):
                value = source[:, column(a)]
                for b in columns:
                    if b <= a:
                        for s in range(2):
                            term = weight(a, 9 * s + b) * value
                            sums[b, s] = sums[b, s] + term if (b, s) in sums else term
            for b in columns:
                mixed[rows, column(b)] = (sums[b, 0] + pltpu.roll(sums[b, 1], 64, 1)).astype(BF)


def frame_order(count):
    row = lax.broadcasted_iota(jnp.int32, (24, 128), 0)
    high = (lax.broadcasted_iota(jnp.int32, (24, 128), 1) >= 64).astype(jnp.int32)
    turned = row >= 9
    base = 2 * jnp.where(turned, row - 9, row)
    key_frame = base + jnp.where(turned, 1 - high, high)
    return jnp.where((row < 18) & (key_frame < count), key_frame - high, 1000)


def second_kernel(micro, fresh, cuts, *refs):
    pieces, refs = refs[: len(cuts)], refs[len(cuts) :]
    (active, frames, w_attn, w_turned, w_up, w_down, gains, cot_h, cot_q, codes, quant) = refs[:11]
    if fresh:
        _, acts, grad_in, sent_back = refs[11:15]
        old = []
    else:
        _, _, *old = refs[11:16]
        acts, grad_in, sent_back = refs[16:19]
    (s_act, s_hidden, s_normed, s_two, s_d_two, s_branch, s_context, s_mixed, new_gains, new_proj, new_code) = refs[-48:-37]
    (x, attn_out, turned, up, down, normed, normed_two, mixed, context, d_context, probs, middle, act, slope, out,
     masked, d_mid, d_two, cot, cot_codes, code_rows, table, proj_wide, proj, g_gains, g_proj, g_code,
     q, k, v, kt, vt, dc, rows_ref, ds, order, sems) = refs[-37:]

    @pl.when(active[0] == 1)
    def _():
        count = frames[micro, 0]
        real = pl.ds(0, SEQ)
        pairs = [(piece, x.at[pl.ds(*cut)]) for piece, cut in zip(pieces, cuts)]
        pairs += [
            (w_turned, turned), (w_attn.at[:, pl.ds(1536, 512)], attn_out), (w_up, up),
            (w_down, down), (codes.at[micro], code_rows.at[real]), (cot_q.at[micro], cot_codes.at[real]),
            (cot_h.at[micro, 0], cot.at[real]),
        ]
        pairs += list(zip(old, (g_gains, g_proj, g_code)))
        loads = [pltpu.make_async_copy(s, t, sems.at[i]) for i, (s, t) in enumerate(pairs)]
        for copy in loads:
            copy.start()
        stores = []

        def save(source, target):
            stores.append(pltpu.make_async_copy(source, target, sems.at[12 + len(stores)]))
            stores[-1].start()

        tail_rows = pl.ds(SEQ, PAD - SEQ)
        x[tail_rows, :] = jnp.zeros((PAD - SEQ, D), BF)
        cot[tail_rows, :] = jnp.zeros((PAD - SEQ, D), BF)
        cot_codes[tail_rows, :] = jnp.zeros((PAD - SEQ, 128), BF)
        code_rows[tail_rows, :] = jnp.zeros((PAD - SEQ, 128), jnp.int32)
        rows_ref[...] = jnp.zeros_like(rows_ref)
        order[...] = frame_order(count)
        if fresh:
            g_gains[...] = jnp.zeros_like(g_gains)
            g_proj[...] = jnp.zeros_like(g_proj)
            g_code[...] = jnp.zeros_like(g_code)
        for j in range(4):
            table[:, column(j)] = quant[:, j, :].astype(BF)
            proj_wide[pl.ds(j, 128, stride=4), :] = quant[:, 4 + j, :]
        proj[...] = proj_wide[...].astype(BF)
        gain_one, gain_two = gains[0:1, :], gains[1:2, :]
        for copy in loads[: len(cuts) + 1]:
            copy.wait()

        def project(i):
            rows, lanes = row_span(i, WIDTH), lanes_at(i * WIDTH, WIDTH)
            normed[rows, :] = (normal(x[rows, :].astype(F32))[0] * gain_one).astype(BF)
            for j in range(3):
                parts = slice(j * 512, (j + 1) * 512)
                mixed[parts, lanes] = dot(turned[parts, :], normed[rows, :], NT).astype(BF)

        loop(WIDTHS, project)
        save(normed, s_normed)
        loop(HEADS, lambda h: temporal_head(h, order, mixed, probs, context, q, k, v, kt, vt, rows_ref))
        save(context, s_context)
        for copy in loads[len(cuts) + 1 :]:
            copy.wait()

        def into_middle(i):
            rows = row_span(i, WIDTH)
            middle[rows, :] = x[rows, :].astype(F32) + dot(context[:, lanes_at(i * WIDTH, WIDTH)], attn_out[...], TN)

        loop(WIDTHS, into_middle)

        def forward_tail(i):
            rows = row_span(i, TALL)
            here = middle[rows, :]
            normed_low, total = feed_forward(here, gain_two, up, down, act, slope, rows)
            normed_two[rows, :] = normed_low
            valid = valid_rows(i * TALL, TALL, count)
            low = total.astype(BF)
            out[rows, :] = low
            masked[rows, :] = jnp.where(valid, total, 0.0).astype(BF)
            mask = valid.astype(F32)
            latent = dot(low, proj[...])
            code = code_rows[rows, :]
            lane = lax.broadcasted_iota(jnp.int32, (TALL, 128), 1)
            high = (lax.div(code, LOW_CODES) == lane).astype(BF)
            near = dot(high, table[...])
            spot = lax.rem(code, LOW_CODES) == lax.rem(lane, LOW_CODES)
            spots = jnp.concatenate([spot] * 4, axis=1)
            place = lax.div(lax.broadcasted_iota(jnp.int32, (512, 128), 0), LOW_CODES)
            pick = (place == lax.broadcasted_iota(jnp.int32, (512, 128), 1)).astype(BF)
            chosen = dot(jnp.where(spots, near, 0.0).astype(BF), pick)
            d_latent = (mask * (cot_codes[rows, :].astype(F32) + 2.0 * BETA * (latent - chosen))).astype(BF)
            d_chosen = (2.0 * mask * (chosen - latent)).astype(BF)
            g_proj[...] += dot(low, d_latent, TN)
            spread = jnp.where(spots, dot(d_chosen, pick, NT), 0.0).astype(BF)
            g_code[...] += dot(high, spread, TN)
            d_out = cot[rows, :].astype(F32) * mask + dot(d_latent, proj[...], NT)
            d_two[rows, :] = d_out.astype(BF)
            d_mid[rows, :] = d_out

        loop(PAD // TALL, forward_tail)
        save(masked.at[real], acts.at[micro])
        save(act, s_act)
        save(normed_two, s_two)
        save(d_two, s_d_two)
        save(g_proj, new_proj)
        save(g_code, new_code)
        d_branch = out

        def backward_tail(i):
            rows = row_span(i, TALL)
            d_low = d_two[rows, :]
            total = jnp.zeros((TALL, D), F32)
            d_act = dot(d_low, down[0:512, :], NT)
            for j in range(4):
                cols = slice(j * 512, (j + 1) * 512)
                after = dot(d_low, down[cols.stop : cols.stop + 512, :], NT) if j < 3 else None
                d_hidden = (d_act * slope[rows, cols].astype(F32)).astype(BF)
                slope[rows, cols] = d_hidden
                total = total + dot(d_hidden, up[:, cols], NT)
                d_act = after
            d_here, g_rows, _ = normal_back(middle[rows, :], gain_two, total)
            g_gains[8:16, :] += g_rows
            d_here = d_mid[rows, :] + d_here
            d_mid[rows, :] = d_here
            d_branch[rows, :] = d_here.astype(BF)

        loop(PAD // TALL, backward_tail)
        save(slope, s_hidden)
        save(d_branch, s_branch)

        def into_context(i):
            lanes = lanes_at(i * WIDTH, WIDTH)
            d_context[:, lanes] = dot(attn_out[...], d_branch[row_span(i, WIDTH), :], NT).astype(BF)

        loop(WIDTHS, into_context)
        loop(
            HEADS,
            lambda h: temporal_head_back(h, mixed, probs, d_context, q, k, v, kt, vt, dc, rows_ref, ds),
        )
        save(mixed, s_mixed)
        d_x = cot

        def finish(i):
            rows = row_span(i, WIDTH)
            total = dot(mixed[:, lanes_at(i * WIDTH, WIDTH)], turned[...], TN)
            d_here, g_rows, _ = normal_back(x[rows, :].astype(F32), gain_one, total)
            g_gains[0:8, :] += g_rows
            d_x[rows, :] = (d_mid[rows, :] + d_here).astype(BF)

        loop(WIDTHS, finish)
        save(d_x.at[real], sent_back)
        save(d_x.at[real], grad_in.at[micro])
        save(g_gains, new_gains)
        for copy in stores:
            copy.wait()


TOKENS = jax.ShapeDtypeStruct((PAD, D), BF)
HIDDEN = jax.ShapeDtypeStruct((PAD, FF), BF)
KEPT = [
    HIDDEN, HIDDEN, TOKENS, TOKENS, TOKENS, TOKENS,
    jax.ShapeDtypeStruct((D, PAD), BF), jax.ShapeDtypeStruct((3 * D, PAD), BF),
]
SMALL = [
    GAINS,
    jax.ShapeDtypeStruct((D, 128), F32),
    jax.ShapeDtypeStruct((128, 512), F32),
]


def second_section(micro, active, frames, cuts, received, weights, cots, acts, grad_in=None, small=None):
    fresh = small is None
    inputs = [*received, active, frames, *weights, *cots, acts]
    place = len(inputs) - 1
    outputs = [
        jax.ShapeDtypeStruct(acts.shape, BF),
        jax.ShapeDtypeStruct(acts.shape, BF),
        jax.ShapeDtypeStruct((SEQ, D), BF),
    ] + KEPT + SMALL
    aliases = {place: 0}
    if not fresh:
        inputs += [grad_in, *small]
        aliases = {place: 0, place + 1: 1}
    tokens = pltpu.VMEM((PAD, D), BF)
    tokens_wide = pltpu.VMEM((PAD, D), F32)
    flipped = pltpu.VMEM((D, PAD), BF)
    hidden = pltpu.VMEM((PAD, FF), BF)
    one_head = pltpu.VMEM((HEAD_DIM, PAD), F32)
    scratch = [
        tokens, pltpu.VMEM((D, D), BF), pltpu.VMEM((3 * D, D), BF), pltpu.VMEM((D, FF), BF), pltpu.VMEM((FF, D), BF),
        tokens, tokens, pltpu.VMEM((3 * D, PAD), BF), flipped, flipped, pltpu.VMEM((HEADS, COLUMNS, 24, 128), F32),
        tokens_wide, hidden, hidden, tokens, tokens, tokens_wide, tokens, tokens, pltpu.VMEM((PAD, 128), BF),
        pltpu.VMEM((PAD, 128), jnp.int32), pltpu.VMEM((128, 512), BF), pltpu.VMEM((D, 128), F32),
        pltpu.VMEM((D, 128), BF),
    ]
    scratch += [pltpu.VMEM(s.shape, s.dtype) for s in SMALL] + [one_head] * 6 + [
        pltpu.VMEM((AHEAD, 24, 128), F32), pltpu.VMEM((COLUMNS, 24, 128), F32), pltpu.VMEM((24, 128), jnp.int32),
        pltpu.SemaphoreType.DMA((30,)),
    ]
    specs = [ANY] * len(cuts) + [SCALARS, SCALARS, ANY, ANY, ANY, ANY, INSIDE, ANY, ANY, ANY, INSIDE]
    result = pl.pallas_call(
        functools.partial(second_kernel, micro, fresh, cuts),
        out_shape=outputs,
        in_specs=specs + [ANY] * (len(inputs) - len(specs)),
        out_specs=[ANY] * len(outputs),
        input_output_aliases=aliases,
        scratch_shapes=scratch,
        compiler_params=pltpu.CompilerParams(vmem_limit_bytes=127 << 19),
        cost_estimate=cost(44),
        name=f"second_section_{micro}",
    )(*inputs)
    return result[0], result[1], result[2], result[3:11], result[11:]


def second_grads_kernel(active, *refs):
    kept = (refs[:8], refs[8:16])
    s_gains, s_proj, s_code, blocks = refs[16:20]
    (act, hidden, normed, normed_two, d_two, d_branch, context, mixed, g_gains, g_proj, g_code, few, block_out, sems) = refs[20:]
    held = (act, hidden, normed, normed_two, d_two, d_branch, context, mixed)

    @pl.when(active[0] == 1)
    def _():
        loads = {}
        for k in (0, 4, 1, 3, 6, 5, 7, 2):
            for m in range(2):
                at = pl.ds(m * PAD, PAD)
                into = held[k].at[:, at] if k >= 6 else held[k].at[at]
                loads[k, m] = pltpu.make_async_copy(kept[m][k], into, sems.at[2 * k + m])
                loads[k, m].start()
        tiny = [
            pltpu.make_async_copy(s, t, sems.at[16 + i])
            for i, (s, t) in enumerate(((s_gains, g_gains), (s_proj, g_proj), (s_code, g_code)))
        ]
        for copy in tiny:
            copy.start()

        def need(*keys):
            for k in keys:
                for m in range(2):
                    loads[k, m].wait()

        need(0, 4)
        for j in range(4):
            put_tall(block_out, None, j, dot(act[:, j * 512 : j * 512 + 512], d_two[...], TN))
        stores = [send_lanes(block_out, blocks, 2048, 1024, sems.at[19])]
        need(1, 3)
        for j in range(2):
            left, right = hidden[:, j * 512 : j * 512 + 512], hidden[:, 1024 + j * 512 : 1536 + j * 512]
            put_wide(
                block_out, None, 1024 + j * 512, dot(normed_two[...], left, TN), dot(normed_two[...], right, TN)
            )
        stores.append(send_lanes(block_out, blocks, 1024, 1024, sems.at[20]))
        need(6, 5, 7, 2)
        parts = [dot(mixed[j * 512 : j * 512 + 512, :], normed[...]).T for j in range(3)]
        put_wide(block_out, None, 0, parts[0], parts[2])
        put_wide(block_out, None, 512, parts[1], dot(context[...], d_branch[...]))
        stores.append(send_lanes(block_out, blocks, 0, 1024, sems.at[21]))
        for copy in tiny:
            copy.wait()
        few[...] = jnp.zeros_like(few)
        spread_gains(g_gains[...], few)
        for j in range(4):
            few[:, j, :] = g_code[0:64, column(j)]
            few[:, 4 + j, :] = g_code[64:128, column(j)]
        for j in range(4):
            first = g_proj[pl.ds(j, 64, stride=4), :]
            second = g_proj[pl.ds(256 + j, 64, stride=4), :]
            few[:, 9 + j, :] = first + pltpu.roll(second, 64, 1)
        block_out[:, :, 3072:] = few[...].astype(BF)
        stores.append(send_lanes(block_out, blocks, 3072, 128, sems.at[22]))
        for copy in stores:
            copy.wait()


def second_grads(active, kept_0, kept_1, small):
    twice = [
        pltpu.VMEM((s.shape[0], 2 * PAD) if s.shape[1] == PAD else (2 * PAD, s.shape[1]), BF) for s in KEPT
    ]
    return pl.pallas_call(
        second_grads_kernel,
        out_shape=BLOCKS,
        in_specs=[SCALARS] + [ANY] * 19,
        out_specs=ANY,
        scratch_shapes=twice + [pltpu.VMEM(s.shape, s.dtype) for s in SMALL]
        + [pltpu.VMEM((64, 16, 128), F32), pltpu.VMEM((64, 16, WIDE), BF), pltpu.SemaphoreType.DMA((23,))],
        compiler_params=pltpu.CompilerParams(vmem_limit_bytes=127 << 19),
        cost_estimate=cost(21),
        name="second_grads",
    )(active, *kept_0, *kept_1, *small)


def average(ema, weight, grad, rate):
    return rate * ema + (1.0 - rate) * (weight - LEARN_RATE * grad)


def average_kernel(first, rates, total, few, *refs):
    weights, emas, grads, news = refs[:6], refs[6:12], refs[12:18], refs[18:24]
    grads[0][0, :, :1024] = total[0:8, 0:1024]
    grads[0][0, :, 1024:] = total[8:16, 0:1024]
    grads[1][0, :, :1024] = total[0:8, 1024:2048]
    grads[1][0, :, 1024:] = total[8:16, 1024:2048]
    grads[2][0, 0:16, :] = total[:, 2048:2560]
    grads[2][0, 16:32, :] = total[:, 2560:3072]
    gain = total[8:9, 3072:3200]
    grads[3][0, 0:1, :] = gain[:, 0:8]
    grads[3][0, 1:2, :] = pltpu.roll(gain, 120, 1)[:, 0:8]
    is_first = first[0] == 1
    proj = few[9:13, :]
    grads[4][...] = jnp.where(is_first, proj, pltpu.roll(proj, 64, 1))[:, 0:8]
    code = jnp.where(is_first, few[0:4, :], few[4:8, :])
    turned = pltpu.roll(code, 64, 1)
    for r in range(4):
        grads[5][2 * r : 2 * r + 1, :] = code[r : r + 1, 0:64]
        grads[5][2 * r + 1 : 2 * r + 2, :] = turned[r : r + 1, 0:64]
    for i in range(6):
        rate = rates[0] if i < 4 else rates[1]
        news[i][...] = average(emas[i][...], weights[i][...].astype(F32), grads[i][...], rate)


def averages(first, rates, total, few, weights, emas):
    shapes = [jax.ShapeDtypeStruct(e.shape, F32) for e in emas]
    return pl.pallas_call(
        average_kernel,
        out_shape=shapes * 2,
        in_specs=[SCALARS, SCALARS] + [INSIDE] * 14,
        out_specs=[INSIDE] * 12,
        name="averages",
    )(first, rates, total, few, *weights, *emas)


def per_device(
    video, cot_h, cot_q, frames, codes, w_attn, w_up, w_down, gains, proj, codebook,
    ema_attn, ema_up, ema_down, ema_gains, ema_proj, ema_code, decay,
):
    segment = lax.axis_index("pipe")
    in_first = (segment == 0).astype(jnp.int32).reshape(1)
    in_second = 1 - in_first
    weights = (w_attn[0], w_up[0], w_down[0], gains[0])

    block = jnp.concatenate([codebook.reshape(4, 128), jnp.pad(proj, ((0, 0), (0, 120)))], axis=0)
    block = block.astype(F32)
    half = 9
    whole = ((0, SEQ),)
    cuts = ((0, half * PATCHES), (half * PATCHES, SEQ - half * PATCHES))
    acts, sent_a, saved_a = first_forward(0, in_first, frames, video, weights, None, 0, half)
    sent_a, block = lax.optimization_barrier((sent_a, block))
    block_first = lax.ppermute(block, "pipe", [(0, 1)])
    received_a = lax.ppermute(sent_a, "pipe", [(0, 1)])
    acts, sent_b, saved_b = first_forward(0, in_first, frames, video, weights, acts, half, FRAMES - half)
    received_b = lax.ppermute(sent_b, "pipe", [(0, 1)])
    acts, sent_1, saved_1 = first_forward(1, in_first, frames, video, weights, acts)
    received_1 = lax.ppermute(sent_1, "pipe", [(0, 1)])
    w_attn_late, w_up_late, w_down_late, gains_late, cot_q, codes, decay, _ = lax.optimization_barrier(
        (w_attn, w_up, w_down, gains, cot_q, codes, decay, sent_1)
    )
    cot_rows = jnp.pad(jnp.swapaxes(cot_q[:, 0], 1, 2), ((0, 0), (0, 0), (0, 120)))
    code_rows = jnp.broadcast_to(codes[:, 0, :, None], (2, SEQ, 128))
    turned = w_attn_late[0, :, : 3 * D].T
    lane = lax.axis_index("dp")
    parts = lax.axis_size("dp")

    def own_rows(weight, axis):
        size = weight.shape[axis] // parts
        return lax.dynamic_slice_in_dim(weight, lane * size, size, axis).astype(F32)

    own = (
        own_rows(w_attn_late, 1), own_rows(w_up_late, 1), own_rows(w_down_late, 1), own_rows(gains_late, 2), proj,
        codebook,
    )
    rates = jnp.stack([lax.dynamic_index_in_dim(decay, segment, 0, keepdims=False), decay[2]])
    cot_rows, code_rows, turned, own, rates, block_first = lax.optimization_barrier(
        (cot_rows, code_rows, turned, own, rates, block_first)
    )
    quant = gather_blocks(jnp.stack([block_first, block]))
    second_weights = (w_attn[0], turned, w_up[0], w_down[0], gains[0])
    cots = (cot_h, cot_rows, code_rows, quant)
    acts, grad_in, back_0, kept_0, small = second_section(
        0, in_second, frames, cuts, (received_a, received_b), second_weights, cots, acts
    )
    returned_0 = lax.ppermute(back_0, "pipe", [(1, 0)])
    acts, grad_in, back_1, kept_1, small = second_section(
        1, in_second, frames, whole, (received_1,), second_weights, cots, acts, grad_in, small
    )
    returned_1 = lax.ppermute(back_1, "pipe", [(1, 0)])
    blocks = second_grads(in_second, kept_0, kept_1, small)

    returned_0, blocks = lax.optimization_barrier((returned_0, blocks))
    grad_in, *before = first_backward(0, in_first, video, weights, returned_0, cuts, (*saved_a, *saved_b), grad_in)

    grad_in, blocks = first_backward(
        1, in_first, video, weights, returned_1, whole, saved_1, grad_in, blocks, before
    )
    total, few = scatter_blocks(blocks)
    results = averages(
        in_first, rates, total, few, own, (ema_attn, ema_up, ema_down, ema_gains, ema_proj, ema_code)
    )
    return (acts[None, :, None], grad_in[None, :, None], *results)


def solution(mesh):
    placed = (
        P(None, "dp", None, None),
        P(None, "dp", None, None),
        P(None, "dp", None, None),
        P(None, "dp"),
        P(None, "dp", None),
        P("pipe", None, None),
        P("pipe", None, None),
        P("pipe", None, None),
        P("pipe", None, None),
        P(("pipe", "dp"), None),
        P(None, ("pipe", "dp")),
        P("pipe", "dp", None),
        P("pipe", "dp", None),
        P("pipe", "dp", None),
        P("pipe", None, "dp"),
        P(("pipe", "dp"), None),
        P(None, ("pipe", "dp")),
        P(),
    )
    return jax.shard_map(
        per_device,
        mesh=mesh,
        in_specs=placed,
        out_specs=(
            P("pipe", None, "dp", None, None),
            P("pipe", None, "dp", None, None),
            P("pipe", "dp", None),
            P("pipe", "dp", None),
            P("pipe", "dp", None),
            P("pipe", None, "dp"),
            P(("pipe", "dp"), None),
            P(None, ("pipe", "dp")),
            P("pipe", "dp", None),
            P("pipe", "dp", None),
            P("pipe", "dp", None),
            P("pipe", None, "dp"),
            P(("pipe", "dp"), None),
            P(None, ("pipe", "dp")),
        ),
        check_vma=False,
    )
```

```python
import functools

import jax
import jax.numpy as jnp
from jax import lax
from jax.experimental import pallas as pl
from jax.experimental.pallas import tpu as pltpu
from jax.sharding import PartitionSpec as P

D = 512
HEADS = 8
HEAD_DIM = 64
FF = 2048
CODES = 8192
CODE_DIM = 8
LOW_CODES = 64
PATCHES = 64
FRAMES = 17
SEQ = 1088


EPSILON = 1e-05
BETA = 0.25
LEARN_RATE = 0.0001
MASKED = -1e30
MESH = pl.DeviceIdType.MESH
WIDE = 3200
ROUNDS = (((0, 1024), (1024, 1024)), ((2048, 640), (2688, 512)))


def gather_kernel(block_ref, out_ref, landed, send_sems, recv_sems):
    pipe = lax.axis_index("pipe")
    dp = lax.axis_index("dp")

    def copy_of(step):
        return pltpu.make_async_remote_copy(
            src_ref=block_ref,
            dst_ref=landed.at[step],
            send_sem=send_sems.at[step],
            recv_sem=recv_sems.at[step],
            device_id=(1, lax.rem(dp + step, 64)),
            device_id_type=MESH,
        )

    @pl.when(pipe == 1)
    def _():
        barrier = pltpu.get_barrier_semaphore()

        def greet(step, carry):
            pl.semaphore_signal(barrier, inc=1, device_id=(1, lax.rem(dp + step, 64)), device_id_type=MESH)
            return carry

        lax.fori_loop(1, 64, greet, 0)
        pl.semaphore_wait(barrier, 63)

        def start(step, carry):
            copy_of(step).start()
            return carry

        lax.fori_loop(1, 64, start, 0)
        for half in range(2):
            out_ref[half * 64 + dp] = block_ref[half]

        def arrive(step, carry):
            copy_of(step).wait_recv()
            source = lax.rem(dp + 64 - step, 64)
            for half in range(2):
                out_ref[half * 64 + source] = landed[step, half]
            return carry

        lax.fori_loop(1, 64, arrive, 0)

        def finish(step, carry):
            copy_of(step).wait_send()
            return carry

        lax.fori_loop(1, 64, finish, 0)


def gather_blocks(block):
    return pl.pallas_call(
        gather_kernel,
        out_shape=jax.ShapeDtypeStruct((128, 8, 128), jnp.float32),
        in_specs=[pl.BlockSpec(memory_space=pltpu.VMEM)],
        out_specs=pl.BlockSpec(memory_space=pltpu.VMEM),
        scratch_shapes=[
            pltpu.VMEM((64, 2, 8, 128), jnp.float32),
            pltpu.SemaphoreType.DMA((64,)),
            pltpu.SemaphoreType.DMA((64,)),
        ],
        compiler_params=pltpu.CompilerParams(collective_id=1, has_side_effects=True),
        name="gather_quantizer",
    )(block)


BF = jnp.bfloat16
F32 = jnp.float32
SCALE = HEAD_DIM**-0.5
PAD = 1152
NN = (((1,), (0,)), ((), ()))
NT = (((1,), (1,)), ((), ()))
TN = (((0,), (0,)), ((), ()))
SPAN = 544
SPANS = SEQ // SPAN
WIDTH = 384
WIDTHS = PAD // WIDTH
COLUMNS = PAD // 128
ANY = pl.BlockSpec(memory_space=pl.ANY)
INSIDE = pl.BlockSpec(memory_space=pltpu.VMEM)
SCALARS = pl.BlockSpec(memory_space=pltpu.SMEM)


def cost(micros):
    return pl.CostEstimate(flops=int(micros * 1.1e9), bytes_accessed=int(micros * 1e6), transcendentals=0)


def dot(left, right, dims=NN):
    return lax.dot_general(left, right, dims, preferred_element_type=F32)


def normal(value):
    center = jnp.mean(value, axis=-1, keepdims=True)
    centred = value - center
    spread = jnp.mean(centred * centred, axis=-1, keepdims=True)
    rate = lax.rsqrt(spread + EPSILON)
    return centred * rate, rate


def normal_back(value, gain, d_normed):
    hat, rate = normal(value)
    scaled = d_normed * gain
    first = jnp.mean(scaled, axis=-1, keepdims=True)
    second = jnp.mean(scaled * hat, axis=-1, keepdims=True)
    terms = d_normed * hat
    return rate * (scaled - first - hat * second), fold_rows(terms), hat


def fold_rows(terms):
    return jnp.sum(terms.reshape(-1, 8, D), axis=0)


def gelu_pair(value):
    square = value * value
    inner = value * (0.7978845608028654 + 0.035677408136300125 * square)
    half = 0.5 + 0.5 * jnp.tanh(inner)
    out = value * half
    slope = half + out * (1.0 - half) * (1.5957691216057308 + 0.21406444881780075 * square)
    return out.astype(BF), slope.astype(BF)


def feed_forward(middle, gain, up, down, act_ref, slope_ref, rows):
    normed = (normal(middle)[0] * gain).astype(BF)
    total = middle
    hidden = dot(normed, up[:, 0:512])
    for j in range(4):
        cols = slice(j * 512, (j + 1) * 512)
        after = dot(normed, up[:, cols.stop : cols.stop + 512]) if j < 3 else None
        act, slope = gelu_pair(hidden)
        act_ref[rows, cols] = act
        slope_ref[rows, cols] = slope
        total = total + dot(act, down[cols, :])
        hidden = after
    return normed, total


def lane_is_low(shape):
    return lax.rem(lax.broadcasted_iota(jnp.int32, shape, len(shape) - 1), 128) < 64


def head_mask(shape):
    lane = lax.broadcasted_iota(jnp.int32, shape, 1)
    return [(lane >= 64 * h) & (lane < 64 * h + 64) for h in range(4)]


def spread_heads(value, masks):
    zero = jnp.zeros_like(value)
    return jnp.concatenate([jnp.where(m, value, zero) for m in masks], axis=0)


def fold_heads(value, masks):
    total = jnp.where(masks[0], value[:64], 0.0)
    for h in range(1, 4):
        total = total + jnp.where(masks[h], value[64 * h : 64 * h + 64], 0.0)
    return total


def head_blocks():
    row = lax.broadcasted_iota(jnp.int32, (256, 256), 0)
    lane = lax.broadcasted_iota(jnp.int32, (256, 256), 1)
    return (lax.div(row, 64) == lax.div(lane, 64)).astype(BF)


def frame_groups(frames=FRAMES):
    for f in range(frames):
        for g in range(2):
            yield slice(f * 64, f * 64 + 64), g * 256


def window_forward(frames, mixed, scores, probs, context):
    masks = head_mask((64, 256))
    slab = frames * 64 // (8 if frames == FRAMES else 4)
    for rows, at in frame_groups(frames):
        keys = spread_heads(mixed[rows, 512 + at : 768 + at], masks)
        scores[rows, at : at + 256] = dot(mixed[rows, at : at + 256], keys, NT)
    low = lane_is_low((slab, 128))

    def soften(i):
        rows = row_span(i, slab)
        for c in range(4):
            cols = slice(c * 128, c * 128 + 128)
            piece = scores[rows, cols]
            left = jnp.max(jnp.where(low, piece, -jnp.inf), axis=1, keepdims=True)
            right = jnp.max(jnp.where(low, -jnp.inf, piece), axis=1, keepdims=True)
            scores[rows, cols] = jnp.exp((piece - jnp.where(low, left, right)) * SCALE)

    loop(frames * 64 // slab, soften)
    ones = head_blocks()
    for rows, at in frame_groups(frames):
        cols = slice(at, at + 256)
        power = scores[rows, cols].astype(BF)
        inverse = 1.0 / dot(power, ones)
        values = spread_heads(mixed[rows, 1024 + at : 1280 + at], masks)
        context[rows, cols] = (dot(power, values) * inverse).astype(BF)
        probs[rows, cols] = (power.astype(F32) * inverse).astype(BF)


def window_backward_probs(mixed, d_context, d_probs):
    masks = head_mask((64, 256))
    for rows, at in frame_groups():
        cols = slice(at, at + 256)
        values = spread_heads(mixed[rows, 1024 + at : 1280 + at], masks)
        d_probs[rows, cols] = dot(d_context[rows, cols], values, NT)


def window_backward(mixed, probs, d_context, d_probs, d_scores, d_mixed):
    masks = head_mask((64, 256))
    ones = head_blocks()

    def soften(i):
        rows = row_span(i, SPAN)
        for g in range(2):
            cols = slice(g * 256, g * 256 + 256)
            wide = probs[rows, cols].astype(F32)
            here = d_probs[rows, cols]
            delta = dot((wide * here).astype(BF), ones)
            d_scores[rows, cols] = (wide * (here - delta) * SCALE).astype(BF)

    loop(SPANS, soften)
    for rows, at in frame_groups():
        cols = slice(at, at + 256)
        here = d_scores[rows, cols]
        keys = spread_heads(mixed[rows, 512 + at : 768 + at], masks)
        d_mixed[rows, at : at + 256] = dot(here, keys).astype(BF)
        d_keys = fold_heads(dot(here, mixed[rows, at : at + 256], TN), masks)
        d_mixed[rows, 512 + at : 768 + at] = d_keys.astype(BF)
        d_values = fold_heads(dot(probs[rows, cols], d_context[rows, cols], TN), masks)
        d_mixed[rows, 1024 + at : 1280 + at] = d_values.astype(BF)


def loop(count, body):
    def step(index, carry):
        body(index)
        return carry

    lax.fori_loop(0, count, step, 0)


def row_span(index, size):
    return pl.ds(pl.multiple_of(index * size, 16), size)


def valid_rows(start, size, count):
    row = lax.broadcasted_iota(jnp.int32, (size, 1), 0) + start
    return row < count * PATCHES


def first_forward_kernel(micro, begin, amount, *refs):
    (active, frames, video, w_attn, w_up, w_down, gains) = refs[:7]
    (acts, sent, s_mixed, s_context, s_probs, s_middle, s_act, s_slope) = refs[-21:-13]
    (x, attn, up, down, mixed, context, probs, middle, act, slope, out, masked, sems) = refs[-13:]
    start, size = begin * PATCHES, amount * PATCHES
    span = size // 2

    @pl.when(active[0] == 1)
    def _():
        count = frames[micro, 0]
        loads = [
            pltpu.make_async_copy(video.at[micro, 0, pl.ds(start, size)], x, sems.at[0]),
            pltpu.make_async_copy(w_attn, attn, sems.at[1]),
            pltpu.make_async_copy(w_up, up, sems.at[2]),
            pltpu.make_async_copy(w_down, down, sems.at[3]),
        ]
        for copy in loads:
            copy.start()
        loads[0].wait()
        loads[1].wait()

        def project(i):
            rows = row_span(i, span)
            hat, _ = normal(x[rows, :].astype(F32))
            normed = (hat * gains[0:1, :]).astype(BF)
            for j in range(3):
                cols = slice(j * 512, (j + 1) * 512)
                mixed[rows, cols] = dot(normed, attn[:, cols]).astype(BF)

        loop(2, project)
        stores = [pltpu.make_async_copy(mixed, s_mixed, sems.at[4])]
        stores[0].start()
        window_forward(amount, mixed, middle, probs, context)
        for k, (source, target) in enumerate(((context, s_context), (probs, s_probs))):
            stores.append(pltpu.make_async_copy(source, target, sems.at[5 + k]))
            stores[-1].start()
        loads[2].wait()
        loads[3].wait()
        real = acts.at[micro, pl.ds(start, size)]
        late = ((out, sent), (masked, real), (middle, s_middle), (act, s_act), (slope, s_slope))

        def late_stores(i):
            rows = row_span(i, span)
            return [
                pltpu.make_async_copy(source.at[rows], target.at[rows], sems.at[7 + k * 2 + i])
                for k, (source, target) in enumerate(late)
            ]

        def tail(i):
            rows = row_span(i, span)
            here = x[rows, :].astype(F32) + dot(context[rows, :], attn[:, 1536:])
            middle[rows, :] = here
            _, total = feed_forward(here, gains[1:2, :], up, down, act, slope, rows)
            out[rows, :] = total.astype(BF)
            masked[rows, :] = jnp.where(valid_rows(start + i * span, span, count), total, 0.0).astype(BF)
            for copy in late_stores(i):
                copy.start()

        loop(2, tail)

        def settle(i):
            for copy in late_stores(i):
                copy.wait()

        loop(2, settle)
        for copy in stores:
            copy.wait()


def saved_shapes(size=SEQ):
    return [
        jax.ShapeDtypeStruct((size, 3 * D), BF),
        jax.ShapeDtypeStruct((size, D), BF),
        jax.ShapeDtypeStruct((size, D), BF),
        jax.ShapeDtypeStruct((size, D), F32),
        jax.ShapeDtypeStruct((size, FF), BF),
        jax.ShapeDtypeStruct((size, FF), BF),
    ]


def weight_scratch():
    return [pltpu.VMEM((D, 4 * D), BF), pltpu.VMEM((D, FF), BF), pltpu.VMEM((FF, D), BF)]


def first_forward(micro, active, frames, video, weights, acts=None, begin=0, amount=FRAMES):
    size = amount * PATCHES
    saved = saved_shapes(size)
    inputs = [active, frames, video, *weights] + ([] if acts is None else [acts])
    tokens = pltpu.VMEM((size, D), BF)
    result = pl.pallas_call(
        functools.partial(first_forward_kernel, micro, begin, amount),
        out_shape=[jax.ShapeDtypeStruct((2, SEQ, D), BF), jax.ShapeDtypeStruct((size, D), BF)] + saved,
        in_specs=([SCALARS, SCALARS, ANY, ANY, ANY, ANY, INSIDE, ANY])[: len(inputs)],
        out_specs=[ANY] * 8,
        input_output_aliases={} if acts is None else {7: 0},
        scratch_shapes=[tokens] + weight_scratch() + [pltpu.VMEM(s.shape, s.dtype) for s in saved]
        + [tokens, tokens, pltpu.SemaphoreType.DMA((17,))],
        compiler_params=pltpu.CompilerParams(vmem_limit_bytes=60 << 20),
        cost_estimate=cost(22 * amount // FRAMES),
        name=f"first_forward_{micro}_{begin}",
    )(*inputs)
    return result[0], result[1], result[2:]


def lanes_at(start, size=512):
    return pl.ds(pl.multiple_of(start, 128), size)


def put_wide(blocks, old, at, left, right):
    lanes = lanes_at(at)
    value = jnp.concatenate([left.reshape(64, 8, 512), right.reshape(64, 8, 512)], axis=1)
    value = value.reshape(4, 2, 4, 2, 16, 512)
    if old is not None:
        value = value + old[:, :, :, :, :, lanes].astype(F32)
    blocks[:, :, :, :, :, lanes] = value.astype(BF)


def put_tall(blocks, old, part, value):
    value = value.reshape(2, 4, 2, 2, 16, 512)
    for half in range(2):
        lanes = slice(half * 512, half * 512 + 512)
        piece = value[:, :, :, half]
        if old is not None:
            piece = piece + old[part, :, :, :, :, lanes].astype(F32)
        blocks[part, :, :, :, :, lanes] = piece.astype(BF)


def send_lanes(source, target, at, size, sem):
    lanes = (slice(None),) * 5 + (pl.ds(at, size),)
    copy = pltpu.make_async_copy(source.at[lanes], target.at[lanes], sem)
    copy.start()
    return copy


def spread_gains(sums, few):
    dst = lax.broadcasted_iota(jnp.int32, (64, D), 0)
    lane = lax.broadcasted_iota(jnp.int32, (64, D), 1)
    source = lax.broadcasted_iota(jnp.int32, (D, 128), 0)
    place = lax.broadcasted_iota(jnp.int32, (D, 128), 1)
    total = jnp.zeros((64, 128), F32)
    for k in range(2):
        row = jnp.sum(sums[8 * k : 8 * k + 8, :], axis=0, keepdims=True)
        mine = jnp.where(lane // 8 == dst, row, 0.0)
        pick = (lax.rem(source, 8) + 8 * k == place).astype(F32)
        total = total + lax.dot_general(mine, pick, NN, precision=lax.Precision.HIGHEST, preferred_element_type=F32)
    few[:, 8, :] = total


BLOCKS = jax.ShapeDtypeStruct((4, 2, 4, 2, 16, WIDE), BF)
GAINS = jax.ShapeDtypeStruct((16, D), F32)


class FirstBackward:
    def __init__(self, micro, fresh, cuts, gains, places, scratch, sems):
        self.gains, self.sems, self.fresh = gains, sems, fresh
        (self.x, self.attn, self.up, self.down, self.mixed, self.context, self.probs, self.middle, self.act, self.slope,
         self.d_two, self.normed, self.d_branch, self.d_mid, self.d_context, self.g_out, self.g_gains, self.more_gains,
         self.few, self.blocks, block_old) = scratch
        self.old = None if fresh else block_old
        video, w_attn, w_up, w_down, d_in, saved, old_blocks, old_gains = places
        self.table = []

        def load_saved(name, k, target, start, size):
            for p, (first, amount) in enumerate(cuts):
                low, high = max(start, first), min(start + size, first + amount)
                if low < high:
                    part = saved[p][k].at[pl.ds(low - first, high - low)]
                    self.table.append((name, part, target.at[pl.ds(low, high - low)]))

        self.table += [("d_in", d_in, self.d_two), ("down", w_down, self.down)]
        load_saved("slope0", 5, self.slope, 0, SPAN)
        self.table.append(("up", w_up, self.up))
        load_saved("middle0", 3, self.middle, 0, SPAN)
        load_saved("slope1", 5, self.slope, SPAN, SPAN)
        load_saved("middle1", 3, self.middle, SPAN, SPAN)
        load_saved("act", 4, self.act, 0, SEQ)
        if not fresh:
            self.table += [("old", old_blocks, block_old), ("old", old_gains, self.more_gains)]
        self.table.append(("attn", w_attn, self.attn))
        load_saved("context", 1, self.context, 0, SEQ)
        load_saved("probs", 2, self.probs, 0, SEQ)
        load_saved("mixed", 0, self.mixed, 0, SEQ)
        self.table.append(("x", video.at[micro, 0], self.x))

    def copies(self, *names):
        return [
            pltpu.make_async_copy(source, target, self.sems.at[18 + i])
            for i, (name, source, target) in enumerate(self.table)
            if not names or name in names
        ]

    def need(self, *names):
        for copy in self.copies(*names):
            copy.wait()

    def feed(self):
        for copy in self.copies():
            copy.start()
        self.g_gains[...] = jnp.zeros_like(self.g_gains)
        gain = self.gains[1:2, :]
        self.need("d_in", "down")
        for i in range(SPANS):
            rows = slice(i * SPAN, (i + 1) * SPAN)
            d_low = self.d_two[rows, :]
            total = jnp.zeros((SPAN, D), F32)
            d_act = dot(d_low, self.down[0:512, :], NT)
            self.need(f"slope{i}")
            for j in range(4):
                cols = slice(j * 512, (j + 1) * 512)
                after = dot(d_low, self.down[cols.stop : cols.stop + 512, :], NT) if j < 3 else None
                d_hidden = (d_act * self.slope[rows, cols].astype(F32)).astype(BF)
                self.slope[rows, cols] = d_hidden
                if i + j == 0:
                    self.need("up")
                total = total + dot(d_hidden, self.up[:, cols], NT)
                d_act = after
            self.need(f"middle{i}")
            here = self.middle[rows, :]
            d_here, g_rows, hat = normal_back(here, gain, total)
            self.g_gains[8:16, :] += g_rows
            self.normed[rows, :] = (hat * gain).astype(BF)
            d_here = d_low.astype(F32) + d_here
            self.d_mid[rows, :] = d_here
            self.d_branch[rows, :] = d_here.astype(BF)

    def put_down(self):
        self.need("act")
        if not self.fresh:
            self.need("old")
        loop(
            4,
            lambda j: put_tall(
                self.blocks, self.old, j, dot(self.act[:, lanes_at(j * 512)], self.d_two[...], TN)
            ),
        )

    def put_up(self):
        def put(j):
            left, right = self.slope[:, lanes_at(j * 512)], self.slope[:, lanes_at(1024 + j * 512)]
            put_wide(
                self.blocks, self.old, 1024 + j * 512, dot(self.normed[...], left, TN), dot(self.normed[...], right, TN)
            )

        loop(2, put)

    def into_context(self):
        self.need("attn", "context", "probs", "mixed", "x")
        self.g_out[...] = dot(self.context[...], self.d_branch[...], TN)

        def into(i):
            rows = row_span(i, SPAN)
            self.d_context[rows, :] = dot(self.d_branch[rows, :], self.attn[:, 1536:], NT).astype(BF)

        loop(SPANS, into)
        window_backward_probs(self.mixed, self.d_context, self.middle)

    def into_input(self, grad_in):
        d_mixed = self.act
        window_backward(self.mixed, self.probs, self.d_context, self.middle, self.normed, d_mixed)
        gain = self.gains[0:1, :]

        def head(i):
            rows = row_span(i, SPAN)
            total = jnp.zeros((SPAN, D), F32)
            for j in range(3):
                cols = slice(j * 512, (j + 1) * 512)
                total = total + dot(d_mixed[rows, cols], self.attn[:, cols], NT)
            d_here, g_rows, hat = normal_back(self.x[rows, :].astype(F32), gain, total)
            self.g_gains[0:8, :] += g_rows
            self.normed[rows, :] = (hat * gain).astype(BF)
            self.d_branch[rows, :] = (self.d_mid[rows, :] + d_here).astype(BF)

        loop(SPANS, head)
        pltpu.make_async_copy(self.d_branch, grad_in, self.sems.at[15]).start()

    def put_attn(self):
        d_mixed, normed = self.act, self.normed
        if not self.fresh:
            self.few[...] = jnp.zeros_like(self.few)
            spread_gains(self.g_gains[...] + self.more_gains[...], self.few)
            self.blocks[:, :, :, :, :, 3072:] = self.few[...].reshape(4, 2, 4, 2, 16, 128).astype(BF)
        put_wide(
            self.blocks, self.old, 2048, dot(normed[...], d_mixed[:, :512], TN),
            dot(normed[...], d_mixed[:, 1024:1536], TN),
        )
        put_wide(self.blocks, self.old, 2560, dot(normed[...], d_mixed[:, 512:1024], TN), self.g_out[...])


def backward_scratch():
    rows = pltpu.VMEM((SEQ, D), BF)
    sums = pltpu.VMEM((16, D), F32)
    return (
        [rows] + weight_scratch() + [pltpu.VMEM(s.shape, s.dtype) for s in saved_shapes()]
        + [rows, rows, rows, pltpu.VMEM((SEQ, D), F32), rows, pltpu.VMEM((D, D), F32), sums, sums]
        + [pltpu.VMEM((64, 16, 128), F32), pltpu.VMEM(BLOCKS.shape, BF), pltpu.VMEM(BLOCKS.shape, BF)]
        + [pltpu.SemaphoreType.DMA((44,))]
    )


def first_backward_kernel(micro, cuts, *refs):
    (active, video, w_attn, w_up, w_down, gains, d_in) = refs[:7]
    saved = [refs[7 + 6 * p : 13 + 6 * p] for p in range(len(cuts))]
    _, grad_in, blocks, new_gains = refs[7 + 6 * len(cuts) : 11 + 6 * len(cuts)]
    *scratch, sems = refs[-22:]

    @pl.when(active[0] == 1)
    def _():
        places = (video, w_attn, w_up, w_down, d_in, saved, None, None)
        work = FirstBackward(micro, True, cuts, gains, places, scratch, sems)
        work.feed()
        work.put_down()
        stores = [send_lanes(work.blocks, blocks, 0, 1024, sems.at[13])]
        work.put_up()
        stores.append(send_lanes(work.blocks, blocks, 1024, 1024, sems.at[14]))
        work.into_context()
        work.into_input(grad_in.at[micro])
        stores.append(pltpu.make_async_copy(work.d_branch, grad_in.at[micro], sems.at[15]))
        stores.append(pltpu.make_async_copy(work.g_gains, new_gains, sems.at[16]))
        stores[-1].start()
        work.put_attn()
        stores.append(send_lanes(work.blocks, blocks, 2048, 1024, sems.at[17]))
        for copy in stores:
            copy.wait()


def first_backward(micro, active, video, weights, d_in, cuts, saved, grad_in):
    inputs = [active, video, *weights, d_in, *saved, grad_in]
    return pl.pallas_call(
        functools.partial(first_backward_kernel, micro, cuts),
        out_shape=[jax.ShapeDtypeStruct(grad_in.shape, BF), BLOCKS, GAINS],
        in_specs=[SCALARS, ANY, ANY, ANY, ANY, INSIDE] + [ANY] * (len(inputs) - 6),
        out_specs=[ANY] * 3,
        input_output_aliases={len(inputs) - 1: 0},
        scratch_shapes=backward_scratch(),
        compiler_params=pltpu.CompilerParams(vmem_limit_bytes=127 << 19),
        cost_estimate=cost(32),
        name=f"first_backward_{micro}",
    )(*inputs)


class Scatter:
    def __init__(self, blocks, out, refs):
        self.blocks, self.out = blocks, out
        (self.other, *lands, self.last_out, self.last_in, self.near_send, self.near_recv, self.one_send, self.one_recv,
         self.two_send, self.two_recv, self.last_send, self.last_recv) = refs
        self.lands = [lands[:6], lands[6:]]
        self.pipe = lax.axis_index("pipe")
        self.dp = lax.axis_index("dp")
        self.core = lax.rem(self.dp, 2)
        self.x = lax.rem(self.dp // 2, 4)
        self.z = lax.rem(self.dp // 8, 2)
        self.y = self.dp // 16

    def at(self, yy, zz, xx, cc):
        return (self.pipe, ((yy * 2 + zz) * 4 + xx) * 2 + cc)

    def x_after(self, step):
        return lax.rem(self.x + step, 4)

    def y_after(self, step):
        return lax.rem(self.y + step, 4)

    def partner(self):
        return self.at(self.y, self.z, self.x, 1 - self.core)

    def greet(self):
        barrier = pltpu.get_barrier_semaphore()
        peers = [self.partner(), self.at(self.y, 1 - self.z, self.x, self.core), (1 - self.pipe, self.dp)]
        peers += [self.at(self.y, self.z, self.x_after(d), self.core) for d in (1, 2, 3)]
        peers += [self.at(self.y_after(d), self.z, self.x, self.core) for d in (1, 2, 3)]
        for peer in peers:
            pl.semaphore_signal(barrier, inc=1, device_id=peer, device_id_type=MESH)
        pl.semaphore_wait(barrier, 9)

    def remote(self, source, target, send, recv, device):
        return pltpu.make_async_remote_copy(
            src_ref=source, dst_ref=target, send_sem=send, recv_sem=recv, device_id=device, device_id_type=MESH
        )

    def near(self, r, part, d):
        lanes = pl.ds(*ROUNDS[r][part])
        slot = 8 * r + 2 * d + part
        if part == 0:
            t = self.x_after(d)
            source = self.blocks.at[:, :, t, 1 - self.core, :, lanes]
            target = self.other.at[:, :, t, :, lanes]
        else:
            t = self.y_after(d)
            source = self.blocks.at[t, :, :, 1 - self.core, :, lanes]
            target = self.other.at[t, :, :, :, lanes]
        return self.remote(source, target, self.near_send.at[slot], self.near_recv.at[slot], self.partner())

    def one(self, r, part, d):
        lanes = pl.ds(*ROUNDS[r][part])
        slot = 6 * r + 2 * d - 2 + part
        if part == 0:
            source = self.blocks.at[:, :, self.x_after(d), self.core, :, lanes]
            device = self.at(self.y, self.z, self.x_after(d), self.core)
        else:
            source = self.blocks.at[self.y_after(d), :, :, self.core, :, lanes]
            device = self.at(self.y_after(d), self.z, self.x, self.core)
        target = self.lands[r][part].at[d - 1]
        return self.remote(source, target, self.one_send.at[slot], self.one_recv.at[slot], device)

    def two(self, r, part, d):
        slot = 6 * r + 2 * d - 2 + part
        t = self.x_after(d) if part else self.y_after(d)
        if part == 0:
            device = self.at(t, self.z, self.x, self.core)
        else:
            device = self.at(self.y, self.z, t, self.core)
        source, target = self.lands[r][2 + part].at[t], self.lands[r][4 + part].at[d - 1]
        return self.remote(source, target, self.two_send.at[slot], self.two_recv.at[slot], device)

    def start_near(self, r, part):
        for d in (2, 1, 3, 0):
            self.near(r, part, d).start()

    def pair(self, r, part):
        lanes = pl.ds(*ROUNDS[r][part])
        for d in (2, 1, 3):
            self.near(r, part, d).wait_recv()

            def add(i, carry, d=d):
                if part == 0:
                    spot = (i // 2, lax.rem(i, 2), self.x_after(d))
                else:
                    spot = (self.y_after(d), i // 4, lax.rem(i, 4))
                mine = (*spot, self.core, slice(None), lanes)
                total = self.blocks[mine].astype(F32) + self.other[(*spot, slice(None), lanes)].astype(F32)
                self.blocks[mine] = total.astype(BF)
                return carry

            lax.fori_loop(0, 8, add, 0)
            self.one(r, part, d).start()

    def gathered(self, r, part, i, zz):
        lanes = pl.ds(*ROUNDS[r][part])
        spot = (i, zz, self.x) if part == 0 else (self.y, zz, i)
        where = (i, zz) if part == 0 else (zz, i)
        total = self.blocks[(*spot, self.core, slice(None), lanes)].astype(F32)
        total = total + self.other[(*spot, slice(None), lanes)].astype(F32)
        for k in range(3):
            total = total + self.lands[r][part][(k, *where)].astype(F32)
        return total

    def cross(self, r):
        for part in range(2):
            self.near(r, part, 0).wait_recv()
            for d in (1, 3, 2):
                self.one(r, part, d).wait_recv()
            for d in (2, 1, 3):
                t = self.x_after(d) if part else self.y_after(d)
                for zz in range(2):
                    self.lands[r][2 + part][t, zz] = self.gathered(r, part, t, zz).astype(BF)
                self.two(r, part, d).start()

    def settle(self, r):
        for part in range(2):
            lanes = pl.ds(*ROUNDS[r][part])
            own = self.x if part else self.y
            away, here = self.gathered(r, part, own, 1 - self.z), self.gathered(r, part, own, self.z)
            for d in (1, 3, 2):
                self.two(r, part, d).wait_recv()
            for k in range(3):
                away = away + self.lands[r][4 + part][k, 1 - self.z].astype(F32)
                here = here + self.lands[r][4 + part][k, self.z].astype(F32)
            self.last_out[:, lanes] = away.astype(BF)
            self.out[:, lanes] = here

    def last(self):
        device = self.at(self.y, 1 - self.z, self.x, self.core)
        return self.remote(self.last_out, self.last_in, self.last_send, self.last_recv, device)

    def sent(self):
        for r in range(2):
            for part in range(2):
                for d in range(4):
                    self.near(r, part, d).wait_send()
                for d in (1, 2, 3):
                    self.one(r, part, d).wait_send()
                    self.two(r, part, d).wait_send()
        self.last().wait_send()


def scatter_scratch():
    sems = pltpu.SemaphoreType.DMA
    refs = [pltpu.VMEM((4, 2, 4, 16, WIDE), BF)]
    for (_, left), (_, right) in ROUNDS:
        refs += [
            pltpu.VMEM((3, 4, 2, 16, left), BF), pltpu.VMEM((3, 2, 4, 16, right), BF),
            pltpu.VMEM((4, 2, 16, left), BF), pltpu.VMEM((4, 2, 16, right), BF),
            pltpu.VMEM((3, 2, 16, left), BF), pltpu.VMEM((3, 2, 16, right), BF),
        ]
    refs += [pltpu.VMEM((16, WIDE), BF), pltpu.VMEM((16, WIDE), BF)]
    return refs + [sems((16,)), sems((16,)), sems((12,)), sems((12,)), sems((12,)), sems((12,)), sems, sems]


def first_backward_scatter_kernel(micro, *refs):
    (video, w_attn, w_up, w_down, gains, d_in) = refs[:6]
    saved = [refs[6:12]]
    blocks, old_blocks, old_gains, grad_in, out, few_out = refs[12:18]
    scratch, sems = refs[18:39], refs[39]
    share, taken, share_send, share_recv = refs[-4:]
    places = (video, w_attn, w_up, w_down, d_in, saved, old_blocks, old_gains)
    work = FirstBackward(micro, False, ((0, SEQ),), gains, places, scratch, sems)
    ring = Scatter(work.blocks, out, refs[40:-4])
    first = ring.pipe == 0

    @pl.when(first)
    def _():
        work.feed()
        work.put_down()

    @pl.when(ring.pipe == 1)
    def _():
        whole = pltpu.make_async_copy(blocks, work.blocks, sems.at[13])
        whole.start()
        whole.wait()

    ring.greet()
    ring.start_near(0, 0)

    @pl.when(first)
    def _():
        work.put_up()

    ring.start_near(0, 1)
    ring.pair(0, 0)

    @pl.when(first)
    def _():
        work.into_context()

    ring.pair(0, 1)

    @pl.when(first)
    def _():
        work.into_input(grad_in)
        work.put_attn()

    ring.start_near(1, 0)
    ring.start_near(1, 1)
    ring.cross(0)
    ring.pair(1, 0)
    ring.pair(1, 1)
    ring.settle(0)
    ring.cross(1)
    ring.settle(1)
    ring.last().start()
    ring.last().wait_recv()
    out[...] = out[...] + ring.last_in[...].astype(F32)
    share[...] = out[:, 3072:]
    across = ring.remote(share, taken, share_send, share_recv, (1 - ring.pipe, ring.dp))

    @pl.when(ring.pipe == 1)
    def _():
        across.start()
        few_out[...] = share[...]
        across.wait_send()

    ring.sent()

    @pl.when(first)
    def _():
        pltpu.make_async_copy(work.d_branch, grad_in, sems.at[15]).wait()
        across.wait_recv()
        few_out[...] = taken[...]


def first_backward_scatter(micro, video, weights, d_in, saved, blocks, before):
    inputs = [video, *weights, d_in, *saved, blocks, *before]
    return pl.pallas_call(
        functools.partial(first_backward_scatter_kernel, micro),
        out_shape=[
            jax.ShapeDtypeStruct((SEQ, D), BF),
            jax.ShapeDtypeStruct((16, WIDE), F32),
            jax.ShapeDtypeStruct((16, 128), F32),
        ],
        in_specs=[ANY, ANY, ANY, ANY, INSIDE] + [ANY] * (len(inputs) - 5),
        out_specs=[ANY, INSIDE, INSIDE],
        scratch_shapes=backward_scratch() + scatter_scratch()
        + [pltpu.VMEM((16, 128), F32)] * 2 + [pltpu.SemaphoreType.DMA] * 2,
        compiler_params=pltpu.CompilerParams(
            collective_id=0, has_side_effects=True, vmem_limit_bytes=127 << 19
        ),
        cost_estimate=cost(60),
        name=f"first_backward_scatter_{micro}",
    )(*inputs)


TALL = 1152
AHEAD = 3
BEHIND = 1


def column(index):
    return slice(index * 128, index * 128 + 128)


def load_head(head, mixed, refs, scale):
    for part, (ref, turned) in enumerate(refs):
        rows = pl.ds(pl.multiple_of(part * D + head * HEAD_DIM, HEAD_DIM), HEAD_DIM)
        for c in range(COLUMNS):
            value = mixed[rows, column(c)].astype(F32)
            if part == 0 and scale:
                value = value * SCALE
            ref[:, column(c)] = value
            if turned is not None:
                turned[:, column(c)] = pltpu.roll(value, 64, 1)


def column_sets(size):
    first = COLUMNS % size
    sets = [list(range(first))] if first else []
    return sets + [list(range(i, i + size)) for i in range(first, COLUMNS, size)]


def pair_rows(lefts, refs, rows_refs):
    for s, ref in enumerate(refs):
        for b in range(max(lefts) + 1):
            right = ref[:, column(b)]
            for i, (a, left) in enumerate(lefts.items()):
                if b <= a:
                    rows_refs[i, 9 * s + b : 9 * s + b + 1, :] = jnp.sum(left * right, axis=0, keepdims=True)


def weighted(rows_of, refs, columns):
    totals = {a: None for a in columns}
    for s, ref in enumerate(refs):
        for b in range(max(columns) + 1):
            right = ref[:, column(b)]
            for a in columns:
                if b <= a:
                    term = rows_of(a, 9 * s + b) * right
                    totals[a] = term if totals[a] is None else totals[a] + term
    return totals


def temporal_head(head, order, mixed, probs, context, q, k, v, kt, vt, rows_ref):
    load_head(head, mixed, ((q, None), (k, kt), (v, vt)), True)
    out_rows = pl.ds(pl.multiple_of(head * HEAD_DIM, HEAD_DIM), HEAD_DIM)
    for columns in column_sets(AHEAD):
        pair_rows({a: q[:, column(a)] for a in columns}, (k, kt), rows_ref)
        for i, a in enumerate(columns):
            scores = jnp.where(order[...] <= 2 * a, rows_ref[i], MASKED)
            power = jnp.exp(scores - jnp.max(scores, axis=0, keepdims=True))
            probs[head, a] = power / jnp.sum(power, axis=0, keepdims=True)
        totals = weighted(lambda a, r: probs[head, a, r : r + 1, :], (v, vt), columns)
        for a in columns:
            context[out_rows, column(a)] = totals[a].astype(BF)


def temporal_head_back(head, mixed, probs, d_context, q, k, v, kt, vt, dc, rows_ref, ds):
    load_head(head, mixed, ((q, None), (k, kt), (v, vt)), False)
    in_rows = pl.ds(pl.multiple_of(head * HEAD_DIM, HEAD_DIM), HEAD_DIM)
    for c in range(COLUMNS):
        dc[:, column(c)] = d_context[in_rows, column(c)].astype(F32)
    for columns in column_sets(AHEAD):
        pair_rows({a: dc[:, column(a)] for a in columns}, (v, vt), rows_ref)
        for i, a in enumerate(columns):
            p = probs[head, a]
            d_probs = jnp.where(p > 0.0, rows_ref[i], 0.0)
            delta = jnp.sum(d_probs * p, axis=0, keepdims=True)
            ds[a] = p * (d_probs - delta) * SCALE
        totals = weighted(lambda a, r: ds[a, r : r + 1, :], (k, kt), columns)
        for a in columns:
            mixed[in_rows, column(a)] = totals[a].astype(BF)
    for part, (weight, source) in enumerate(
        ((lambda a, r: ds[a, r : r + 1, :], q), (lambda a, r: probs[head, a, r : r + 1, :], dc))
    ):
        rows = pl.ds(pl.multiple_of((part + 1) * D + head * HEAD_DIM, HEAD_DIM), HEAD_DIM)
        for columns in column_sets(BEHIND):
            sums = {}
            for a in range(min(columns), COLUMNS):
                value = source[:, column(a)]
                for b in columns:
                    if b <= a:
                        for s in range(2):
                            term = weight(a, 9 * s + b) * value
                            sums[b, s] = sums[b, s] + term if (b, s) in sums else term
            for b in columns:
                mixed[rows, column(b)] = (sums[b, 0] + pltpu.roll(sums[b, 1], 64, 1)).astype(BF)


def frame_order(count):
    row = lax.broadcasted_iota(jnp.int32, (24, 128), 0)
    high = (lax.broadcasted_iota(jnp.int32, (24, 128), 1) >= 64).astype(jnp.int32)
    turned = row >= 9
    base = 2 * jnp.where(turned, row - 9, row)
    key_frame = base + jnp.where(turned, 1 - high, high)
    return jnp.where((row < 18) & (key_frame < count), key_frame - high, 1000)


def second_kernel(micro, fresh, cuts, *refs):
    pieces, refs = refs[: len(cuts)], refs[len(cuts) :]
    (active, frames, w_attn, w_turned, w_up, w_down, gains, cot_h, cot_q, codes, quant) = refs[:11]
    if fresh:
        _, acts, grad_in, sent_back = refs[11:15]
        old = []
    else:
        _, _, *old = refs[11:16]
        acts, grad_in, sent_back = refs[16:19]
    (s_act, s_hidden, s_normed, s_two, s_d_two, s_branch, s_context, s_mixed, new_gains, new_proj, new_code) = refs[-48:-37]
    (x, attn_out, turned, up, down, normed, normed_two, mixed, context, d_context, probs, middle, act, slope, out,
     masked, d_mid, d_two, cot, cot_codes, code_rows, table, proj_wide, proj, g_gains, g_proj, g_code,
     q, k, v, kt, vt, dc, rows_ref, ds, order, sems) = refs[-37:]

    @pl.when(active[0] == 1)
    def _():
        count = frames[micro, 0]
        real = pl.ds(0, SEQ)
        pairs = [(piece, x.at[pl.ds(*cut)]) for piece, cut in zip(pieces, cuts)]
        pairs += [
            (w_turned, turned), (w_attn.at[:, pl.ds(1536, 512)], attn_out), (w_up, up),
            (w_down, down), (codes.at[micro], code_rows.at[real]), (cot_q.at[micro], cot_codes.at[real]),
            (cot_h.at[micro, 0], cot.at[real]),
        ]
        pairs += list(zip(old, (g_gains, g_proj, g_code)))
        loads = [pltpu.make_async_copy(s, t, sems.at[i]) for i, (s, t) in enumerate(pairs)]
        for copy in loads:
            copy.start()
        stores = []

        def save(source, target):
            stores.append(pltpu.make_async_copy(source, target, sems.at[12 + len(stores)]))
            stores[-1].start()

        tail_rows = pl.ds(SEQ, PAD - SEQ)
        x[tail_rows, :] = jnp.zeros((PAD - SEQ, D), BF)
        cot[tail_rows, :] = jnp.zeros((PAD - SEQ, D), BF)
        cot_codes[tail_rows, :] = jnp.zeros((PAD - SEQ, 128), BF)
        code_rows[tail_rows, :] = jnp.zeros((PAD - SEQ, 128), jnp.int32)
        rows_ref[...] = jnp.zeros_like(rows_ref)
        order[...] = frame_order(count)
        if fresh:
            g_gains[...] = jnp.zeros_like(g_gains)
            g_proj[...] = jnp.zeros_like(g_proj)
            g_code[...] = jnp.zeros_like(g_code)
        for j in range(4):
            table[:, column(j)] = quant[:, j, :].astype(BF)
            proj_wide[pl.ds(j, 128, stride=4), :] = quant[:, 4 + j, :]
        proj[...] = proj_wide[...].astype(BF)
        gain_one, gain_two = gains[0:1, :], gains[1:2, :]
        for copy in loads[: len(cuts) + 1]:
            copy.wait()

        def project(i):
            rows, lanes = row_span(i, WIDTH), lanes_at(i * WIDTH, WIDTH)
            normed[rows, :] = (normal(x[rows, :].astype(F32))[0] * gain_one).astype(BF)
            for j in range(3):
                parts = slice(j * 512, (j + 1) * 512)
                mixed[parts, lanes] = dot(turned[parts, :], normed[rows, :], NT).astype(BF)

        loop(WIDTHS, project)
        save(normed, s_normed)
        loop(HEADS, lambda h: temporal_head(h, order, mixed, probs, context, q, k, v, kt, vt, rows_ref))
        save(context, s_context)
        for copy in loads[len(cuts) + 1 :]:
            copy.wait()

        def into_middle(i):
            rows = row_span(i, WIDTH)
            middle[rows, :] = x[rows, :].astype(F32) + dot(context[:, lanes_at(i * WIDTH, WIDTH)], attn_out[...], TN)

        loop(WIDTHS, into_middle)

        def forward_tail(i):
            rows = row_span(i, TALL)
            here = middle[rows, :]
            normed_low, total = feed_forward(here, gain_two, up, down, act, slope, rows)
            normed_two[rows, :] = normed_low
            valid = valid_rows(i * TALL, TALL, count)
            low = total.astype(BF)
            out[rows, :] = low
            masked[rows, :] = jnp.where(valid, total, 0.0).astype(BF)
            mask = valid.astype(F32)
            latent = dot(low, proj[...])
            code = code_rows[rows, :]
            lane = lax.broadcasted_iota(jnp.int32, (TALL, 128), 1)
            high = (lax.div(code, LOW_CODES) == lane).astype(BF)
            near = dot(high, table[...])
            spot = lax.rem(code, LOW_CODES) == lax.rem(lane, LOW_CODES)
            spots = jnp.concatenate([spot] * 4, axis=1)
            place = lax.div(lax.broadcasted_iota(jnp.int32, (512, 128), 0), LOW_CODES)
            pick = (place == lax.broadcasted_iota(jnp.int32, (512, 128), 1)).astype(BF)
            chosen = dot(jnp.where(spots, near, 0.0).astype(BF), pick)
            d_latent = (mask * (cot_codes[rows, :].astype(F32) + 2.0 * BETA * (latent - chosen))).astype(BF)
            d_chosen = (2.0 * mask * (chosen - latent)).astype(BF)
            g_proj[...] += dot(low, d_latent, TN)
            spread = jnp.where(spots, dot(d_chosen, pick, NT), 0.0).astype(BF)
            g_code[...] += dot(high, spread, TN)
            d_out = cot[rows, :].astype(F32) * mask + dot(d_latent, proj[...], NT)
            d_two[rows, :] = d_out.astype(BF)
            d_mid[rows, :] = d_out

        loop(PAD // TALL, forward_tail)
        save(masked.at[real], acts.at[micro])
        save(act, s_act)
        save(normed_two, s_two)
        save(d_two, s_d_two)
        save(g_proj, new_proj)
        save(g_code, new_code)
        d_branch = out

        def backward_tail(i):
            rows = row_span(i, TALL)
            d_low = d_two[rows, :]
            total = jnp.zeros((TALL, D), F32)
            d_act = dot(d_low, down[0:512, :], NT)
            for j in range(4):
                cols = slice(j * 512, (j + 1) * 512)
                after = dot(d_low, down[cols.stop : cols.stop + 512, :], NT) if j < 3 else None
                d_hidden = (d_act * slope[rows, cols].astype(F32)).astype(BF)
                slope[rows, cols] = d_hidden
                total = total + dot(d_hidden, up[:, cols], NT)
                d_act = after
            d_here, g_rows, _ = normal_back(middle[rows, :], gain_two, total)
            g_gains[8:16, :] += g_rows
            d_here = d_mid[rows, :] + d_here
            d_mid[rows, :] = d_here
            d_branch[rows, :] = d_here.astype(BF)

        loop(PAD // TALL, backward_tail)
        save(slope, s_hidden)
        save(d_branch, s_branch)

        def into_context(i):
            lanes = lanes_at(i * WIDTH, WIDTH)
            d_context[:, lanes] = dot(attn_out[...], d_branch[row_span(i, WIDTH), :], NT).astype(BF)

        loop(WIDTHS, into_context)
        loop(
            HEADS,
            lambda h: temporal_head_back(h, mixed, probs, d_context, q, k, v, kt, vt, dc, rows_ref, ds),
        )
        save(mixed, s_mixed)
        d_x = cot

        def finish(i):
            rows = row_span(i, WIDTH)
            total = dot(mixed[:, lanes_at(i * WIDTH, WIDTH)], turned[...], TN)
            d_here, g_rows, _ = normal_back(x[rows, :].astype(F32), gain_one, total)
            g_gains[0:8, :] += g_rows
            d_x[rows, :] = (d_mid[rows, :] + d_here).astype(BF)

        loop(WIDTHS, finish)
        save(d_x.at[real], sent_back)
        save(d_x.at[real], grad_in.at[micro])
        save(g_gains, new_gains)
        for copy in stores:
            copy.wait()


TOKENS = jax.ShapeDtypeStruct((PAD, D), BF)
HIDDEN = jax.ShapeDtypeStruct((PAD, FF), BF)
KEPT = [
    HIDDEN, HIDDEN, TOKENS, TOKENS, TOKENS, TOKENS,
    jax.ShapeDtypeStruct((D, PAD), BF), jax.ShapeDtypeStruct((3 * D, PAD), BF),
]
SMALL = [
    GAINS,
    jax.ShapeDtypeStruct((D, 128), F32),
    jax.ShapeDtypeStruct((128, 512), F32),
]


def second_section(micro, active, frames, cuts, received, weights, cots, acts, grad_in=None, small=None):
    fresh = small is None
    inputs = [*received, active, frames, *weights, *cots, acts]
    place = len(inputs) - 1
    outputs = [
        jax.ShapeDtypeStruct(acts.shape, BF),
        jax.ShapeDtypeStruct(acts.shape, BF),
        jax.ShapeDtypeStruct((SEQ, D), BF),
    ] + KEPT + SMALL
    aliases = {place: 0}
    if not fresh:
        inputs += [grad_in, *small]
        aliases = {place: 0, place + 1: 1}
    tokens = pltpu.VMEM((PAD, D), BF)
    tokens_wide = pltpu.VMEM((PAD, D), F32)
    flipped = pltpu.VMEM((D, PAD), BF)
    hidden = pltpu.VMEM((PAD, FF), BF)
    one_head = pltpu.VMEM((HEAD_DIM, PAD), F32)
    scratch = [
        tokens, pltpu.VMEM((D, D), BF), pltpu.VMEM((3 * D, D), BF), pltpu.VMEM((D, FF), BF), pltpu.VMEM((FF, D), BF),
        tokens, tokens, pltpu.VMEM((3 * D, PAD), BF), flipped, flipped, pltpu.VMEM((HEADS, COLUMNS, 24, 128), F32),
        tokens_wide, hidden, hidden, tokens, tokens, tokens_wide, tokens, tokens, pltpu.VMEM((PAD, 128), BF),
        pltpu.VMEM((PAD, 128), jnp.int32), pltpu.VMEM((128, 512), BF), pltpu.VMEM((D, 128), F32),
        pltpu.VMEM((D, 128), BF),
    ]
    scratch += [pltpu.VMEM(s.shape, s.dtype) for s in SMALL] + [one_head] * 6 + [
        pltpu.VMEM((AHEAD, 24, 128), F32), pltpu.VMEM((COLUMNS, 24, 128), F32), pltpu.VMEM((24, 128), jnp.int32),
        pltpu.SemaphoreType.DMA((30,)),
    ]
    specs = [ANY] * len(cuts) + [SCALARS, SCALARS, ANY, ANY, ANY, ANY, INSIDE, ANY, ANY, ANY, INSIDE]
    result = pl.pallas_call(
        functools.partial(second_kernel, micro, fresh, cuts),
        out_shape=outputs,
        in_specs=specs + [ANY] * (len(inputs) - len(specs)),
        out_specs=[ANY] * len(outputs),
        input_output_aliases=aliases,
        scratch_shapes=scratch,
        compiler_params=pltpu.CompilerParams(vmem_limit_bytes=127 << 19),
        cost_estimate=cost(44),
        name=f"second_section_{micro}",
    )(*inputs)
    return result[0], result[1], result[2], result[3:11], result[11:]


def second_grads_kernel(active, *refs):
    kept = (refs[:8], refs[8:16])
    s_gains, s_proj, s_code, blocks = refs[16:20]
    (act, hidden, normed, normed_two, d_two, d_branch, context, mixed, g_gains, g_proj, g_code, few, block_out, sems) = refs[20:]
    held = (act, hidden, normed, normed_two, d_two, d_branch, context, mixed)

    @pl.when(active[0] == 1)
    def _():
        loads = {}
        for k in (0, 4, 1, 3, 6, 5, 7, 2):
            for m in range(2):
                at = pl.ds(m * PAD, PAD)
                into = held[k].at[:, at] if k >= 6 else held[k].at[at]
                loads[k, m] = pltpu.make_async_copy(kept[m][k], into, sems.at[2 * k + m])
                loads[k, m].start()
        tiny = [
            pltpu.make_async_copy(s, t, sems.at[16 + i])
            for i, (s, t) in enumerate(((s_gains, g_gains), (s_proj, g_proj), (s_code, g_code)))
        ]
        for copy in tiny:
            copy.start()

        def need(*keys):
            for k in keys:
                for m in range(2):
                    loads[k, m].wait()

        need(0, 4)
        for j in range(4):
            put_tall(block_out, None, j, dot(act[:, j * 512 : j * 512 + 512], d_two[...], TN))
        stores = [send_lanes(block_out, blocks, 0, 1024, sems.at[19])]
        need(1, 3)
        for j in range(2):
            left, right = hidden[:, j * 512 : j * 512 + 512], hidden[:, 1024 + j * 512 : 1536 + j * 512]
            put_wide(
                block_out, None, 1024 + j * 512, dot(normed_two[...], left, TN), dot(normed_two[...], right, TN)
            )
        stores.append(send_lanes(block_out, blocks, 1024, 1024, sems.at[20]))
        need(6, 5, 7, 2)
        parts = [dot(mixed[j * 512 : j * 512 + 512, :], normed[...]).T for j in range(3)]
        put_wide(block_out, None, 2048, parts[0], parts[2])
        put_wide(block_out, None, 2560, parts[1], dot(context[...], d_branch[...]))
        stores.append(send_lanes(block_out, blocks, 2048, 1024, sems.at[21]))
        for copy in tiny:
            copy.wait()
        few[...] = jnp.zeros_like(few)
        spread_gains(g_gains[...], few)
        for j in range(4):
            few[:, j, :] = g_code[0:64, column(j)]
            few[:, 4 + j, :] = g_code[64:128, column(j)]
        for j in range(4):
            first = g_proj[pl.ds(j, 64, stride=4), :]
            second = g_proj[pl.ds(256 + j, 64, stride=4), :]
            few[:, 9 + j, :] = first + pltpu.roll(second, 64, 1)
        block_out[:, :, :, :, :, 3072:] = few[...].reshape(4, 2, 4, 2, 16, 128).astype(BF)
        stores.append(send_lanes(block_out, blocks, 3072, 128, sems.at[22]))
        for copy in stores:
            copy.wait()


def second_grads(active, kept_0, kept_1, small):
    twice = [
        pltpu.VMEM((s.shape[0], 2 * PAD) if s.shape[1] == PAD else (2 * PAD, s.shape[1]), BF) for s in KEPT
    ]
    return pl.pallas_call(
        second_grads_kernel,
        out_shape=BLOCKS,
        in_specs=[SCALARS] + [ANY] * 19,
        out_specs=ANY,
        scratch_shapes=twice + [pltpu.VMEM(s.shape, s.dtype) for s in SMALL]
        + [pltpu.VMEM((64, 16, 128), F32), pltpu.VMEM(BLOCKS.shape, BF), pltpu.SemaphoreType.DMA((23,))],
        compiler_params=pltpu.CompilerParams(vmem_limit_bytes=127 << 19),
        cost_estimate=cost(21),
        name="second_grads",
    )(active, *kept_0, *kept_1, *small)


def average(ema, weight, grad, rate):
    return rate * ema + (1.0 - rate) * (weight - LEARN_RATE * grad)


def average_kernel(first, rates, total, few, *refs):
    weights, emas, d_x, grads, news, grad_in, held, sems = refs[:6], refs[6:12], refs[12], refs[14:20], refs[20:26], *refs[26:]
    fetch = pltpu.make_async_copy(d_x, held, sems.at[0])
    place = pltpu.make_async_copy(held, grad_in.at[1], sems.at[1])

    @pl.when(first[0] == 1)
    def _():
        fetch.start()
        fetch.wait()
        place.start()

    grads[0][0, :, :1024] = total[0:8, 2048:3072]
    grads[0][0, :, 1024:] = total[8:16, 2048:3072]
    grads[1][0, :, :1024] = total[0:8, 1024:2048]
    grads[1][0, :, 1024:] = total[8:16, 1024:2048]
    grads[2][0, 0:16, :] = total[:, 0:512]
    grads[2][0, 16:32, :] = total[:, 512:1024]
    gain = total[8:9, 3072:3200]
    grads[3][0, 0:1, :] = gain[:, 0:8]
    grads[3][0, 1:2, :] = pltpu.roll(gain, 120, 1)[:, 0:8]
    is_first = first[0] == 1
    proj = few[9:13, :]
    grads[4][...] = jnp.where(is_first, proj, pltpu.roll(proj, 64, 1))[:, 0:8]
    code = jnp.where(is_first, few[0:4, :], few[4:8, :])
    turned = pltpu.roll(code, 64, 1)
    for r in range(4):
        grads[5][2 * r : 2 * r + 1, :] = code[r : r + 1, 0:64]
        grads[5][2 * r + 1 : 2 * r + 2, :] = turned[r : r + 1, 0:64]
    for i in range(6):
        rate = rates[0] if i < 4 else rates[1]
        news[i][...] = average(emas[i][...], weights[i][...].astype(F32), grads[i][...], rate)

    @pl.when(first[0] == 1)
    def _():
        place.wait()


def averages(first, rates, total, few, weights, emas, d_x, grad_in):
    shapes = [jax.ShapeDtypeStruct(e.shape, F32) for e in emas]
    return pl.pallas_call(
        average_kernel,
        out_shape=shapes * 2 + [jax.ShapeDtypeStruct(grad_in.shape, BF)],
        in_specs=[SCALARS, SCALARS] + [INSIDE] * 14 + [ANY, ANY],
        out_specs=[INSIDE] * 12 + [ANY],
        input_output_aliases={17: 12},
        scratch_shapes=[pltpu.VMEM((SEQ, D), BF), pltpu.SemaphoreType.DMA((2,))],
        name="averages",
    )(first, rates, total, few, *weights, *emas, d_x, grad_in)


def per_device(
    video, cot_h, cot_q, frames, codes, w_attn, w_up, w_down, gains, proj, codebook,
    ema_attn, ema_up, ema_down, ema_gains, ema_proj, ema_code, decay,
):
    segment = lax.axis_index("pipe")
    in_first = (segment == 0).astype(jnp.int32).reshape(1)
    in_second = 1 - in_first
    weights = (w_attn[0], w_up[0], w_down[0], gains[0])

    block = jnp.concatenate([codebook.reshape(4, 128), jnp.pad(proj, ((0, 0), (0, 120)))], axis=0)
    block = block.astype(F32)
    half = 9
    whole = ((0, SEQ),)
    cuts = ((0, half * PATCHES), (half * PATCHES, SEQ - half * PATCHES))
    acts, sent_a, saved_a = first_forward(0, in_first, frames, video, weights, None, 0, half)
    sent_a, block = lax.optimization_barrier((sent_a, block))
    block_first = lax.ppermute(block, "pipe", [(0, 1)])
    received_a = lax.ppermute(sent_a, "pipe", [(0, 1)])
    acts, sent_b, saved_b = first_forward(0, in_first, frames, video, weights, acts, half, FRAMES - half)
    received_b = lax.ppermute(sent_b, "pipe", [(0, 1)])
    acts, sent_1, saved_1 = first_forward(1, in_first, frames, video, weights, acts)
    received_1 = lax.ppermute(sent_1, "pipe", [(0, 1)])
    w_attn_late, w_up_late, w_down_late, gains_late, cot_q, codes, decay, _ = lax.optimization_barrier(
        (w_attn, w_up, w_down, gains, cot_q, codes, decay, sent_1)
    )
    cot_rows = jnp.pad(jnp.swapaxes(cot_q[:, 0], 1, 2), ((0, 0), (0, 0), (0, 120)))
    code_rows = jnp.broadcast_to(codes[:, 0, :, None], (2, SEQ, 128))
    turned = w_attn_late[0, :, : 3 * D].T
    lane = lax.axis_index("dp")
    parts = lax.axis_size("dp")

    def own_rows(weight, axis):
        size = weight.shape[axis] // parts
        return lax.dynamic_slice_in_dim(weight, lane * size, size, axis).astype(F32)

    own = (
        own_rows(w_attn_late, 1), own_rows(w_up_late, 1), own_rows(w_down_late, 1), own_rows(gains_late, 2), proj,
        codebook,
    )
    rates = jnp.stack([lax.dynamic_index_in_dim(decay, segment, 0, keepdims=False), decay[2]])
    cot_rows, code_rows, turned, own, rates, block_first = lax.optimization_barrier(
        (cot_rows, code_rows, turned, own, rates, block_first)
    )
    quant = gather_blocks(jnp.stack([block_first, block]))
    second_weights = (w_attn[0], turned, w_up[0], w_down[0], gains[0])
    cots = (cot_h, cot_rows, code_rows, quant)
    acts, grad_in, back_0, kept_0, small = second_section(
        0, in_second, frames, cuts, (received_a, received_b), second_weights, cots, acts
    )
    returned_0 = lax.ppermute(back_0, "pipe", [(1, 0)])
    acts, grad_in, back_1, kept_1, small = second_section(
        1, in_second, frames, whole, (received_1,), second_weights, cots, acts, grad_in, small
    )
    returned_1 = lax.ppermute(back_1, "pipe", [(1, 0)])
    blocks = second_grads(in_second, kept_0, kept_1, small)

    returned_0, blocks = lax.optimization_barrier((returned_0, blocks))
    grad_in, *before = first_backward(0, in_first, video, weights, returned_0, cuts, (*saved_a, *saved_b), grad_in)

    d_x, total, few = first_backward_scatter(1, video, weights, returned_1, saved_1, blocks, before)
    emas = (ema_attn, ema_up, ema_down, ema_gains, ema_proj, ema_code)
    *results, grad_in = averages(in_first, rates, total, few, own, emas, d_x, grad_in)
    return (acts[None, :, None], grad_in[None, :, None], *results)


def solution(mesh):
    placed = (
        P(None, "dp", None, None),
        P(None, "dp", None, None),
        P(None, "dp", None, None),
        P(None, "dp"),
        P(None, "dp", None),
        P("pipe", None, None),
        P("pipe", None, None),
        P("pipe", None, None),
        P("pipe", None, None),
        P(("pipe", "dp"), None),
        P(None, ("pipe", "dp")),
        P("pipe", "dp", None),
        P("pipe", "dp", None),
        P("pipe", "dp", None),
        P("pipe", None, "dp"),
        P(("pipe", "dp"), None),
        P(None, ("pipe", "dp")),
        P(),
    )
    return jax.shard_map(
        per_device,
        mesh=mesh,
        in_specs=placed,
        out_specs=(
            P("pipe", None, "dp", None, None),
            P("pipe", None, "dp", None, None),
            P("pipe", "dp", None),
            P("pipe", "dp", None),
            P("pipe", "dp", None),
            P("pipe", None, "dp"),
            P(("pipe", "dp"), None),
            P(None, ("pipe", "dp")),
            P("pipe", "dp", None),
            P("pipe", "dp", None),
            P("pipe", "dp", None),
            P("pipe", None, "dp"),
            P(("pipe", "dp"), None),
            P(None, ("pipe", "dp")),
        ),
        check_vma=False,
    )
```

```python
import functools

import jax
import jax.numpy as jnp
from jax import lax
from jax.experimental import pallas as pl
from jax.experimental.pallas import tpu as pltpu
from jax.sharding import PartitionSpec as P

D = 512
HEADS = 8
HEAD_DIM = 64
FF = 2048
CODES = 8192
CODE_DIM = 8
LOW_CODES = 64
PATCHES = 64
FRAMES = 17
SEQ = 1088


EPSILON = 1e-05
BETA = 0.25
LEARN_RATE = 0.0001
MASKED = -1e30
MESH = pl.DeviceIdType.MESH
WIDE = 3200
ROUNDS = (((0, 1024), (1024, 1024)), ((2048, 640), (2688, 512)))


def gather_kernel(block_ref, out_ref, landed, send_sems, recv_sems):
    pipe = lax.axis_index("pipe")
    dp = lax.axis_index("dp")

    def copy_of(step):
        return pltpu.make_async_remote_copy(
            src_ref=block_ref,
            dst_ref=landed.at[step],
            send_sem=send_sems.at[step],
            recv_sem=recv_sems.at[step],
            device_id=(1, lax.rem(dp + step, 64)),
            device_id_type=MESH,
        )

    @pl.when(pipe == 1)
    def _():
        barrier = pltpu.get_barrier_semaphore()

        def greet(step, carry):
            pl.semaphore_signal(barrier, inc=1, device_id=(1, lax.rem(dp + step, 64)), device_id_type=MESH)
            return carry

        lax.fori_loop(1, 64, greet, 0)
        pl.semaphore_wait(barrier, 63)

        def start(step, carry):
            copy_of(step).start()
            return carry

        lax.fori_loop(1, 64, start, 0)
        for half in range(2):
            out_ref[half * 64 + dp] = block_ref[half]

        def arrive(step, carry):
            copy_of(step).wait_recv()
            source = lax.rem(dp + 64 - step, 64)
            for half in range(2):
                out_ref[half * 64 + source] = landed[step, half]
            return carry

        lax.fori_loop(1, 64, arrive, 0)

        def finish(step, carry):
            copy_of(step).wait_send()
            return carry

        lax.fori_loop(1, 64, finish, 0)


def gather_blocks(block):
    return pl.pallas_call(
        gather_kernel,
        out_shape=jax.ShapeDtypeStruct((128, 8, 128), jnp.float32),
        in_specs=[pl.BlockSpec(memory_space=pltpu.VMEM)],
        out_specs=pl.BlockSpec(memory_space=pltpu.VMEM),
        scratch_shapes=[
            pltpu.VMEM((64, 2, 8, 128), jnp.float32),
            pltpu.SemaphoreType.DMA((64,)),
            pltpu.SemaphoreType.DMA((64,)),
        ],
        compiler_params=pltpu.CompilerParams(collective_id=1, has_side_effects=True),
        name="gather_quantizer",
    )(block)


BF = jnp.bfloat16
F32 = jnp.float32
SCALE = HEAD_DIM**-0.5
PAD = 1152
NN = (((1,), (0,)), ((), ()))
NT = (((1,), (1,)), ((), ()))
TN = (((0,), (0,)), ((), ()))
SPAN = 544
SPANS = SEQ // SPAN
WIDTH = 384
WIDTHS = PAD // WIDTH
COLUMNS = PAD // 128
ANY = pl.BlockSpec(memory_space=pl.ANY)
INSIDE = pl.BlockSpec(memory_space=pltpu.VMEM)
SCALARS = pl.BlockSpec(memory_space=pltpu.SMEM)


def cost(micros):
    return pl.CostEstimate(flops=int(micros * 1.1e9), bytes_accessed=int(micros * 1e6), transcendentals=0)


def dot(left, right, dims=NN):
    return lax.dot_general(left, right, dims, preferred_element_type=F32)


def normal(value):
    center = jnp.mean(value, axis=-1, keepdims=True)
    centred = value - center
    spread = jnp.mean(centred * centred, axis=-1, keepdims=True)
    rate = lax.rsqrt(spread + EPSILON)
    return centred * rate, rate


def normal_back(value, gain, d_normed):
    hat, rate = normal(value)
    scaled = d_normed * gain
    first = jnp.mean(scaled, axis=-1, keepdims=True)
    second = jnp.mean(scaled * hat, axis=-1, keepdims=True)
    terms = d_normed * hat
    return rate * (scaled - first - hat * second), fold_rows(terms), hat


def fold_rows(terms):
    return jnp.sum(terms.reshape(-1, 8, D), axis=0)


def gelu_pair(value):
    square = value * value
    inner = value * (0.7978845608028654 + 0.035677408136300125 * square)
    half = 0.5 + 0.5 * jnp.tanh(inner)
    out = value * half
    slope = half + out * (1.0 - half) * (1.5957691216057308 + 0.21406444881780075 * square)
    return out.astype(BF), slope.astype(BF)


def feed_forward(middle, gain, up, down, act_ref, slope_ref, rows):
    normed = (normal(middle)[0] * gain).astype(BF)
    total = middle
    hidden = dot(normed, up[:, 0:512])
    for j in range(4):
        cols = slice(j * 512, (j + 1) * 512)
        after = dot(normed, up[:, cols.stop : cols.stop + 512]) if j < 3 else None
        act, slope = gelu_pair(hidden)
        act_ref[rows, cols] = act
        slope_ref[rows, cols] = slope
        total = total + dot(act, down[cols, :])
        hidden = after
    return normed, total


def lane_is_low(shape):
    return lax.rem(lax.broadcasted_iota(jnp.int32, shape, len(shape) - 1), 128) < 64


def head_mask(shape):
    lane = lax.broadcasted_iota(jnp.int32, shape, 1)
    return [(lane >= 64 * h) & (lane < 64 * h + 64) for h in range(4)]


def spread_heads(value, masks):
    zero = jnp.zeros_like(value)
    return jnp.concatenate([jnp.where(m, value, zero) for m in masks], axis=0)


def fold_heads(value, masks):
    total = jnp.where(masks[0], value[:64], 0.0)
    for h in range(1, 4):
        total = total + jnp.where(masks[h], value[64 * h : 64 * h + 64], 0.0)
    return total


def head_blocks():
    row = lax.broadcasted_iota(jnp.int32, (256, 256), 0)
    lane = lax.broadcasted_iota(jnp.int32, (256, 256), 1)
    return (lax.div(row, 64) == lax.div(lane, 64)).astype(BF)


def frame_groups(frames=FRAMES):
    for f in range(frames):
        for g in range(2):
            yield slice(f * 64, f * 64 + 64), g * 256


def window_forward(frames, mixed, scores, probs, context):
    masks = head_mask((64, 256))
    slab = frames * 64 // (8 if frames == FRAMES else 4)
    for rows, at in frame_groups(frames):
        keys = spread_heads(mixed[rows, 512 + at : 768 + at], masks)
        scores[rows, at : at + 256] = dot(mixed[rows, at : at + 256], keys, NT)
    low = lane_is_low((slab, 128))

    def soften(i):
        rows = row_span(i, slab)
        for c in range(4):
            cols = slice(c * 128, c * 128 + 128)
            piece = scores[rows, cols]
            left = jnp.max(jnp.where(low, piece, -jnp.inf), axis=1, keepdims=True)
            right = jnp.max(jnp.where(low, -jnp.inf, piece), axis=1, keepdims=True)
            scores[rows, cols] = jnp.exp((piece - jnp.where(low, left, right)) * SCALE)

    loop(frames * 64 // slab, soften)
    ones = head_blocks()
    for rows, at in frame_groups(frames):
        cols = slice(at, at + 256)
        power = scores[rows, cols].astype(BF)
        inverse = 1.0 / dot(power, ones)
        values = spread_heads(mixed[rows, 1024 + at : 1280 + at], masks)
        context[rows, cols] = (dot(power, values) * inverse).astype(BF)
        probs[rows, cols] = (power.astype(F32) * inverse).astype(BF)


def window_backward_probs(mixed, d_context, d_probs):
    masks = head_mask((64, 256))
    for rows, at in frame_groups():
        cols = slice(at, at + 256)
        values = spread_heads(mixed[rows, 1024 + at : 1280 + at], masks)
        d_probs[rows, cols] = dot(d_context[rows, cols], values, NT)


def window_backward(mixed, probs, d_context, d_probs, d_scores, d_mixed):
    masks = head_mask((64, 256))
    ones = head_blocks()

    def soften(i):
        rows = row_span(i, SPAN)
        for g in range(2):
            cols = slice(g * 256, g * 256 + 256)
            wide = probs[rows, cols].astype(F32)
            here = d_probs[rows, cols]
            delta = dot((wide * here).astype(BF), ones)
            d_scores[rows, cols] = (wide * (here - delta) * SCALE).astype(BF)

    loop(SPANS, soften)
    for rows, at in frame_groups():
        cols = slice(at, at + 256)
        here = d_scores[rows, cols]
        keys = spread_heads(mixed[rows, 512 + at : 768 + at], masks)
        d_mixed[rows, at : at + 256] = dot(here, keys).astype(BF)
        d_keys = fold_heads(dot(here, mixed[rows, at : at + 256], TN), masks)
        d_mixed[rows, 512 + at : 768 + at] = d_keys.astype(BF)
        d_values = fold_heads(dot(probs[rows, cols], d_context[rows, cols], TN), masks)
        d_mixed[rows, 1024 + at : 1280 + at] = d_values.astype(BF)


def loop(count, body):
    def step(index, carry):
        body(index)
        return carry

    lax.fori_loop(0, count, step, 0)


def each(count, body):
    for index in range(count):
        body(index)


def row_span(index, size):
    return pl.ds(pl.multiple_of(index * size, 16), size)


def valid_rows(start, size, count):
    row = lax.broadcasted_iota(jnp.int32, (size, 1), 0) + start
    return row < count * PATCHES


def first_forward_kernel(micro, begin, amount, *refs):
    (active, frames, video, w_attn, w_up, w_down, gains) = refs[:7]
    (acts, sent, s_mixed, s_context, s_probs, s_middle, s_act, s_slope) = refs[-21:-13]
    (x, attn, up, down, mixed, context, probs, middle, act, slope, out, masked, sems) = refs[-13:]
    start, size = begin * PATCHES, amount * PATCHES
    span = size // 2
    repeat = each if amount == FRAMES else loop

    @pl.when(active[0] == 1)
    def _():
        count = frames[micro]
        loads = [
            pltpu.make_async_copy(video.at[micro, 0, pl.ds(start, size)], x, sems.at[0]),
            pltpu.make_async_copy(w_attn, attn, sems.at[1]),
            pltpu.make_async_copy(w_up, up, sems.at[2]),
            pltpu.make_async_copy(w_down, down, sems.at[3]),
        ]
        for copy in loads:
            copy.start()
        loads[0].wait()
        loads[1].wait()

        def project(i):
            rows = row_span(i, span)
            hat, _ = normal(x[rows, :].astype(F32))
            normed = (hat * gains[0:1, :]).astype(BF)
            for j in range(3):
                cols = slice(j * 512, (j + 1) * 512)
                mixed[rows, cols] = dot(normed, attn[:, cols]).astype(BF)

        repeat(2, project)
        stores = [pltpu.make_async_copy(mixed, s_mixed, sems.at[4])]
        stores[0].start()
        window_forward(amount, mixed, middle, probs, context)
        for k, (source, target) in enumerate(((context, s_context), (probs, s_probs))):
            stores.append(pltpu.make_async_copy(source, target, sems.at[5 + k]))
            stores[-1].start()
        loads[2].wait()
        loads[3].wait()
        real = acts.at[micro, pl.ds(start, size)]
        late = ((out, sent), (masked, real), (middle, s_middle), (act, s_act), (slope, s_slope))

        def late_stores(i):
            rows = row_span(i, span)
            return [
                pltpu.make_async_copy(source.at[rows], target.at[rows], sems.at[7 + k * 2 + i])
                for k, (source, target) in enumerate(late)
            ]

        def tail(i):
            rows = row_span(i, span)
            here = x[rows, :].astype(F32) + dot(context[rows, :], attn[:, 1536:])
            middle[rows, :] = here
            _, total = feed_forward(here, gains[1:2, :], up, down, act, slope, rows)
            out[rows, :] = total.astype(BF)
            masked[rows, :] = jnp.where(valid_rows(start + i * span, span, count), total, 0.0).astype(BF)
            for copy in late_stores(i):
                copy.start()

        repeat(2, tail)

        def settle(i):
            for copy in late_stores(i):
                copy.wait()

        loop(2, settle)
        for copy in stores:
            copy.wait()


def saved_shapes(size=SEQ):
    return [
        jax.ShapeDtypeStruct((size, 3 * D), BF),
        jax.ShapeDtypeStruct((size, D), BF),
        jax.ShapeDtypeStruct((size, D), BF),
        jax.ShapeDtypeStruct((size, D), F32),
        jax.ShapeDtypeStruct((size, FF), BF),
        jax.ShapeDtypeStruct((size, FF), BF),
    ]


def weight_scratch():
    return [pltpu.VMEM((D, 4 * D), BF), pltpu.VMEM((D, FF), BF), pltpu.VMEM((FF, D), BF)]


def first_forward(micro, active, frames, video, weights, acts=None, begin=0, amount=FRAMES):
    size = amount * PATCHES
    saved = saved_shapes(size)
    inputs = [active, frames, video, *weights] + ([] if acts is None else [acts])
    tokens = pltpu.VMEM((size, D), BF)
    result = pl.pallas_call(
        functools.partial(first_forward_kernel, micro, begin, amount),
        out_shape=[jax.ShapeDtypeStruct((2, SEQ, D), BF), jax.ShapeDtypeStruct((size, D), BF)] + saved,
        in_specs=([SCALARS, SCALARS, ANY, ANY, ANY, ANY, INSIDE, ANY])[: len(inputs)],
        out_specs=[ANY] * 8,
        input_output_aliases={} if acts is None else {7: 0},
        scratch_shapes=[tokens] + weight_scratch() + [pltpu.VMEM(s.shape, s.dtype) for s in saved]
        + [tokens, tokens, pltpu.SemaphoreType.DMA((17,))],
        compiler_params=pltpu.CompilerParams(vmem_limit_bytes=127 << 19),
        cost_estimate=cost(22 * amount // FRAMES),
        name=f"first_forward_{micro}_{begin}",
    )(*inputs)
    return result[0], result[1], result[2:]


def lanes_at(start, size=512):
    return pl.ds(pl.multiple_of(start, 128), size)


def put_wide(blocks, old, at, left, right):
    lanes = lanes_at(at)
    value = jnp.concatenate([left.reshape(64, 8, 512), right.reshape(64, 8, 512)], axis=1)
    value = value.reshape(4, 2, 4, 2, 16, 512)
    if old is not None:
        value = value + old[:, :, :, :, :, lanes].astype(F32)
    blocks[:, :, :, :, :, lanes] = value.astype(BF)


def put_tall(blocks, old, part, value):
    value = value.reshape(2, 4, 2, 2, 16, 512)
    for half in range(2):
        lanes = slice(half * 512, half * 512 + 512)
        piece = value[:, :, :, half]
        if old is not None:
            piece = piece + old[part, :, :, :, :, lanes].astype(F32)
        blocks[part, :, :, :, :, lanes] = piece.astype(BF)


def send_lanes(source, target, at, size, sem):
    lanes = (slice(None),) * 5 + (pl.ds(at, size),)
    copy = pltpu.make_async_copy(source.at[lanes], target.at[lanes], sem)
    copy.start()
    return copy


def spread_gains(sums, few):
    dst = lax.broadcasted_iota(jnp.int32, (64, D), 0)
    lane = lax.broadcasted_iota(jnp.int32, (64, D), 1)
    source = lax.broadcasted_iota(jnp.int32, (D, 128), 0)
    place = lax.broadcasted_iota(jnp.int32, (D, 128), 1)
    total = jnp.zeros((64, 128), F32)
    for k in range(2):
        row = jnp.sum(sums[8 * k : 8 * k + 8, :], axis=0, keepdims=True)
        mine = jnp.where(lane // 8 == dst, row, 0.0)
        pick = (lax.rem(source, 8) + 8 * k == place).astype(F32)
        total = total + lax.dot_general(mine, pick, NN, precision=lax.Precision.HIGHEST, preferred_element_type=F32)
    few[:, 8, :] = total


BLOCKS = jax.ShapeDtypeStruct((4, 2, 4, 2, 16, WIDE), BF)
GAINS = jax.ShapeDtypeStruct((16, D), F32)


class FirstBackward:
    def __init__(self, micro, fresh, cuts, gains, places, scratch, sems):
        self.gains, self.sems, self.fresh = gains, sems, fresh
        (self.x, self.attn, self.up, self.down, self.mixed, self.context, self.probs, self.middle, self.act, self.slope,
         self.d_two, self.normed, self.d_branch, self.d_mid, self.d_context, self.g_out, self.g_gains, self.more_gains,
         self.few, self.blocks, block_old) = scratch
        self.old = None if fresh else block_old
        video, w_attn, w_up, w_down, d_in, saved, old_blocks, old_gains = places
        self.table = []

        def load_saved(name, k, target, start, size):
            for p, (first, amount) in enumerate(cuts):
                low, high = max(start, first), min(start + size, first + amount)
                if low < high:
                    part = saved[p][k].at[pl.ds(low - first, high - low)]
                    self.table.append((name, part, target.at[pl.ds(low, high - low)]))

        self.table += [("d_in", d_in, self.d_two), ("down", w_down, self.down)]
        load_saved("slope0", 5, self.slope, 0, SPAN)
        self.table.append(("up", w_up, self.up))
        load_saved("middle0", 3, self.middle, 0, SPAN)
        load_saved("slope1", 5, self.slope, SPAN, SPAN)
        load_saved("middle1", 3, self.middle, SPAN, SPAN)
        load_saved("act", 4, self.act, 0, SEQ)
        if not fresh:
            self.table += [("old", old_blocks, block_old), ("old", old_gains, self.more_gains)]
        self.table.append(("attn", w_attn, self.attn))
        load_saved("context", 1, self.context, 0, SEQ)
        load_saved("probs", 2, self.probs, 0, SEQ)
        load_saved("mixed", 0, self.mixed, 0, SEQ)
        self.table.append(("x", video.at[micro, 0], self.x))

    def copies(self, *names):
        return [
            pltpu.make_async_copy(source, target, self.sems.at[18 + i])
            for i, (name, source, target) in enumerate(self.table)
            if not names or name in names
        ]

    def need(self, *names):
        for copy in self.copies(*names):
            copy.wait()

    def feed(self):
        for copy in self.copies():
            copy.start()
        self.g_gains[...] = jnp.zeros_like(self.g_gains)
        gain = self.gains[1:2, :]
        self.need("d_in", "down")
        for i in range(SPANS):
            rows = slice(i * SPAN, (i + 1) * SPAN)
            d_low = self.d_two[rows, :]
            total = jnp.zeros((SPAN, D), F32)
            d_act = dot(d_low, self.down[0:512, :], NT)
            self.need(f"slope{i}")
            for j in range(4):
                cols = slice(j * 512, (j + 1) * 512)
                after = dot(d_low, self.down[cols.stop : cols.stop + 512, :], NT) if j < 3 else None
                d_hidden = (d_act * self.slope[rows, cols].astype(F32)).astype(BF)
                self.slope[rows, cols] = d_hidden
                if i + j == 0:
                    self.need("up")
                total = total + dot(d_hidden, self.up[:, cols], NT)
                d_act = after
            self.need(f"middle{i}")
            here = self.middle[rows, :]
            d_here, g_rows, hat = normal_back(here, gain, total)
            self.g_gains[8:16, :] += g_rows
            self.normed[rows, :] = (hat * gain).astype(BF)
            d_here = d_low.astype(F32) + d_here
            self.d_mid[rows, :] = d_here
            self.d_branch[rows, :] = d_here.astype(BF)

    def put_down(self):
        self.need("act")
        if not self.fresh:
            self.need("old")
        loop(
            4,
            lambda j: put_tall(
                self.blocks, self.old, j, dot(self.act[:, lanes_at(j * 512)], self.d_two[...], TN)
            ),
        )

    def put_up(self):
        def put(j):
            left, right = self.slope[:, lanes_at(j * 512)], self.slope[:, lanes_at(1024 + j * 512)]
            put_wide(
                self.blocks, self.old, 1024 + j * 512, dot(self.normed[...], left, TN), dot(self.normed[...], right, TN)
            )

        loop(2, put)

    def into_context(self):
        self.need("attn", "context", "probs", "mixed", "x")
        self.g_out[...] = dot(self.context[...], self.d_branch[...], TN)

        def into(i):
            rows = row_span(i, SPAN)
            self.d_context[rows, :] = dot(self.d_branch[rows, :], self.attn[:, 1536:], NT).astype(BF)

        each(SPANS, into)
        window_backward_probs(self.mixed, self.d_context, self.middle)

    def into_input(self, grad_in):
        d_mixed = self.act
        window_backward(self.mixed, self.probs, self.d_context, self.middle, self.normed, d_mixed)
        gain = self.gains[0:1, :]

        def head(i):
            rows = row_span(i, SPAN)
            total = jnp.zeros((SPAN, D), F32)
            for j in range(3):
                cols = slice(j * 512, (j + 1) * 512)
                total = total + dot(d_mixed[rows, cols], self.attn[:, cols], NT)
            d_here, g_rows, hat = normal_back(self.x[rows, :].astype(F32), gain, total)
            self.g_gains[0:8, :] += g_rows
            self.normed[rows, :] = (hat * gain).astype(BF)
            self.d_branch[rows, :] = (self.d_mid[rows, :] + d_here).astype(BF)

        each(SPANS, head)
        pltpu.make_async_copy(self.d_branch, grad_in, self.sems.at[15]).start()

    def put_attn(self):
        d_mixed, normed = self.act, self.normed
        if not self.fresh:
            self.few[...] = jnp.zeros_like(self.few)
            spread_gains(self.g_gains[...] + self.more_gains[...], self.few)
            self.blocks[:, :, :, :, :, 3072:] = self.few[...].reshape(4, 2, 4, 2, 16, 128).astype(BF)
        put_wide(
            self.blocks, self.old, 2048, dot(normed[...], d_mixed[:, :512], TN),
            dot(normed[...], d_mixed[:, 1024:1536], TN),
        )
        put_wide(self.blocks, self.old, 2560, dot(normed[...], d_mixed[:, 512:1024], TN), self.g_out[...])


def backward_scratch():
    rows = pltpu.VMEM((SEQ, D), BF)
    sums = pltpu.VMEM((16, D), F32)
    return (
        [rows] + weight_scratch() + [pltpu.VMEM(s.shape, s.dtype) for s in saved_shapes()]
        + [rows, rows, rows, pltpu.VMEM((SEQ, D), F32), rows, pltpu.VMEM((D, D), F32), sums, sums]
        + [pltpu.VMEM((64, 16, 128), F32), pltpu.VMEM(BLOCKS.shape, BF), pltpu.VMEM(BLOCKS.shape, BF)]
        + [pltpu.SemaphoreType.DMA((44,))]
    )


def first_backward_kernel(micro, cuts, *refs):
    (active, video, w_attn, w_up, w_down, gains, d_in) = refs[:7]
    saved = [refs[7 + 6 * p : 13 + 6 * p] for p in range(len(cuts))]
    _, grad_in, blocks, new_gains = refs[7 + 6 * len(cuts) : 11 + 6 * len(cuts)]
    *scratch, sems = refs[-22:]

    @pl.when(active[0] == 1)
    def _():
        places = (video, w_attn, w_up, w_down, d_in, saved, None, None)
        work = FirstBackward(micro, True, cuts, gains, places, scratch, sems)
        work.feed()
        work.put_down()
        stores = [send_lanes(work.blocks, blocks, 0, 1024, sems.at[13])]
        work.put_up()
        stores.append(send_lanes(work.blocks, blocks, 1024, 1024, sems.at[14]))
        work.into_context()
        work.into_input(grad_in.at[micro])
        stores.append(pltpu.make_async_copy(work.d_branch, grad_in.at[micro], sems.at[15]))
        stores.append(pltpu.make_async_copy(work.g_gains, new_gains, sems.at[16]))
        stores[-1].start()
        work.put_attn()
        stores.append(send_lanes(work.blocks, blocks, 2048, 1024, sems.at[17]))
        for copy in stores:
            copy.wait()


def first_backward(micro, active, video, weights, d_in, cuts, saved, grad_in):
    inputs = [active, video, *weights, d_in, *saved, grad_in]
    return pl.pallas_call(
        functools.partial(first_backward_kernel, micro, cuts),
        out_shape=[jax.ShapeDtypeStruct(grad_in.shape, BF), BLOCKS, GAINS],
        in_specs=[SCALARS, ANY, ANY, ANY, ANY, INSIDE] + [ANY] * (len(inputs) - 6),
        out_specs=[ANY] * 3,
        input_output_aliases={len(inputs) - 1: 0},
        scratch_shapes=backward_scratch(),
        compiler_params=pltpu.CompilerParams(vmem_limit_bytes=127 << 19),
        cost_estimate=cost(32),
        name=f"first_backward_{micro}",
    )(*inputs)


class Scatter:
    def __init__(self, blocks, out, refs):
        self.blocks, self.out = blocks, out
        (self.other, *lands, self.last_out, self.last_in, self.near_send, self.near_recv, self.one_send, self.one_recv,
         self.two_send, self.two_recv, self.last_send, self.last_recv) = refs
        self.lands = [lands[:6], lands[6:]]
        self.pipe = lax.axis_index("pipe")
        self.dp = lax.axis_index("dp")
        self.core = lax.rem(self.dp, 2)
        self.x = lax.rem(self.dp // 2, 4)
        self.z = lax.rem(self.dp // 8, 2)
        self.y = self.dp // 16

    def at(self, yy, zz, xx, cc):
        return (self.pipe, ((yy * 2 + zz) * 4 + xx) * 2 + cc)

    def x_after(self, step):
        return lax.rem(self.x + step, 4)

    def y_after(self, step):
        return lax.rem(self.y + step, 4)

    def partner(self):
        return self.at(self.y, self.z, self.x, 1 - self.core)

    def greet(self):
        barrier = pltpu.get_barrier_semaphore()
        peers = [self.partner(), self.at(self.y, 1 - self.z, self.x, self.core), (1 - self.pipe, self.dp)]
        peers += [self.at(self.y, self.z, self.x_after(d), self.core) for d in (1, 2, 3)]
        peers += [self.at(self.y_after(d), self.z, self.x, self.core) for d in (1, 2, 3)]
        for peer in peers:
            pl.semaphore_signal(barrier, inc=1, device_id=peer, device_id_type=MESH)
        pl.semaphore_wait(barrier, 9)

    def remote(self, source, target, send, recv, device):
        return pltpu.make_async_remote_copy(
            src_ref=source, dst_ref=target, send_sem=send, recv_sem=recv, device_id=device, device_id_type=MESH
        )

    def near(self, r, part, d):
        lanes = pl.ds(*ROUNDS[r][part])
        slot = 8 * r + 2 * d + part
        if part == 0:
            t = self.x_after(d)
            source = self.blocks.at[:, :, t, 1 - self.core, :, lanes]
            target = self.other.at[:, :, t, :, lanes]
        else:
            t = self.y_after(d)
            source = self.blocks.at[t, :, :, 1 - self.core, :, lanes]
            target = self.other.at[t, :, :, :, lanes]
        return self.remote(source, target, self.near_send.at[slot], self.near_recv.at[slot], self.partner())

    def one(self, r, part, d):
        lanes = pl.ds(*ROUNDS[r][part])
        slot = 6 * r + 2 * d - 2 + part
        if part == 0:
            source = self.blocks.at[:, :, self.x_after(d), self.core, :, lanes]
            device = self.at(self.y, self.z, self.x_after(d), self.core)
        else:
            source = self.blocks.at[self.y_after(d), :, :, self.core, :, lanes]
            device = self.at(self.y_after(d), self.z, self.x, self.core)
        target = self.lands[r][part].at[d - 1]
        return self.remote(source, target, self.one_send.at[slot], self.one_recv.at[slot], device)

    def two(self, r, part, d):
        slot = 6 * r + 2 * d - 2 + part
        t = self.x_after(d) if part else self.y_after(d)
        if part == 0:
            device = self.at(t, self.z, self.x, self.core)
        else:
            device = self.at(self.y, self.z, t, self.core)
        source, target = self.lands[r][2 + part].at[t], self.lands[r][4 + part].at[d - 1]
        return self.remote(source, target, self.two_send.at[slot], self.two_recv.at[slot], device)

    def start_near(self, r, part):
        for d in (2, 1, 3, 0):
            self.near(r, part, d).start()

    def pair(self, r, part):
        lanes = pl.ds(*ROUNDS[r][part])
        for d in (2, 1, 3):
            self.near(r, part, d).wait_recv()

            def add(i, carry, d=d):
                if part == 0:
                    spot = (i // 2, lax.rem(i, 2), self.x_after(d))
                else:
                    spot = (self.y_after(d), i // 4, lax.rem(i, 4))
                mine = (*spot, self.core, slice(None), lanes)
                total = self.blocks[mine].astype(F32) + self.other[(*spot, slice(None), lanes)].astype(F32)
                self.blocks[mine] = total.astype(BF)
                return carry

            lax.fori_loop(0, 8, add, 0)
            self.one(r, part, d).start()

    def gathered(self, r, part, i, zz):
        lanes = pl.ds(*ROUNDS[r][part])
        spot = (i, zz, self.x) if part == 0 else (self.y, zz, i)
        where = (i, zz) if part == 0 else (zz, i)
        total = self.blocks[(*spot, self.core, slice(None), lanes)].astype(F32)
        total = total + self.other[(*spot, slice(None), lanes)].astype(F32)
        for k in range(3):
            total = total + self.lands[r][part][(k, *where)].astype(F32)
        return total

    def cross(self, r):
        for part in range(2):
            self.near(r, part, 0).wait_recv()
            for d in (1, 3, 2):
                self.one(r, part, d).wait_recv()
            for d in (2, 1, 3):
                t = self.x_after(d) if part else self.y_after(d)
                for zz in range(2):
                    self.lands[r][2 + part][t, zz] = self.gathered(r, part, t, zz).astype(BF)
                self.two(r, part, d).start()

    def settle(self, r):
        for part in range(2):
            lanes = pl.ds(*ROUNDS[r][part])
            own = self.x if part else self.y
            away, here = self.gathered(r, part, own, 1 - self.z), self.gathered(r, part, own, self.z)
            for d in (1, 3, 2):
                self.two(r, part, d).wait_recv()
            for k in range(3):
                away = away + self.lands[r][4 + part][k, 1 - self.z].astype(F32)
                here = here + self.lands[r][4 + part][k, self.z].astype(F32)
            self.last_out[:, lanes] = away.astype(BF)
            self.out[:, lanes] = here
        self.last(r).start()

    def last(self, r):
        device = self.at(self.y, 1 - self.z, self.x, self.core)
        (begin, left), (_, right) = ROUNDS[r]
        lanes = pl.ds(begin, left + right)
        return self.remote(
            self.last_out.at[:, lanes], self.last_in.at[:, lanes], self.last_send.at[r], self.last_recv.at[r], device
        )

    def close(self, r):
        self.last(r).wait_recv()
        (begin, left), (_, right) = ROUNDS[r]
        lanes = pl.ds(begin, left + right)
        self.out[:, lanes] = self.out[:, lanes] + self.last_in[:, lanes].astype(F32)

    def sent(self):
        for r in range(2):
            for part in range(2):
                for d in range(4):
                    self.near(r, part, d).wait_send()
                for d in (1, 2, 3):
                    self.one(r, part, d).wait_send()
                    self.two(r, part, d).wait_send()
            self.last(r).wait_send()


def scatter_scratch():
    sems = pltpu.SemaphoreType.DMA
    refs = [pltpu.VMEM((4, 2, 4, 16, WIDE), BF)]
    for (_, left), (_, right) in ROUNDS:
        refs += [
            pltpu.VMEM((3, 4, 2, 16, left), BF), pltpu.VMEM((3, 2, 4, 16, right), BF),
            pltpu.VMEM((4, 2, 16, left), BF), pltpu.VMEM((4, 2, 16, right), BF),
            pltpu.VMEM((3, 2, 16, left), BF), pltpu.VMEM((3, 2, 16, right), BF),
        ]
    refs += [pltpu.VMEM((16, WIDE), BF), pltpu.VMEM((16, WIDE), BF)]
    return refs + [sems((16,)), sems((16,)), sems((12,)), sems((12,)), sems((12,)), sems((12,)), sems((2,)), sems((2,))]


def first_backward_scatter_kernel(micro, *refs):
    (video, w_attn, w_up, w_down, gains, d_in) = refs[:6]
    saved = [refs[6:12]]
    blocks, old_blocks, old_gains, grad_in, out, few_out = refs[12:18]
    scratch, sems = refs[18:39], refs[39]
    share, taken, share_send, share_recv = refs[-4:]
    places = (video, w_attn, w_up, w_down, d_in, saved, old_blocks, old_gains)
    work = FirstBackward(micro, False, ((0, SEQ),), gains, places, scratch, sems)
    ring = Scatter(work.blocks, out, refs[40:-4])
    first = ring.pipe == 0

    @pl.when(first)
    def _():
        work.feed()
        work.put_down()

    @pl.when(ring.pipe == 1)
    def _():
        whole = pltpu.make_async_copy(blocks, work.blocks, sems.at[13])
        whole.start()
        whole.wait()

    ring.greet()
    ring.start_near(0, 0)

    @pl.when(first)
    def _():
        work.put_up()

    ring.start_near(0, 1)
    ring.pair(0, 0)

    @pl.when(first)
    def _():
        work.into_context()

    ring.pair(0, 1)

    @pl.when(first)
    def _():
        work.into_input(grad_in)
        work.put_attn()

    ring.start_near(1, 0)
    ring.start_near(1, 1)
    ring.cross(0)
    ring.pair(1, 0)
    ring.pair(1, 1)
    ring.settle(0)
    ring.cross(1)
    ring.settle(1)
    ring.close(0)
    ring.close(1)
    share[...] = out[:, 3072:]
    across = ring.remote(share, taken, share_send, share_recv, (1 - ring.pipe, ring.dp))

    @pl.when(ring.pipe == 1)
    def _():
        across.start()
        few_out[...] = share[...]
        across.wait_send()

    ring.sent()

    @pl.when(first)
    def _():
        pltpu.make_async_copy(work.d_branch, grad_in, sems.at[15]).wait()
        across.wait_recv()
        few_out[...] = taken[...]


def first_backward_scatter(micro, video, weights, d_in, saved, blocks, before):
    inputs = [video, *weights, d_in, *saved, blocks, *before]
    return pl.pallas_call(
        functools.partial(first_backward_scatter_kernel, micro),
        out_shape=[
            jax.ShapeDtypeStruct((SEQ, D), BF),
            jax.ShapeDtypeStruct((16, WIDE), F32),
            jax.ShapeDtypeStruct((16, 128), F32),
        ],
        in_specs=[ANY, ANY, ANY, ANY, INSIDE] + [ANY] * (len(inputs) - 5),
        out_specs=[ANY, INSIDE, INSIDE],
        scratch_shapes=backward_scratch() + scatter_scratch()
        + [pltpu.VMEM((16, 128), F32)] * 2 + [pltpu.SemaphoreType.DMA] * 2,
        compiler_params=pltpu.CompilerParams(
            collective_id=0, has_side_effects=True, vmem_limit_bytes=127 << 19
        ),
        cost_estimate=cost(60),
        name=f"first_backward_scatter_{micro}",
    )(*inputs)


TALL = 1152
AHEAD = 3
BEHIND = 3


def column(index):
    return slice(index * 128, index * 128 + 128)


def load_head(head, mixed, refs, scale):
    for part, (ref, turned) in enumerate(refs):
        rows = pl.ds(pl.multiple_of(part * D + head * HEAD_DIM, HEAD_DIM), HEAD_DIM)
        for c in range(COLUMNS):
            value = mixed[rows, column(c)].astype(F32)
            if part == 0 and scale:
                value = value * SCALE
            ref[:, column(c)] = value
            if turned is not None:
                turned[:, column(c)] = pltpu.roll(value, 64, 1)


def column_sets(size):
    first = COLUMNS % size
    sets = [list(range(first))] if first else []
    return sets + [list(range(i, i + size)) for i in range(first, COLUMNS, size)]


def pair_rows(lefts, refs, rows_refs):
    for s, ref in enumerate(refs):
        for b in range(max(lefts) + 1):
            right = ref[:, column(b)]
            for i, (a, left) in enumerate(lefts.items()):
                if b <= a:
                    rows_refs[i, 9 * s + b : 9 * s + b + 1, :] = jnp.sum(left * right, axis=0, keepdims=True)


def weighted(rows_of, refs, columns):
    totals = {a: None for a in columns}
    for s, ref in enumerate(refs):
        for b in range(max(columns) + 1):
            right = ref[:, column(b)]
            for a in columns:
                if b <= a:
                    term = rows_of(a, 9 * s + b) * right
                    totals[a] = term if totals[a] is None else totals[a] + term
    return totals


def temporal_head(head, order, mixed, probs, context, q, k, v, kt, vt, rows_ref):
    load_head(head, mixed, ((q, None), (k, kt), (v, vt)), True)
    out_rows = pl.ds(pl.multiple_of(head * HEAD_DIM, HEAD_DIM), HEAD_DIM)
    for columns in column_sets(AHEAD):
        pair_rows({a: q[:, column(a)] for a in columns}, (k, kt), rows_ref)
        for i, a in enumerate(columns):
            scores = jnp.where(order[...] <= 2 * a, rows_ref[i], MASKED)
            power = jnp.exp(scores - jnp.max(scores, axis=0, keepdims=True))
            probs[head, a] = power / jnp.sum(power, axis=0, keepdims=True)
        totals = weighted(lambda a, r: probs[head, a, r : r + 1, :], (v, vt), columns)
        for a in columns:
            context[out_rows, column(a)] = totals[a].astype(BF)


def temporal_head_back(head, mixed, probs, d_context, q, k, v, kt, vt, dc, rows_ref, ds):
    load_head(head, mixed, ((q, None), (k, kt), (v, vt)), False)
    in_rows = pl.ds(pl.multiple_of(head * HEAD_DIM, HEAD_DIM), HEAD_DIM)
    for c in range(COLUMNS):
        dc[:, column(c)] = d_context[in_rows, column(c)].astype(F32)
    for columns in column_sets(AHEAD):
        pair_rows({a: dc[:, column(a)] for a in columns}, (v, vt), rows_ref)
        for i, a in enumerate(columns):
            p = probs[head, a]
            d_probs = jnp.where(p > 0.0, rows_ref[i], 0.0)
            delta = jnp.sum(d_probs * p, axis=0, keepdims=True)
            ds[a] = p * (d_probs - delta) * SCALE
        totals = weighted(lambda a, r: ds[a, r : r + 1, :], (k, kt), columns)
        for a in columns:
            mixed[in_rows, column(a)] = totals[a].astype(BF)
    for part, (weight, source) in enumerate(
        ((lambda a, r: ds[a, r : r + 1, :], q), (lambda a, r: probs[head, a, r : r + 1, :], dc))
    ):
        rows = pl.ds(pl.multiple_of((part + 1) * D + head * HEAD_DIM, HEAD_DIM), HEAD_DIM)
        for columns in column_sets(BEHIND):
            sums = {}
            for a in range(min(columns), COLUMNS):
                value = source[:, column(a)]
                for b in columns:
                    if b <= a:
                        for s in range(2):
                            term = weight(a, 9 * s + b) * value
                            sums[b, s] = sums[b, s] + term if (b, s) in sums else term
            for b in columns:
                mixed[rows, column(b)] = (sums[b, 0] + pltpu.roll(sums[b, 1], 64, 1)).astype(BF)


def frame_order(count):
    row = lax.broadcasted_iota(jnp.int32, (24, 128), 0)
    high = (lax.broadcasted_iota(jnp.int32, (24, 128), 1) >= 64).astype(jnp.int32)
    turned = row >= 9
    base = 2 * jnp.where(turned, row - 9, row)
    key_frame = base + jnp.where(turned, 1 - high, high)
    return jnp.where((row < 18) & (key_frame < count), key_frame - high, 1000)


def second_kernel(micro, fresh, cuts, *refs):
    pieces, refs = refs[: len(cuts)], refs[len(cuts) :]
    (active, frames, w_attn, w_turned, w_up, w_down, gains, cot_h, cot_q, codes, s_quant) = refs[:11]
    if fresh:
        _, acts, grad_in, sent_back = refs[11:15]
        old = []
    else:
        _, _, *old = refs[11:16]
        acts, grad_in, sent_back = refs[16:19]
    (s_act, s_hidden, s_normed, s_two, s_d_two, s_branch, s_context, s_mixed, new_gains, new_proj, new_code) = refs[-49:-38]
    (x, attn_out, turned, up, down, normed, normed_two, mixed, context, d_context, probs, middle, act, slope, out,
     masked, d_mid, d_two, cot, cot_codes, code_rows, table, proj_wide, proj, g_gains, g_proj, g_code,
     q, k, v, kt, vt, dc, rows_ref, ds, order, quant, sems) = refs[-38:]

    @pl.when(active[0] == 1)
    def _():
        count = frames[micro]
        real = pl.ds(0, SEQ)
        pairs = [(piece, x.at[pl.ds(*cut)]) for piece, cut in zip(pieces, cuts)]
        pairs += [
            (w_turned, turned), (w_attn.at[:, pl.ds(1536, 512)], attn_out), (w_up, up),
            (w_down, down), (codes.at[micro], code_rows.at[real]), (cot_q.at[micro], cot_codes.at[real]),
            (cot_h.at[micro, 0], cot.at[real]), (s_quant, quant),
        ]
        pairs += list(zip(old, (g_gains, g_proj, g_code)))
        loads = [pltpu.make_async_copy(s, t, sems.at[i]) for i, (s, t) in enumerate(pairs)]
        for copy in loads:
            copy.start()
        stores = []

        def save(source, target):
            stores.append(pltpu.make_async_copy(source, target, sems.at[14 + len(stores)]))
            stores[-1].start()

        tail_rows = pl.ds(SEQ, PAD - SEQ)
        x[tail_rows, :] = jnp.zeros((PAD - SEQ, D), BF)
        cot[tail_rows, :] = jnp.zeros((PAD - SEQ, D), BF)
        cot_codes[tail_rows, :] = jnp.zeros((PAD - SEQ, 128), BF)
        code_rows[tail_rows, :] = jnp.zeros((PAD - SEQ, 128), jnp.int32)
        rows_ref[...] = jnp.zeros_like(rows_ref)
        order[...] = frame_order(count)
        if fresh:
            g_gains[...] = jnp.zeros_like(g_gains)
            g_proj[...] = jnp.zeros_like(g_proj)
            g_code[...] = jnp.zeros_like(g_code)
        gain_one, gain_two = gains[0:1, :], gains[1:2, :]
        for copy in loads[: len(cuts) + 1]:
            copy.wait()

        def project(i):
            rows, lanes = row_span(i, WIDTH), lanes_at(i * WIDTH, WIDTH)
            normed[rows, :] = (normal(x[rows, :].astype(F32))[0] * gain_one).astype(BF)
            for j in range(3):
                parts = slice(j * 512, (j + 1) * 512)
                mixed[parts, lanes] = dot(turned[parts, :], normed[rows, :], NT).astype(BF)

        each(WIDTHS, project)
        save(normed, s_normed)
        loop(HEADS, lambda h: temporal_head(h, order, mixed, probs, context, q, k, v, kt, vt, rows_ref))
        save(context, s_context)
        for copy in loads[len(cuts) + 1 :]:
            copy.wait()
        for j in range(4):
            table[:, column(j)] = quant[:, j, :].astype(BF)
            proj_wide[pl.ds(j, 128, stride=4), :] = quant[:, 4 + j, :]
        proj[...] = proj_wide[...].astype(BF)

        def into_middle(i):
            rows = row_span(i, WIDTH)
            middle[rows, :] = x[rows, :].astype(F32) + dot(context[:, lanes_at(i * WIDTH, WIDTH)], attn_out[...], TN)

        each(WIDTHS, into_middle)

        def forward_tail(i):
            rows = row_span(i, TALL)
            here = middle[rows, :]
            normed_low, total = feed_forward(here, gain_two, up, down, act, slope, rows)
            normed_two[rows, :] = normed_low
            valid = valid_rows(i * TALL, TALL, count)
            low = total.astype(BF)
            out[rows, :] = low
            masked[rows, :] = jnp.where(valid, total, 0.0).astype(BF)
            mask = valid.astype(F32)
            latent = dot(low, proj[...])
            code = code_rows[rows, :]
            lane = lax.broadcasted_iota(jnp.int32, (TALL, 128), 1)
            high = (lax.div(code, LOW_CODES) == lane).astype(BF)
            near = dot(high, table[...])
            spot = lax.rem(code, LOW_CODES) == lax.rem(lane, LOW_CODES)
            spots = jnp.concatenate([spot] * 4, axis=1)
            place = lax.div(lax.broadcasted_iota(jnp.int32, (512, 128), 0), LOW_CODES)
            pick = (place == lax.broadcasted_iota(jnp.int32, (512, 128), 1)).astype(BF)
            chosen = dot(jnp.where(spots, near, 0.0).astype(BF), pick)
            d_latent = (mask * (cot_codes[rows, :].astype(F32) + 2.0 * BETA * (latent - chosen))).astype(BF)
            d_chosen = (2.0 * mask * (chosen - latent)).astype(BF)
            g_proj[...] += dot(low, d_latent, TN)
            spread = jnp.where(spots, dot(d_chosen, pick, NT), 0.0).astype(BF)
            g_code[...] += dot(high, spread, TN)
            d_out = cot[rows, :].astype(F32) * mask + dot(d_latent, proj[...], NT)
            d_two[rows, :] = d_out.astype(BF)
            d_mid[rows, :] = d_out

        loop(PAD // TALL, forward_tail)
        save(masked.at[real], acts.at[micro])
        save(act, s_act)
        save(normed_two, s_two)
        save(d_two, s_d_two)
        save(g_proj, new_proj)
        save(g_code, new_code)
        d_branch = out

        def backward_tail(i):
            rows = row_span(i, TALL)
            d_low = d_two[rows, :]
            total = jnp.zeros((TALL, D), F32)
            d_act = dot(d_low, down[0:512, :], NT)
            for j in range(4):
                cols = slice(j * 512, (j + 1) * 512)
                after = dot(d_low, down[cols.stop : cols.stop + 512, :], NT) if j < 3 else None
                d_hidden = (d_act * slope[rows, cols].astype(F32)).astype(BF)
                slope[rows, cols] = d_hidden
                total = total + dot(d_hidden, up[:, cols], NT)
                d_act = after
            d_here, g_rows, _ = normal_back(middle[rows, :], gain_two, total)
            g_gains[8:16, :] += g_rows
            d_here = d_mid[rows, :] + d_here
            d_mid[rows, :] = d_here
            d_branch[rows, :] = d_here.astype(BF)

        loop(PAD // TALL, backward_tail)
        save(slope, s_hidden)
        save(d_branch, s_branch)

        def into_context(i):
            lanes = lanes_at(i * WIDTH, WIDTH)
            d_context[:, lanes] = dot(attn_out[...], d_branch[row_span(i, WIDTH), :], NT).astype(BF)

        each(WIDTHS, into_context)
        loop(
            HEADS,
            lambda h: temporal_head_back(h, mixed, probs, d_context, q, k, v, kt, vt, dc, rows_ref, ds),
        )
        save(mixed, s_mixed)
        d_x = cot

        def finish(i):
            rows = row_span(i, WIDTH)
            total = dot(mixed[:, lanes_at(i * WIDTH, WIDTH)], turned[...], TN)
            d_here, g_rows, _ = normal_back(x[rows, :].astype(F32), gain_one, total)
            g_gains[0:8, :] += g_rows
            d_x[rows, :] = (d_mid[rows, :] + d_here).astype(BF)

        each(WIDTHS, finish)
        save(d_x.at[real], sent_back)
        save(d_x.at[real], grad_in.at[micro])
        save(g_gains, new_gains)
        for copy in stores:
            copy.wait()


TOKENS = jax.ShapeDtypeStruct((PAD, D), BF)
HIDDEN = jax.ShapeDtypeStruct((PAD, FF), BF)
KEPT = [
    HIDDEN, HIDDEN, TOKENS, TOKENS, TOKENS, TOKENS,
    jax.ShapeDtypeStruct((D, PAD), BF), jax.ShapeDtypeStruct((3 * D, PAD), BF),
]
SMALL = [
    GAINS,
    jax.ShapeDtypeStruct((D, 128), F32),
    jax.ShapeDtypeStruct((128, 512), F32),
]


def second_section(micro, active, frames, cuts, received, weights, cots, acts, grad_in=None, small=None):
    fresh = small is None
    inputs = [*received, active, frames, *weights, *cots, acts]
    place = len(inputs) - 1
    outputs = [
        jax.ShapeDtypeStruct(acts.shape, BF),
        jax.ShapeDtypeStruct(acts.shape, BF),
        jax.ShapeDtypeStruct((SEQ, D), BF),
    ] + KEPT + SMALL
    aliases = {place: 0}
    if not fresh:
        inputs += [grad_in, *small]
        aliases = {place: 0, place + 1: 1}
    tokens = pltpu.VMEM((PAD, D), BF)
    tokens_wide = pltpu.VMEM((PAD, D), F32)
    flipped = pltpu.VMEM((D, PAD), BF)
    hidden = pltpu.VMEM((PAD, FF), BF)
    one_head = pltpu.VMEM((HEAD_DIM, PAD), F32)
    scratch = [
        tokens, pltpu.VMEM((D, D), BF), pltpu.VMEM((3 * D, D), BF), pltpu.VMEM((D, FF), BF), pltpu.VMEM((FF, D), BF),
        tokens, tokens, pltpu.VMEM((3 * D, PAD), BF), flipped, flipped, pltpu.VMEM((HEADS, COLUMNS, 24, 128), F32),
        tokens_wide, hidden, hidden, tokens, tokens, tokens_wide, tokens, tokens, pltpu.VMEM((PAD, 128), BF),
        pltpu.VMEM((PAD, 128), jnp.int32), pltpu.VMEM((128, 512), BF), pltpu.VMEM((D, 128), F32),
        pltpu.VMEM((D, 128), BF),
    ]
    scratch += [pltpu.VMEM(s.shape, s.dtype) for s in SMALL] + [one_head] * 6 + [
        pltpu.VMEM((AHEAD, 24, 128), F32), pltpu.VMEM((COLUMNS, 24, 128), F32), pltpu.VMEM((24, 128), jnp.int32),
        pltpu.VMEM((128, 8, 128), F32), pltpu.SemaphoreType.DMA((32,)),
    ]
    specs = [ANY] * len(cuts) + [SCALARS, SCALARS, ANY, ANY, ANY, ANY, INSIDE, ANY, ANY, ANY, ANY]
    result = pl.pallas_call(
        functools.partial(second_kernel, micro, fresh, cuts),
        out_shape=outputs,
        in_specs=specs + [ANY] * (len(inputs) - len(specs)),
        out_specs=[ANY] * len(outputs),
        input_output_aliases=aliases,
        scratch_shapes=scratch,
        compiler_params=pltpu.CompilerParams(vmem_limit_bytes=127 << 19),
        cost_estimate=cost(44),
        name=f"second_section_{micro}",
    )(*inputs)
    return result[0], result[1], result[2], result[3:11], result[11:]


def second_grads_kernel(active, *refs):
    kept = (refs[:8], refs[8:16])
    s_gains, s_proj, s_code, blocks = refs[16:20]
    (act, hidden, normed, normed_two, d_two, d_branch, context, mixed, g_gains, g_proj, g_code, few, block_out, sems) = refs[20:]
    held = (act, hidden, normed, normed_two, d_two, d_branch, context, mixed)

    @pl.when(active[0] == 1)
    def _():
        loads = {}
        for k in (0, 4, 1, 3, 6, 5, 7, 2):
            for m in range(2):
                at = pl.ds(m * PAD, PAD)
                into = held[k].at[:, at] if k >= 6 else held[k].at[at]
                loads[k, m] = pltpu.make_async_copy(kept[m][k], into, sems.at[2 * k + m])
                loads[k, m].start()
        tiny = [
            pltpu.make_async_copy(s, t, sems.at[16 + i])
            for i, (s, t) in enumerate(((s_gains, g_gains), (s_proj, g_proj), (s_code, g_code)))
        ]
        for copy in tiny:
            copy.start()

        def need(*keys):
            for k in keys:
                for m in range(2):
                    loads[k, m].wait()

        need(0, 4)
        for j in range(4):
            put_tall(block_out, None, j, dot(act[:, j * 512 : j * 512 + 512], d_two[...], TN))
        stores = [send_lanes(block_out, blocks, 0, 1024, sems.at[19])]
        need(1, 3)
        for j in range(2):
            left, right = hidden[:, j * 512 : j * 512 + 512], hidden[:, 1024 + j * 512 : 1536 + j * 512]
            put_wide(
                block_out, None, 1024 + j * 512, dot(normed_two[...], left, TN), dot(normed_two[...], right, TN)
            )
        stores.append(send_lanes(block_out, blocks, 1024, 1024, sems.at[20]))
        need(6, 5, 7, 2)
        parts = [dot(mixed[j * 512 : j * 512 + 512, :], normed[...]).T for j in range(3)]
        put_wide(block_out, None, 2048, parts[0], parts[2])
        put_wide(block_out, None, 2560, parts[1], dot(context[...], d_branch[...]))
        stores.append(send_lanes(block_out, blocks, 2048, 1024, sems.at[21]))
        for copy in tiny:
            copy.wait()
        few[...] = jnp.zeros_like(few)
        spread_gains(g_gains[...], few)
        for j in range(4):
            few[:, j, :] = g_code[0:64, column(j)]
            few[:, 4 + j, :] = g_code[64:128, column(j)]
        for j in range(4):
            first = g_proj[pl.ds(j, 64, stride=4), :]
            second = g_proj[pl.ds(256 + j, 64, stride=4), :]
            few[:, 9 + j, :] = first + pltpu.roll(second, 64, 1)
        block_out[:, :, :, :, :, 3072:] = few[...].reshape(4, 2, 4, 2, 16, 128).astype(BF)
        stores.append(send_lanes(block_out, blocks, 3072, 128, sems.at[22]))
        for copy in stores:
            copy.wait()


def second_grads(active, kept_0, kept_1, small):
    twice = [
        pltpu.VMEM((s.shape[0], 2 * PAD) if s.shape[1] == PAD else (2 * PAD, s.shape[1]), BF) for s in KEPT
    ]
    return pl.pallas_call(
        second_grads_kernel,
        out_shape=BLOCKS,
        in_specs=[SCALARS] + [ANY] * 19,
        out_specs=ANY,
        scratch_shapes=twice + [pltpu.VMEM(s.shape, s.dtype) for s in SMALL]
        + [pltpu.VMEM((64, 16, 128), F32), pltpu.VMEM(BLOCKS.shape, BF), pltpu.SemaphoreType.DMA((23,))],
        compiler_params=pltpu.CompilerParams(vmem_limit_bytes=127 << 19),
        cost_estimate=cost(21),
        name="second_grads",
    )(active, *kept_0, *kept_1, *small)


def average(ema, weight, grad, rate):
    return rate * ema + (1.0 - rate) * (weight - LEARN_RATE * grad)


def average_kernel(first, rates, total, few, *refs):
    weights, emas, d_x, grads, news, grad_in, held, sems = refs[:6], refs[6:12], refs[12], refs[14:20], refs[20:26], *refs[26:]
    fetch = pltpu.make_async_copy(d_x, held, sems.at[0])
    place = pltpu.make_async_copy(held, grad_in.at[1], sems.at[1])

    @pl.when(first[0] == 1)
    def _():
        fetch.start()

    grads[0][0, :, :1024] = total[0:8, 2048:3072]
    grads[0][0, :, 1024:] = total[8:16, 2048:3072]
    grads[1][0, :, :1024] = total[0:8, 1024:2048]
    grads[1][0, :, 1024:] = total[8:16, 1024:2048]
    grads[2][0, 0:16, :] = total[:, 0:512]
    grads[2][0, 16:32, :] = total[:, 512:1024]
    gain = total[8:9, 3072:3200]
    grads[3][0, 0:1, :] = gain[:, 0:8]
    grads[3][0, 1:2, :] = pltpu.roll(gain, 120, 1)[:, 0:8]
    is_first = first[0] == 1
    proj = few[9:13, :]
    grads[4][...] = jnp.where(is_first, proj, pltpu.roll(proj, 64, 1))[:, 0:8]
    code = jnp.where(is_first, few[0:4, :], few[4:8, :])
    turned = pltpu.roll(code, 64, 1)
    for r in range(4):
        grads[5][2 * r : 2 * r + 1, :] = code[r : r + 1, 0:64]
        grads[5][2 * r + 1 : 2 * r + 2, :] = turned[r : r + 1, 0:64]
    for i in range(6):
        rate = rates[0] if i < 4 else rates[1]
        news[i][...] = average(emas[i][...], weights[i][...].astype(F32), grads[i][...], rate)

    @pl.when(first[0] == 1)
    def _():
        fetch.wait()
        place.start()
        place.wait()


def averages(first, rates, total, few, weights, emas, d_x, grad_in):
    shapes = [jax.ShapeDtypeStruct(e.shape, F32) for e in emas]
    return pl.pallas_call(
        average_kernel,
        out_shape=shapes * 2 + [jax.ShapeDtypeStruct(grad_in.shape, BF)],
        in_specs=[SCALARS, SCALARS] + [INSIDE] * 14 + [ANY, ANY],
        out_specs=[INSIDE] * 12 + [ANY],
        input_output_aliases={17: 12},
        scratch_shapes=[pltpu.VMEM((SEQ, D), BF), pltpu.SemaphoreType.DMA((2,))],
        name="averages",
    )(first, rates, total, few, *weights, *emas, d_x, grad_in)


def per_device(
    video, cot_h, cot_q, frames, codes, w_attn, w_up, w_down, gains, proj, codebook,
    ema_attn, ema_up, ema_down, ema_gains, ema_proj, ema_code, decay,
):
    segment = lax.axis_index("pipe")
    in_first = (segment == 0).astype(jnp.int32).reshape(1)
    in_second = 1 - in_first
    weights = (w_attn[0], w_up[0], w_down[0], gains[0])
    frames = frames.reshape(2)

    block = jnp.concatenate([codebook.reshape(4, 128), jnp.pad(proj, ((0, 0), (0, 120)))], axis=0)
    block = block.astype(F32)
    half = 9
    whole = ((0, SEQ),)
    cuts = ((0, half * PATCHES), (half * PATCHES, SEQ - half * PATCHES))
    acts, sent_a, saved_a = first_forward(0, in_first, frames, video, weights, None, 0, half)
    sent_a, block = lax.optimization_barrier((sent_a, block))
    block_first = lax.ppermute(block, "pipe", [(0, 1)])
    received_a = lax.ppermute(sent_a, "pipe", [(0, 1)])
    acts, sent_b, saved_b = first_forward(0, in_first, frames, video, weights, acts, half, FRAMES - half)
    received_b = lax.ppermute(sent_b, "pipe", [(0, 1)])
    acts, sent_1, saved_1 = first_forward(1, in_first, frames, video, weights, acts)
    received_1 = lax.ppermute(sent_1, "pipe", [(0, 1)])
    w_attn_late, w_up_late, w_down_late, gains_late, cot_q, codes, decay, _ = lax.optimization_barrier(
        (w_attn, w_up, w_down, gains, cot_q, codes, decay, sent_1)
    )
    cot_rows = jnp.pad(jnp.swapaxes(cot_q[:, 0], 1, 2), ((0, 0), (0, 0), (0, 120)))
    code_rows = jnp.broadcast_to(codes[:, 0, :, None], (2, SEQ, 128))
    turned = w_attn_late[0, :, : 3 * D].T
    lane = lax.axis_index("dp")
    parts = lax.axis_size("dp")

    def own_rows(weight, axis):
        size = weight.shape[axis] // parts
        return lax.dynamic_slice_in_dim(weight, lane * size, size, axis).astype(F32)

    own = (
        own_rows(w_attn_late, 1), own_rows(w_up_late, 1), own_rows(w_down_late, 1), own_rows(gains_late, 2), proj,
        codebook,
    )
    rates = jnp.stack([lax.dynamic_index_in_dim(decay, segment, 0, keepdims=False), decay[2]])
    cot_rows, code_rows, turned, own, rates, block_first = lax.optimization_barrier(
        (cot_rows, code_rows, turned, own, rates, block_first)
    )
    quant = gather_blocks(jnp.stack([block_first, block]))
    second_weights = (w_attn[0], turned, w_up[0], w_down[0], gains[0])
    cots = (cot_h, cot_rows, code_rows, quant)
    acts, grad_in, back_0, kept_0, small = second_section(
        0, in_second, frames, cuts, (received_a, received_b), second_weights, cots, acts
    )
    returned_0 = lax.ppermute(back_0, "pipe", [(1, 0)])
    acts, grad_in, back_1, kept_1, small = second_section(
        1, in_second, frames, whole, (received_1,), second_weights, cots, acts, grad_in, small
    )
    returned_1 = lax.ppermute(back_1, "pipe", [(1, 0)])
    blocks = second_grads(in_second, kept_0, kept_1, small)

    returned_0, blocks = lax.optimization_barrier((returned_0, blocks))
    grad_in, *before = first_backward(0, in_first, video, weights, returned_0, cuts, (*saved_a, *saved_b), grad_in)

    d_x, total, few = first_backward_scatter(1, video, weights, returned_1, saved_1, blocks, before)
    emas = (ema_attn, ema_up, ema_down, ema_gains, ema_proj, ema_code)
    *results, grad_in = averages(in_first, rates, total, few, own, emas, d_x, grad_in)
    return (acts[None, :, None], grad_in[None, :, None], *results)


def solution(mesh):
    placed = (
        P(None, "dp", None, None),
        P(None, "dp", None, None),
        P(None, "dp", None, None),
        P(None, "dp"),
        P(None, "dp", None),
        P("pipe", None, None),
        P("pipe", None, None),
        P("pipe", None, None),
        P("pipe", None, None),
        P(("pipe", "dp"), None),
        P(None, ("pipe", "dp")),
        P("pipe", "dp", None),
        P("pipe", "dp", None),
        P("pipe", "dp", None),
        P("pipe", None, "dp"),
        P(("pipe", "dp"), None),
        P(None, ("pipe", "dp")),
        P(),
    )
    return jax.shard_map(
        per_device,
        mesh=mesh,
        in_specs=placed,
        out_specs=(
            P("pipe", None, "dp", None, None),
            P("pipe", None, "dp", None, None),
            P("pipe", "dp", None),
            P("pipe", "dp", None),
            P("pipe", "dp", None),
            P("pipe", None, "dp"),
            P(("pipe", "dp"), None),
            P(None, ("pipe", "dp")),
            P("pipe", "dp", None),
            P("pipe", "dp", None),
            P("pipe", "dp", None),
            P("pipe", None, "dp"),
            P(("pipe", "dp"), None),
            P(None, ("pipe", "dp")),
        ),
        check_vma=False,
    )
```
